512 devices in a mesh: lon: 32 (over x_lo, y, core), lat: 16 (over z, x_hi).
Axes of the slice: x: 4 (x_hi: 2, x_lo: 2; x = x_hi * 2 + x_lo), y: 8, z: 8, core: 2. Of those that a mesh axis runs over, the one named last changes fastest.
Arguments:
- fields: bfloat16 [2, 192, 294912], P(None, 'lat', 'lon'), may hold values from -6 to 6
- qkv_low: bfloat16 [192, 576], replicated, may hold values from -0.4375 to 0.4375
- proj_low: bfloat16 [192, 192], replicated, may hold values from -0.4375 to 0.4375
- merge_proj: bfloat16 [768, 384], replicated, may hold values from -0.21875 to 0.21875
- qkv_high: bfloat16 [384, 1152], replicated, may hold values from -0.3125 to 0.3125
- proj_high: bfloat16 [384, 384], replicated, may hold values from -0.3125 to 0.3125
- bias_low: float32 [1, 32, 6, 3312], P(None, 'lat'), may hold values from -4 to 265
- bias_high: float32 [1, 16, 12, 3312], P(None, 'lat'), may hold values from -4 to 265
Outputs:
- output: bfloat16 [2, 96, 294912], P(None, 'lat', 'lon')
The draws below stay inside these ranges and needn't reach their ends.
All inputs are finite; a program needn't handle non-finite values.
Results may differ from the reference program's by a relative error of at most 0.02.
Values may be sent and summed in bfloat16 or wider, within the bound.
A program may use at most 64 MiB of HBM per device.

```python
import jax
import jax.numpy as jnp
import numpy as np
from jax import lax

PL = 2
C1 = 192
H1 = 6
C2 = 384
H2 = 12
WPL = 2
WLAT = 6
WLON = 12
NPOS = 3312
NLAT1 = 192
NLON1 = 1536
LATWIN1 = 32
LATWIN2 = 16


def drawn_bias(key, shape, reach):
    return jnp.clip(jax.random.normal(key, shape, jnp.float32), -reach, reach)


def draw_bias_low(key, part):
    key = jax.random.fold_in(key, 7)
    shape = (PL // WPL, LATWIN1, H1, NPOS)
    return drawn_bias(key, shape, 4.0)


def draw_bias_high(key, part):
    key = jax.random.fold_in(key, 13)
    shape = (PL // WPL, LATWIN2, H2, NPOS)
    return drawn_bias(key, shape, 4.0)


def block_scale(key, dims, cuts, smallest, high):
    level, own = 1.0, jax.random.fold_in(key, 6)
    for dim, parts in cuts:
        heights = jnp.exp(jax.random.uniform(jax.random.fold_in(own, dim), (parts,), jnp.float32, smallest / len(cuts), high / len(cuts)))
        level = level * jnp.repeat(heights, dims[dim] // parts).reshape([-1 if axis == dim else 1 for axis in range(len(dims))])
    return level


def scatter_about(rng, dims, deviation, limit, cuts=(), kind=jnp.bfloat16):
    entries = jax.random.normal(rng, dims, jnp.float32) * deviation
    if len(cuts) > 0:
        entries = block_scale(rng, dims, cuts, -0.22, 0.18) * entries
    return jnp.clip(entries, min=-limit, max=limit).astype(kind)


def setup_inputs(seed: int = 0) -> dict:
    splits = jax.random.split(jax.random.key(seed), 9)
    fields = scatter_about(splits[0], (PL, NLAT1, NLON1 * C1), 1.0, 6.0, ((1, 16), (2, 32)))
    qkv_low = scatter_about(splits[1], (C1, 3 * C1), C1 ** -0.5, 0.4375)
    proj_low = scatter_about(splits[2], (C1, C1), C1 ** -0.5, 0.4375)
    merge_proj = scatter_about(splits[3], (4 * C1, C2), (4 * C1) ** -0.5, 0.21875)
    qkv_high = scatter_about(splits[4], (C2, 3 * C2), C2 ** -0.5, 0.3125)
    proj_high = scatter_about(splits[5], (C2, C2), C2 ** -0.5, 0.3125)
    bias_low = draw_bias_low(jax.random.fold_in(splits[8], 71), 0)
    bias_high = draw_bias_high(jax.random.fold_in(splits[8], 71), 0)
    return dict(fields=fields, qkv_low=qkv_low, proj_low=proj_low, merge_proj=merge_proj, qkv_high=qkv_high, proj_high=proj_high, bias_low=bias_low, bias_high=bias_high)


EPSILON = 1e-05

def normalize(values):
    widened = values.astype(jnp.float32)
    centre = lax.optimization_barrier(jnp.mean(widened, axis=-1, keepdims=True))
    spread = lax.optimization_barrier(jnp.mean(jnp.square(widened - centre), axis=-1, keepdims=True))
    return ((widened - centre) * lax.rsqrt(spread + EPSILON)).astype(jnp.bfloat16)

def position_table():
    level_pos, row_pos, col_pos = np.meshgrid(np.arange(WPL), np.arange(WLAT), np.arange(WLON), indexing='ij')
    level_pos = level_pos.reshape(-1)
    row_pos = row_pos.reshape(-1)
    col_pos = col_pos.reshape(-1)
    pairs = ((level_pos[:, None] * WPL + level_pos[None, :]) * WLAT + row_pos[:, None]) * WLAT + row_pos[None, :]
    pairs = pairs * (2 * WLON - 1) + col_pos[:, None] - col_pos[None, :] + WLON - 1
    return pairs.reshape(-1).astype(np.int32)

def attend(hidden, qkv_weight, out_weight, bias_table, head_count, row_start, row_total):
    levels, row_count, col_count, channels = hidden.shape
    head_size = channels // head_count
    groups = (levels // WPL, row_count // WLAT, col_count // WLON)
    window = WPL * WLAT * WLON
    packed = jnp.dot(hidden.reshape(-1, channels), qkv_weight, preferred_element_type=jnp.float32).astype(jnp.bfloat16)
    packed = packed.reshape(groups[0], WPL, groups[1], WLAT, groups[2], WLON, 3, head_count, head_size)
    packed = packed.transpose(6, 0, 2, 4, 7, 1, 3, 5, 8).reshape(3, groups[0], groups[1], groups[2], head_count, window, head_size)
    packed = packed.astype(jnp.float32)
    scores = jnp.einsum('abcnqd,abcnkd->abcnqk', packed[0], packed[1], precision=lax.Precision.HIGHEST)
    offsets = jnp.take(bias_table, jnp.asarray(position_table()), axis=3)
    offsets = offsets.reshape(groups[0], groups[1], 1, head_count, window, window)
    level_ids = jnp.arange(levels, dtype=jnp.int32)[:, None]
    row_ids = row_start + jnp.arange(row_count, dtype=jnp.int32)[None, :]
    labels = 2 * (level_ids == levels - 1).astype(jnp.int32) + (row_ids >= row_total - 3).astype(jnp.int32)
    labels = labels.reshape(groups[0], WPL, groups[1], WLAT).transpose(0, 2, 1, 3)
    labels = jnp.broadcast_to(labels[..., None], (groups[0], groups[1], WPL, WLAT, WLON)).reshape(groups[0], groups[1], window)
    allowed = (labels[:, :, :, None] == labels[:, :, None, :])[:, :, None, None]
    scores = jnp.where(allowed, scores * head_size ** (-0.5) + offsets, -jnp.inf)
    highest = lax.optimization_barrier(jnp.max(scores, axis=-1, keepdims=True))
    weights = jnp.exp(scores - highest)
    shares = (weights / lax.optimization_barrier(jnp.sum(weights, axis=-1, keepdims=True))).astype(jnp.bfloat16)
    blended = jnp.einsum('abcnqk,abcnkd->abcnqd', shares.astype(jnp.float32), packed[2], precision=lax.Precision.HIGHEST).astype(jnp.bfloat16)
    blended = blended.reshape(groups[0], groups[1], groups[2], head_count, WPL, WLAT, WLON, head_size)
    blended = blended.transpose(0, 4, 1, 5, 2, 6, 3, 7).reshape(-1, channels)
    projected = jnp.dot(blended, out_weight, preferred_element_type=jnp.float32).astype(jnp.bfloat16)
    return projected.reshape(levels, row_count, col_count, channels)

def banded(hidden, qkv_weight, out_weight, bias_table, head_count):
    levels, row_count, col_count, channels = hidden.shape
    band_count = row_count // WLAT
    stacked = hidden.reshape(levels, band_count, WLAT, col_count, channels).transpose(1, 0, 2, 3, 4)
    tables = bias_table.transpose(1, 0, 2, 3)[:, :, None]
    starts = jnp.arange(band_count, dtype=jnp.int32) * WLAT

    def one_band(band_item):
        band_part, part_table, start = band_item
        return attend(band_part, qkv_weight, out_weight, part_table, head_count, start, row_count)
    result = lax.map(one_band, (stacked, tables, starts))
    return result.transpose(1, 0, 2, 3, 4).reshape(levels, row_count, col_count, channels)

def merge_patches(values, merge_weight):
    levels, row_count, col_count, channels = values.shape
    grouped = values.reshape(levels, row_count // 2, 2, col_count // 2, 2, channels).transpose(0, 1, 3, 2, 4, 5)
    grouped = normalize(grouped.reshape(levels, row_count // 2, col_count // 2, 4 * channels))
    merged = jnp.dot(grouped.reshape(-1, 4 * channels), merge_weight, preferred_element_type=jnp.float32).astype(jnp.bfloat16)
    return merged.reshape(levels, row_count // 2, col_count // 2, -1)

def reference(fields, qkv_low, proj_low, merge_proj, qkv_high, proj_high, bias_low, bias_high):
    levels, row_count, flat_count = fields.shape
    tokens = fields.reshape(levels, row_count, flat_count // C1, C1)
    rolled = jnp.roll(tokens, (-1, -3, -6), (0, 1, 2))
    att_low = banded(normalize(rolled), qkv_low, proj_low, bias_low, H1)
    returned = jnp.roll(att_low, (1, 3, 6), (0, 1, 2))
    low_out = (tokens.astype(jnp.float32) + returned.astype(jnp.float32)).astype(jnp.bfloat16)
    merged = merge_patches(low_out, merge_proj)
    shifted = jnp.roll(merged, (-1, -3, -6), (0, 1, 2))
    att_high = banded(normalize(shifted), qkv_high, proj_high, bias_high, H2)
    result = (shifted.astype(jnp.float32) + att_high.astype(jnp.float32)).astype(jnp.bfloat16)
    result = jnp.roll(result, (1, 3, 6), (0, 1, 2))
    return result.reshape(levels, row_count // 2, -1)
```

```python
import functools

import jax
import jax.numpy as jnp
import ml_dtypes
import numpy as np
from jax import lax
from jax.experimental import pallas as pl
from jax.experimental.pallas import tpu as pltpu
from jax.sharding import PartitionSpec as P

MESH = pl.DeviceIdType.MESH
F32 = jnp.float32
BF16 = jnp.bfloat16

EPSILON = 1e-05
NEG = -1e30
SCALE = 32 ** (-0.5)
NPOS = 3312
HALF = 828
PAIRS = 24
WIDE = 384
PLACES = ((3, 4, 5, 6, 7, 0), (1, 2, 3, 4, 5, 6), (7, 0, 2, 4, 6, 1))
TABLE_ROWS = ((0, 16), (16, 16), (32, 32))


def one_hot_tables():
    out = np.zeros((3, 6, 256, 256), np.float32)
    for kind in range(3):
        for ia in range(6):
            for ib in range(6):
                lane = PLACES[kind][ib]
                for m in range(-5, 6):
                    out[kind, ia, 10 * ia + 23 * ib + 11 - 2 * m, (m + 5) * 8 + lane] = 1
                for m in range(-6, 6):
                    out[kind, ia, 10 * ia + 23 * ib + 10 - 2 * m, 128 + (m + 6) * 8 + lane] = 1
    return out.reshape(3 * 6 * 256, 256).astype(ml_dtypes.bfloat16)


def sublanes(rows):
    return lax.rem(lax.broadcasted_iota(jnp.int32, (rows, 1), 0), 8)


def roll8(value, shift):
    shift %= 8
    if shift == 0:
        return value
    rows, cols = value.shape
    if rows == 8:
        return pltpu.roll(value, shift, 0)
    return pltpu.roll(value.reshape(rows // 8, 8, cols), shift, 1).reshape(rows, cols)


def kernel(
    fields_hbm, qkv_low_hbm, proj_low_hbm, merge_hbm, qkv_high_hbm, proj_high_hbm, bias_low_hbm,
    bias_high_hbm, onehot_hbm,
    out_ref,
    fields, wl, wp, wm, wh, wph, bl, bh, oh,
    w_even, w_odd, wp_even, wp_odd,
    tabs, strip_e, strip_o, t_low, t_high,
    xu, xn, qkv, ob, lo,
    s1_lat, s1_lon, s1_cor, r1_lat, r1_lon, r1_cor,
    s2_lat, s2_lon, s2_cor, r2_lat, r2_lon, r2_cor,
    s3_lat, s3_lon, s3_cor, r3_lat, r3_lon, r3_cor,
    mi, mn, mg, xh, qh, oh2, res,
    local_sem, send_sem, recv_sem,
    *, lat_total, lon_total,
):
    lat = lax.axis_index("lat")
    lon = lax.axis_index("lon")
    lat_prev = lax.rem(lat + lat_total - 1, lat_total)
    lat_next = lax.rem(lat + 1, lat_total)
    lon_prev = lax.rem(lon + lon_total - 1, lon_total)
    lon_next = lax.rem(lon + 1, lon_total)
    before = ((lat_prev, lon), (lat, lon_prev), (lat_prev, lon_prev))
    after = ((lat_next, lon), (lat, lon_next), (lat_next, lon_next))

    def device(place):
        return {"lat": place[0], "lon": place[1]}

    barrier = pltpu.get_barrier_semaphore()
    for place in before + after:
        pl.semaphore_signal(barrier, inc=1, device_id=device(place), device_id_type=MESH)

    def fetch(source, target, index):
        copy = pltpu.make_async_copy(source, target, local_sem.at[index])
        copy.start()
        return copy

    get_fields = fetch(fields_hbm, fields, 0)
    get_bl = fetch(bias_low_hbm, bl, 1)
    get_bh = fetch(bias_high_hbm, bh, 2)
    get_oh = fetch(onehot_hbm, oh, 3)
    get_wl = fetch(qkv_low_hbm, wl, 4)
    get_wp = fetch(proj_low_hbm, wp, 5)
    get_wm = fetch(merge_hbm, wm, 6)
    get_wh = fetch(qkv_high_hbm, wh, 7)
    get_wph = fetch(proj_high_hbm, wph, 8)

    def remote(source, target, index, place):
        return pltpu.make_async_remote_copy(
            src_ref=source,
            dst_ref=target,
            send_sem=send_sem.at[index],
            recv_sem=recv_sem.at[index],
            device_id=device(place),
            device_id_type=MESH,
        )

    p1 = (
        remote(s1_lat, r1_lat, 0, before[0]),
        remote(s1_lon, r1_lon, 1, before[1]),
        remote(s1_cor, r1_cor, 2, before[2]),
    )
    p2 = (
        remote(s2_lat, r2_lat, 3, before[0]),
        remote(s2_lon, r2_lon, 4, before[1]),
        remote(s2_cor, r2_cor, 5, before[2]),
    )
    p3 = (
        remote(s3_lat, r3_lat, 6, after[0]),
        remote(s3_lon, r3_lon, 7, after[1]),
        remote(s3_cor, r3_cor, 8, after[2]),
    )

    sub8 = sublanes(8)
    zeros4 = jnp.zeros((4, WIDE), F32)

    def tiles(p, jj):
        both = fields[p, :, jj * WIDE:(jj + 1) * WIDE].astype(F32)
        return both[0:8], jnp.concatenate([both[8:12], zeros4], axis=0)

    get_fields.wait()
    for jj in range(PAIRS):
        top = [fields[p, 0:8, jj * WIDE:(jj + 1) * WIDE].astype(F32) for p in range(2)]
        slab = jnp.where(sub8 < 4, top[1], roll8(top[0], 4)).astype(BF16)
        if jj < 3:
            s1_cor[8 * jj:8 * jj + 8, :] = slab
        else:
            s1_lat[8 * (jj - 3):8 * (jj - 3) + 8, :] = slab
    for jj in range(3):
        lower = []
        for p in range(2):
            t0, t1 = tiles(p, jj)
            at = (2 * jj + p) * 8
            s1_lon[at:at + 8, :] = jnp.where(sub8 >= 3, t0, t1).astype(BF16)
            lower.append(t1)
        s1_lon[48 + 8 * jj:56 + 8 * jj, :] = jnp.where(sub8 < 4, lower[0], roll8(lower[1], 4)).astype(BF16)
    pl.semaphore_wait(barrier, 6)
    for copy in p1:
        copy.start()

    def put_unit(r, jjr, p, slab):
        u = 8 * r + 2 * (jjr // 6) + p
        xu[u, 8 * (jjr % 6):8 * (jjr % 6) + 8, :] = slab

    for p in range(2):
        for jjr in range(PAIRS - 3):
            t0, t1 = tiles(p, jjr + 3)
            put_unit(0, jjr, p, jnp.where(sub8 >= 3, t0, t1))
            put_unit(1, jjr, p, t1)

    w_even[...] = jnp.zeros_like(w_even)
    w_odd[...] = jnp.zeros_like(w_odd)
    wp_even[...] = jnp.zeros_like(wp_even)
    wp_odd[...] = jnp.zeros_like(wp_odd)
    strip_e[...] = jnp.zeros_like(strip_e)
    strip_o[...] = jnp.zeros_like(strip_o)
    tabs[...] = jnp.zeros_like(tabs)
    get_wl.wait()
    for part in range(3):
        piece = wl[:, 192 * part:192 * part + 192]
        w_even[0:192, 256 * part:256 * part + 192] = piece
        w_odd[64:256, 256 * part:256 * part + 192] = piece
    get_wp.wait()
    wp_even[0:192, 0:192] = wp[...]
    wp_odd[0:192, 192:384] = wp[...]

    get_bl.wait()
    get_bh.wait()
    for p in range(2):
        start = 0 if p == 1 else NPOS - HALF
        for r in range(2):
            at = 16 * r + 8 * p
            tabs[at:at + 6, 0:HALF] = bl[0, r, :, start:start + HALF]
        at = 32 + 16 * p
        tabs[at:at + 12, 0:HALF] = bh[0, 0, :, start:start + HALF]
    get_oh.wait()
    for kind in range(3):
        first, count = TABLE_ROWS[kind]
        for ia in range(6):
            wide = tabs[first:first + count, 128 * ia:128 * ia + 256]
            high = wide.astype(BF16)
            rest = wide - high.astype(F32)
            middle = rest.astype(BF16)
            low = (rest - middle.astype(F32)).astype(BF16)
            at = (kind * 6 + ia) * 256
            spread = jnp.dot(
                jnp.concatenate([high, middle, low], axis=0), oh[at:at + 256, :], preferred_element_type=F32
            )
            spread = spread[0:count] + spread[count:2 * count] + spread[2 * count:3 * count]
            where = pl.ds(first * 8 + PLACES[kind][ia], count, stride=8)
            strip_e[where, :] = spread[:, 0:128]
            strip_o[where, :] = spread[:, 128:256]

    lane = lax.broadcasted_iota(jnp.int32, (8, 128), 1)
    row8 = lax.broadcasted_iota(jnp.int32, (8, 128), 0)
    key8 = lax.rem(lane, 8)
    last = lat == lat_total - 1

    def any_of(value, options):
        hit = value == options[0]
        for option in options[1:]:
            hit = hit | (value == option)
        return hit

    def mask_of(kind):
        places = PLACES[kind]
        mask = jnp.where((lane < 96) & any_of(key8, places), 0.0, NEG)
        if kind > 0:
            differ = jnp.where(any_of(row8, places[3:]), 1, 0) != jnp.where(any_of(key8, places[3:]), 1, 0)
            mask = jnp.where(differ & last, NEG, mask)
        return mask

    def build_tables(kind, target):
        mask = mask_of(kind)
        first, count = TABLE_ROWS[kind]
        stride = count // 2
        heads = 12 if kind == 2 else 6

        def one(index, carry):
            p, head = index // heads, lax.rem(index, heads)
            at = pl.multiple_of((first + p * stride + head) * 8, 8)
            even = strip_e[pl.ds(at, 8), :]
            odd = strip_o[pl.ds(at, 8), :]
            for parity in range(2):
                left, right = (even, odd) if parity == 0 else (odd, even)
                for k in range(6):
                    tile = jnp.where(
                        lane < 48,
                        pltpu.roll(left, (128 - (5 - k) * 8) % 128, 1),
                        pltpu.roll(right, 8 * k + 8 * parity, 1),
                    )
                    row = 48 * parity + 8 * k
                    target[index, row:row + 8, :] = tile + mask
            return carry

        lax.fori_loop(0, 2 * heads, one, 0)

    build_tables(0, t_low.at[0])
    build_tables(1, t_low.at[1])
    build_tables(2, t_high)

    wide_lane = lax.broadcasted_iota(jnp.int32, (1, 128), 1)
    low_half = wide_lane < 64
    head_masks = [
        jnp.where(wide_lane // 32 == h, 1.0, 0.0).astype(BF16) for h in range(4)
    ]
    ones = jnp.ones((128, 128), BF16)
    zeros32 = jnp.zeros((32, 128), BF16)

    def norm_unit(u, carry):
        x = xu[u]
        x0, x1, x2 = x[:, 0:128], x[:, 128:256], x[:, 256:384]
        me = jnp.sum(x0 + jnp.where(low_half, x1, 0.0), axis=1, keepdims=True) / 192
        mo = jnp.sum(x2 + jnp.where(low_half, 0.0, x1), axis=1, keepdims=True) / 192
        d0, d1, d2 = x0 - me, x1 - jnp.where(low_half, me, mo), x2 - mo
        q1 = d1 * d1
        ve = jnp.sum(d0 * d0 + jnp.where(low_half, q1, 0.0), axis=1, keepdims=True) / 192
        vo = jnp.sum(d2 * d2 + jnp.where(low_half, 0.0, q1), axis=1, keepdims=True) / 192
        re, ro = lax.rsqrt(ve + EPSILON), lax.rsqrt(vo + EPSILON)
        xn[u, :, 0:128] = (d0 * re).astype(BF16)
        xn[u, :, 128:256] = (d1 * jnp.where(low_half, re, ro)).astype(BF16)
        xn[u, :, 256:384] = (d2 * ro).astype(BF16)
        return carry

    def qkv_units(first, count):
        lax.fori_loop(first, first + count, norm_unit, 0)
        for parity, weight in ((0, w_even), (1, w_odd)):
            rows = xn[first:first + count, :, 128 * parity:128 * parity + 256].reshape(count * 48, 256)
            for part in range(3):
                piece = jnp.dot(rows, weight[:, 256 * part:256 * part + 256], preferred_element_type=F32)
                qkv[first:first + count, 48 * parity:48 * parity + 48, 256 * part:256 * part + 256] = (
                    piece.astype(BF16).reshape(count, 48, 256)
                )

    def group_attend(q, k, v, heads, table):
        stack = jnp.concatenate([q * head_masks[h] for h in range(heads)], axis=0)
        keys = jnp.concatenate([k, zeros32], axis=0)
        scores = lax.dot_general(stack, keys, (((1,), (1,)), ((), ())), preferred_element_type=F32)
        scores = scores * SCALE + table.reshape(heads * 96, 128)
        weights = jnp.exp(scores - jnp.max(scores, axis=1, keepdims=True)).astype(BF16)
        values = jnp.concatenate([jnp.concatenate([v, zeros32], axis=0), ones], axis=1)
        mixed = jnp.dot(weights, values, preferred_element_type=F32)
        top, bottom = mixed[0:96, 0:128], mixed[0:96, 128:256]
        for h in range(1, heads):
            own = wide_lane // 32 == h
            top = jnp.where(own, mixed[96 * h:96 * h + 96, 0:128], top)
            bottom = jnp.where(own, mixed[96 * h:96 * h + 96, 128:256], bottom)
        return (top / bottom).astype(BF16)

    def attend_low(r, first, count):
        def one(u, carry):
            p = lax.rem(u, 2)
            for group, heads in ((0, 4), (1, 2)):
                at = 128 * group
                ob[u, :, at:at + 128] = group_attend(
                    qkv[u, :, at:at + 128],
                    qkv[u, :, 256 + at:384 + at],
                    qkv[u, :, 512 + at:640 + at],
                    heads,
                    t_low[r, pl.ds(p * 6 + 4 * group, heads)],
                )
            return carry

        lax.fori_loop(first, first + count, one, 0)

    def project_low(first, count):
        even = ob[first:first + count, 0:48, :].reshape(count * 48, 256)
        odd = ob[first:first + count, 48:96, :].reshape(count * 48, 256)
        att = jnp.dot(even, wp_even[...], preferred_element_type=F32) + jnp.dot(
            odd, wp_odd[...], preferred_element_type=F32
        )
        att = att.astype(BF16).astype(F32).reshape(count, 48, WIDE)
        lo[first:first + count] = (xu[first:first + count] + att).astype(BF16).astype(F32)

    def low_slab(r, jjr, p):
        return lo[8 * r + 2 * (jjr // 6) + p, 8 * (jjr % 6):8 * (jjr % 6) + 8, :]

    qkv_units(0, 6)
    attend_low(0, 0, 6)

    p1[1].wait_recv()
    for k in range(3):
        for p in range(2):
            at = (2 * k + p) * 8
            put_unit(0, 21 + k, p, r1_lon[at:at + 8, :].astype(F32))
    qkv_units(6, 2)
    attend_low(0, 6, 2)
    project_low(0, 8)
    for jjr in range(PAIRS):
        slab = jnp.where(
            (sub8 >= 2) & (sub8 < 6), low_slab(0, jjr, 1), roll8(low_slab(0, jjr, 0), 4)
        ).astype(BF16)
        if jjr < 3:
            s2_cor[8 * jjr:8 * jjr + 8, :] = slab
        else:
            s2_lat[8 * (jjr - 3):8 * (jjr - 3) + 8, :] = slab
    p2[0].start()
    p2[2].start()

    p1[0].wait_recv()
    p1[2].wait_recv()
    for jjr in range(PAIRS):
        if jjr < 21:
            halo = r1_lat[8 * jjr:8 * jjr + 8, :].astype(F32)
        else:
            k = jjr - 21
            halo = r1_cor[8 * k:8 * k + 8, :].astype(F32)
            lower = r1_lon[48 + 8 * k:56 + 8 * k, :].astype(F32)
        for p in range(2):
            place = (8 + 2 * (jjr // 6) + p, slice(8 * (jjr % 6), 8 * (jjr % 6) + 8))
            own = xu[place[0], place[1], :] if jjr < 21 else roll8(lower, 4 * p)
            put_unit(1, jjr, p, jnp.where(sub8 < 4, own, roll8(halo, 4 * p)))
    qkv_units(8, 8)
    attend_low(1, 8, 2)
    project_low(8, 2)
    for k in range(3):
        for p in range(2):
            at = (2 * k + p) * 8
            s2_lon[at:at + 8, :] = jnp.where(sub8 == 0, low_slab(0, k, p), low_slab(1, k, p)).astype(BF16)
        s2_lon[48 + 8 * k:56 + 8 * k, :] = jnp.where(
            sub8 >= 4, low_slab(0, k, 0), roll8(low_slab(0, k, 1), 4)
        ).astype(BF16)
    p2[1].start()
    attend_low(1, 10, 6)
    project_low(10, 6)

    for copy in p2:
        copy.wait_recv()
    for col in range(PAIRS):
        jjr = col + 3
        if col < 21:
            halo = r2_lat[8 * col:8 * col + 8, :].astype(F32)
        else:
            k = col - 21
            halo = r2_cor[8 * k:8 * k + 8, :].astype(F32)
            upper = r2_lon[48 + 8 * k:56 + 8 * k, :].astype(F32)
        for p in range(2):
            beyond = roll8(halo, 4 * p)
            if col < 21:
                first, second = low_slab(0, jjr, p), low_slab(1, jjr, p)
                inner = jnp.where(sub8 == 0, first, second)
            else:
                first = roll8(upper, 4 * p)
                at = (2 * k + p) * 8
                inner = r2_lon[at:at + 8, :].astype(F32)
            at = (p * PAIRS + col) * 8
            mi[0, at:at + 8, :] = jnp.where(sub8 == 7, beyond, inner)
            mi[1, at:at + 8, :] = jnp.where(sub8 >= 6, first, beyond)

    def pair_sum(value):
        rows = value.shape[0]
        value = jnp.broadcast_to(value, (rows, 128))
        even = lax.rem(sublanes(rows), 2) == 0
        return value + jnp.where(even, roll8(value, 7), roll8(value, 1))

    def triple(value):
        return jnp.concatenate([value, value, value], axis=1)

    def norm_merge(index, carry):
        rows = pl.ds(pl.multiple_of(index * 48, 48), 48)
        for kind in range(2):
            x = mi[kind, rows, :]
            centre = pair_sum(jnp.sum(x, axis=1, keepdims=True)) / 768
            d = x - triple(centre)
            spread = pair_sum(jnp.sum(d * d, axis=1, keepdims=True)) / 768
            mn[kind, rows, :] = (d * triple(lax.rsqrt(spread + EPSILON))).astype(BF16)
        return carry

    lax.fori_loop(0, 8, norm_merge, 0)
    get_wm.wait()
    even_row = lax.rem(sublanes(192), 2) == 0
    for p in range(2):
        rows = slice(192 * p, 192 * p + 192)
        sums = []
        for kind in range(2):
            y0 = jnp.dot(mn[kind, rows, :], wm[0:384, :], preferred_element_type=F32)
            y1 = jnp.dot(mn[kind, rows, :], wm[384:768, :], preferred_element_type=F32)
            sums.append(y0 + roll8(y1, 7) if kind == 0 else roll8(y0, 1) + y1)
        merged = jnp.where(even_row, sums[0], sums[1]).astype(BF16).astype(F32)
        for col in range(PAIRS):
            w, within = col // 12, col % 12
            at = 48 * (within % 2) + 8 * (within // 2)
            mg[2 * p + w, at:at + 8, :] = merged[8 * col:8 * col + 8, :]

    def norm_high(index, carry):
        u, rows = index // 2, pl.ds(pl.multiple_of(lax.rem(index, 2) * 48, 48), 48)
        x = mg[u, rows, :]
        d = x - jnp.sum(x, axis=1, keepdims=True) / 384
        spread = jnp.sum(d * d, axis=1, keepdims=True) / 384
        xh[u, rows, :] = (d * lax.rsqrt(spread + EPSILON)).astype(BF16)
        return carry

    lax.fori_loop(0, 8, norm_high, 0)
    get_wh.wait()
    rows = xh[...].reshape(384, 384)
    for part in range(3):
        piece = jnp.dot(rows, wh[:, 384 * part:384 * part + 384], preferred_element_type=F32)
        qh[:, :, 384 * part:384 * part + 384] = piece.astype(BF16).reshape(4, 96, 384)

    def attend_high(u, carry):
        p = u // 2
        for group in range(3):
            at = 128 * group
            oh2[u, :, at:at + 128] = group_attend(
                qh[u, :, at:at + 128],
                qh[u, :, 384 + at:512 + at],
                qh[u, :, 768 + at:896 + at],
                4,
                t_high[pl.ds(p * 12 + 4 * group, 4)],
            )
        return carry

    lax.fori_loop(0, 4, attend_high, 0)
    get_wph.wait()
    att = jnp.dot(oh2[...].reshape(384, 384), wph[...], preferred_element_type=F32)
    att = att.astype(BF16).astype(F32).reshape(4, 96, 384)
    res[...] = (mg[...] + att).astype(BF16).astype(F32)

    def result(col, p):
        w, within = col // 12, col % 12
        at = 48 * (within % 2) + 8 * (within // 2)
        return res[2 * p + w, at:at + 8, :]

    def own_rows(x, shift):
        return jnp.where(sub8 == (5 + shift) % 8, roll8(x, 3 + shift), roll8(x, 4 + shift))

    def far_rows(x, shift):
        return jnp.where(
            sub8 == shift,
            roll8(x, 4 + shift),
            jnp.where(sub8 == 1 + shift, roll8(x, 3 + shift), roll8(x, 1 + shift)),
        )

    for col in range(PAIRS):
        slab = jnp.where(sub8 < 4, far_rows(result(col, 0), 0), far_rows(result(col, 1), 4)).astype(BF16)
        if col < 18:
            s3_lat[8 * col:8 * col + 8, :] = slab
        else:
            k = col - 18
            s3_cor[8 * k:8 * k + 8, :] = slab
            s3_lon[8 * k:8 * k + 8, :] = jnp.where(
                (sub8 >= 3) & (sub8 < 6), own_rows(result(col, 0), 0), own_rows(result(col, 1), 4)
            ).astype(BF16)
    for copy in p3:
        copy.start()
    for copy in p3:
        copy.wait_recv()
    for target in range(PAIRS):
        for p in range(2):
            if target < 6:
                first = r3_cor[8 * target:8 * target + 8, :].astype(F32)
                second = roll8(r3_lon[8 * target:8 * target + 8, :].astype(F32), 4 * p)
            else:
                k = target - 6
                first = r3_lat[8 * k:8 * k + 8, :].astype(F32)
                second = own_rows(result(k, p), 0)
            whole = jnp.where(sub8 < 3, roll8(first, 4 * p), second).astype(BF16)
            out_ref[p, :, target * WIDE:(target + 1) * WIDE] = whole[0:6, :]
    for copy in p1 + p2 + p3:
        copy.wait_send()


def solution(mesh):
    lat_total, lon_total = mesh.shape["lat"], mesh.shape["lon"]
    onehot = one_hot_tables()

    def step(fields, qkv_low, proj_low, merge_proj, qkv_high, proj_high, bias_low, bias_high):
        def vmem(*shape, dtype=BF16):
            return pltpu.VMEM(shape, dtype)

        halo = [vmem(176, WIDE), vmem(80, WIDE), vmem(32, WIDE)]
        last_halo = [vmem(144, WIDE), vmem(48, WIDE), vmem(48, WIDE)]
        return pl.pallas_call(
            functools.partial(kernel, lat_total=lat_total, lon_total=lon_total),
            out_shape=jax.ShapeDtypeStruct((2, 6, PAIRS * WIDE), BF16),
            in_specs=[pl.BlockSpec(memory_space=pl.ANY)] * 9,
            out_specs=pl.BlockSpec(memory_space=pltpu.VMEM),
            scratch_shapes=[
                vmem(2, 12, PAIRS * WIDE),
                vmem(192, 576),
                vmem(192, 192),
                vmem(768, 384),
                vmem(384, 1152),
                vmem(384, 384),
                vmem(1, 2, 6, NPOS, dtype=F32),
                vmem(1, 1, 12, NPOS, dtype=F32),
                vmem(3 * 6 * 256, 256),
                vmem(256, 768),
                vmem(256, 768),
                vmem(256, 384),
                vmem(256, 384),
                vmem(64, 896, dtype=F32),
                vmem(512, 128, dtype=F32),
                vmem(512, 128, dtype=F32),
                vmem(2, 12, 96, 128, dtype=F32),
                vmem(24, 96, 128, dtype=F32),
                vmem(16, 48, WIDE, dtype=F32),
                vmem(16, 48, WIDE),
                vmem(16, 96, 768),
                vmem(16, 96, 256),
                vmem(16, 48, WIDE, dtype=F32),
                *halo, *halo, *halo, *halo, *last_halo, *last_halo,
                vmem(2, 384, WIDE, dtype=F32),
                vmem(2, 384, WIDE),
                vmem(4, 96, WIDE, dtype=F32),
                vmem(4, 96, WIDE),
                vmem(4, 96, 3 * WIDE),
                vmem(4, 96, WIDE),
                vmem(4, 96, WIDE, dtype=F32),
                pltpu.SemaphoreType.DMA((9,)),
                pltpu.SemaphoreType.DMA((9,)),
                pltpu.SemaphoreType.DMA((9,)),
            ],
            compiler_params=pltpu.CompilerParams(
                collective_id=0, has_side_effects=True, vmem_limit_bytes=48 * 1024 * 1024
            ),
            name="block",
        )(
            fields, qkv_low, proj_low, merge_proj, qkv_high, proj_high, bias_low, bias_high,
            jnp.asarray(onehot),
        )

    return jax.shard_map(
        step,
        mesh=mesh,
        in_specs=(
            P(None, "lat", "lon"),
            P(),
            P(),
            P(),
            P(),
            P(),
            P(None, "lat", None, None),
            P(None, "lat", None, None),
        ),
        out_specs=P(None, "lat", "lon"),
        check_vma=False,
    )
```

```python
import functools

import jax
import jax.numpy as jnp
from jax import lax
from jax.experimental import pallas as pl
from jax.experimental.pallas import tpu as pltpu
from jax.sharding import PartitionSpec as P

MESH = pl.DeviceIdType.MESH
F32 = jnp.float32
BF16 = jnp.bfloat16

EPSILON = 1e-05
NEG = -1e30
SCALE = 32 ** (-0.5)
NPOS = 3312
HALF = 828
PAIRS = 24
WIDE = 384
PLACES = ((3, 4, 5, 6, 7, 0), (1, 2, 3, 4, 5, 6), (7, 0, 2, 4, 6, 1))
TABLE_ROWS = ((0, 16), (16, 16), (32, 32))


def sublanes(rows):
    return lax.rem(lax.broadcasted_iota(jnp.int32, (rows, 1), 0), 8)


def roll8(value, shift):
    shift %= 8
    if shift == 0:
        return value
    rows, cols = value.shape
    if rows == 8:
        return pltpu.roll(value, shift, 0)
    return pltpu.roll(value.reshape(rows // 8, 8, cols), shift, 1).reshape(rows, cols)


def kernel(
    fields_hbm, qkv_low_hbm, proj_low_hbm, merge_hbm, qkv_high_hbm, proj_high_hbm, bias_low_hbm,
    bias_high_hbm,
    out_ref,
    fields, flat, wl, wp, wm, wh, wph, bl, bh,
    w_even, w_odd, wp_even, wp_odd,
    tabs, strip_e, strip_o, t_low, t_high,
    xu, xn, qkv, ob, lo,
    s2_lat, s2_lon, s2_cor, r2_lat, r2_lon, r2_cor,
    s3_lat, s3_lon, s3_cor, r3_lat, r3_lon, r3_cor,
    mi, mn, mg, xh, qh, oh2, res,
    local_sem, send_sem, recv_sem,
    *, lat_total, lon_total,
):
    lat = lax.axis_index("lat")
    lon = lax.axis_index("lon")
    lat_prev = lax.rem(lat + lat_total - 1, lat_total)
    lat_next = lax.rem(lat + 1, lat_total)
    lon_prev = lax.rem(lon + lon_total - 1, lon_total)
    lon_next = lax.rem(lon + 1, lon_total)
    before = ((lat_prev, lon), (lat, lon_prev), (lat_prev, lon_prev))
    after = ((lat_next, lon), (lat, lon_next), (lat_next, lon_next))

    def device(place):
        return {"lat": place[0], "lon": place[1]}

    barrier = pltpu.get_barrier_semaphore()
    for place in before + after:
        pl.semaphore_signal(barrier, inc=1, device_id=device(place), device_id_type=MESH)

    def fetch(source, target, index):
        copy = pltpu.make_async_copy(source, target, local_sem.at[index])
        copy.start()
        return copy

    get_fields = fetch(fields_hbm, fields.at[0:12, :, 0:PAIRS * WIDE], 0)
    get_bl = fetch(bias_low_hbm, bl, 1)
    get_bh = fetch(bias_high_hbm, bh, 2)
    get_wl = fetch(qkv_low_hbm, wl, 4)
    get_wp = fetch(proj_low_hbm, wp, 5)
    get_wm = fetch(merge_hbm, wm, 6)
    get_wh = fetch(qkv_high_hbm, wh, 7)
    get_wph = fetch(proj_high_hbm, wph, 8)

    def remote(source, target, index, place):
        return pltpu.make_async_remote_copy(
            src_ref=source,
            dst_ref=target,
            send_sem=send_sem.at[index],
            recv_sem=recv_sem.at[index],
            device_id=device(place),
            device_id_type=MESH,
        )

    inner, edge = pl.ds(3 * WIDE, 21 * WIDE), pl.ds(0, 3 * WIDE)
    beyond = pl.ds(PAIRS * WIDE, 3 * WIDE)
    p1 = (
        remote(fields_hbm.at[0:3, :, inner], fields.at[12:15, :, inner], 0, before[0]),
        remote(fields_hbm.at[3:12, :, edge], fields.at[3:12, :, beyond], 1, before[1]),
        remote(fields_hbm.at[0:3, :, edge], fields.at[12:15, :, beyond], 2, before[2]),
    )
    p2 = (
        remote(s2_lat, r2_lat, 3, before[0]),
        remote(s2_lon, r2_lon, 4, before[1]),
        remote(s2_cor, r2_cor, 5, before[2]),
    )
    p3 = (
        remote(s3_lat, r3_lat, 6, after[0]),
        remote(s3_lon, r3_lon, 7, after[1]),
        remote(s3_cor, r3_cor, 8, after[2]),
    )

    sub8 = sublanes(8)
    pl.semaphore_wait(barrier, 6)
    for copy in p1:
        copy.start()

    def put_unit(r, jjr, p, part, slab):
        u = 8 * r + 2 * (jjr // 6) + p
        xu[u, 8 * (jjr % 6):8 * (jjr % 6) + 8, 128 * part:128 * part + 128] = slab

    def widen(jj, first, count):
        for part in range(3):
            at = jj * WIDE + 128 * part
            flat[3 * jj + part, 2 * first:2 * (first + count), :] = (
                fields[first:first + count, :, at:at + 128].astype(F32).reshape(2 * count, 128)
            )

    def put_first(jj):
        for part in range(3):
            for p in range(2):
                upper = flat[3 * jj + part, pl.ds(p, 8, stride=2), :]
                lower = flat[3 * jj + part, pl.ds(16 + p, 8, stride=2), :]
                put_unit(0, jj - 3, p, part, jnp.where(sub8 >= 3, upper, lower))

    def put_second(jj):
        for part in range(3):
            for p in range(2):
                put_unit(1, jj - 3, p, part, flat[3 * jj + part, pl.ds(16 + p, 8, stride=2), :])

    def stage_own():
        flat[:, 24:32, :] = jnp.zeros_like(flat[:, 24:32, :])
        for jj in range(3, PAIRS):
            widen(jj, 0, 12)
            put_first(jj)

    get_fields.wait()
    stage_own()

    def stage_pad():
        w_even[...] = jnp.zeros_like(w_even)
        w_odd[...] = jnp.zeros_like(w_odd)
        wp_even[...] = jnp.zeros_like(wp_even)
        wp_odd[...] = jnp.zeros_like(wp_odd)
        strip_e[...] = jnp.zeros_like(strip_e)
        strip_o[...] = jnp.zeros_like(strip_o)
        tabs[...] = jnp.zeros_like(tabs)
        for part in range(3):
            piece = wl[:, 192 * part:192 * part + 192]
            w_even[0:192, 256 * part:256 * part + 192] = piece
            w_odd[64:256, 256 * part:256 * part + 192] = piece
        wp_even[0:192, 0:192] = wp[...]
        wp_odd[0:192, 192:384] = wp[...]

    get_wl.wait()
    get_wp.wait()
    stage_pad()

    def one_hot(kind):
        wide = lax.broadcasted_iota(jnp.int32, (8, 256), 1)
        within = lax.rem(wide, 128)
        step, place = within // 8, lax.rem(within, 8)
        offset = jnp.where(wide < 128, 2 * step - 10, 2 * step - 11)
        entry = jnp.full((8, 256), -1, jnp.int32)
        for ib in range(6):
            entry = jnp.where(place == PLACES[kind][ib], 23 * ib + 11 - offset, entry)
        entry = jnp.where(step < jnp.where(wide < 128, 11, 12), entry, -1)
        row = lax.broadcasted_iota(jnp.int32, (256, 256), 0)
        return jnp.where(row == entry[0:1, :], 1.0, 0.0).astype(BF16)

    def stage_strips():
        for p in range(2):
            start = 0 if p == 1 else NPOS - HALF
            for ia in range(6):
                source = slice(start + 138 * ia, start + 138 * ia + 138)
                for r in range(2):
                    at = 96 * r + 16 * ia + 8 * p
                    tabs[at:at + 6, 0:138] = bl[0, :, r, source]
                at = 192 + 32 * ia + 16 * p
                tabs[at:at + 12, 0:138] = bh[0, :, 0, source]
        for kind in range(3):
            first, count = TABLE_ROWS[kind]
            wide = tabs[6 * first:6 * (first + count), :]
            high = wide.astype(BF16)
            rest = wide - high.astype(F32)
            middle = rest.astype(BF16)
            low = (rest - middle.astype(F32)).astype(BF16)
            hot = one_hot(kind)
            spread = jnp.dot(high, hot, preferred_element_type=F32)
            spread = spread + jnp.dot(middle, hot, preferred_element_type=F32)
            spread = spread + jnp.dot(low, hot, preferred_element_type=F32)
            for ia in range(6):
                piece = spread[count * ia:count * (ia + 1)]
                where = pl.ds(first * 8 + PLACES[kind][ia], count, stride=8)
                strip_e[where, :] = piece[:, 0:128]
                strip_o[where, :] = piece[:, 128:256]

    get_bl.wait()
    get_bh.wait()
    stage_strips()

    lane = lax.broadcasted_iota(jnp.int32, (8, 128), 1)
    row8 = lax.broadcasted_iota(jnp.int32, (8, 128), 0)
    key8 = lax.rem(lane, 8)
    last = lat == lat_total - 1

    def any_of(value, options):
        hit = value == options[0]
        for option in options[1:]:
            hit = hit | (value == option)
        return hit

    def mask_of(kind):
        places = PLACES[kind]
        mask = jnp.where((lane < 96) & any_of(key8, places), 0.0, NEG)
        if kind > 0:
            differ = jnp.where(any_of(row8, places[3:]), 1, 0) != jnp.where(any_of(key8, places[3:]), 1, 0)
            mask = jnp.where(differ & last, NEG, mask)
        return mask

    def build_tables(kind, target):
        mask = mask_of(kind)
        first, count = TABLE_ROWS[kind]
        stride = count // 2
        heads = 12 if kind == 2 else 6

        def one(index, carry):
            p, head = index // heads, lax.rem(index, heads)
            at = pl.multiple_of((first + p * stride + head) * 8, 8)
            even = strip_e[pl.ds(at, 8), :]
            odd = strip_o[pl.ds(at, 8), :]
            for parity in range(2):
                left, right = (even, odd) if parity == 0 else (odd, even)
                for k in range(6):
                    tile = jnp.where(
                        lane < 48,
                        pltpu.roll(left, (128 - (5 - k) * 8) % 128, 1),
                        pltpu.roll(right, 8 * k + 8 * parity, 1),
                    )
                    row = 48 * parity + 8 * k
                    target[index, row:row + 8, :] = tile + mask
            return carry

        lax.fori_loop(0, 2 * heads, one, 0)

    def stage_tables():
        build_tables(0, t_low.at[0])
        build_tables(1, t_low.at[1])
        build_tables(2, t_high)

    stage_tables()

    wide_lane = lax.broadcasted_iota(jnp.int32, (1, 128), 1)
    low_half = wide_lane < 64
    head_masks = [
        jnp.where(wide_lane // 32 == h, 1.0, 0.0).astype(BF16) for h in range(4)
    ]
    ones = jnp.ones((128, 128), BF16)
    zeros32 = jnp.zeros((32, 128), BF16)

    def norm_unit(u, carry):
        x = xu[u]
        x0, x1, x2 = x[:, 0:128], x[:, 128:256], x[:, 256:384]
        me = jnp.sum(x0 + jnp.where(low_half, x1, 0.0), axis=1, keepdims=True) / 192
        mo = jnp.sum(x2 + jnp.where(low_half, 0.0, x1), axis=1, keepdims=True) / 192
        d0, d1, d2 = x0 - me, x1 - jnp.where(low_half, me, mo), x2 - mo
        q1 = d1 * d1
        ve = jnp.sum(d0 * d0 + jnp.where(low_half, q1, 0.0), axis=1, keepdims=True) / 192
        vo = jnp.sum(d2 * d2 + jnp.where(low_half, 0.0, q1), axis=1, keepdims=True) / 192
        re, ro = lax.rsqrt(ve + EPSILON), lax.rsqrt(vo + EPSILON)
        xn[u, :, 0:128] = (d0 * re).astype(BF16)
        xn[u, :, 128:256] = (d1 * jnp.where(low_half, re, ro)).astype(BF16)
        xn[u, :, 256:384] = (d2 * ro).astype(BF16)
        return carry

    def qkv_units(first, count):
        lax.fori_loop(first, first + count, norm_unit, 0)
        for parity, weight in ((0, w_even), (1, w_odd)):
            rows = xn[first:first + count, :, 128 * parity:128 * parity + 256].reshape(count * 48, 256)
            for part in range(3):
                piece = jnp.dot(rows, weight[:, 256 * part:256 * part + 256], preferred_element_type=F32)
                qkv[first:first + count, 48 * parity:48 * parity + 48, 256 * part:256 * part + 256] = (
                    piece.astype(BF16).reshape(count, 48, 256)
                )

    def group_attend(q, k, v, heads, table):
        stack = jnp.concatenate([q * head_masks[h] for h in range(heads)], axis=0)
        keys = jnp.concatenate([k, zeros32], axis=0)
        scores = lax.dot_general(stack, keys, (((1,), (1,)), ((), ())), preferred_element_type=F32)
        scores = scores * SCALE + table.reshape(heads * 96, 128)
        weights = jnp.exp(scores - jnp.max(scores, axis=1, keepdims=True)).astype(BF16)
        values = jnp.concatenate([jnp.concatenate([v, zeros32], axis=0), ones], axis=1)
        mixed = jnp.dot(weights, values, preferred_element_type=F32)
        top, bottom = mixed[0:96, 0:128], mixed[0:96, 128:256]
        for h in range(1, heads):
            own = wide_lane // 32 == h
            top = jnp.where(own, mixed[96 * h:96 * h + 96, 0:128], top)
            bottom = jnp.where(own, mixed[96 * h:96 * h + 96, 128:256], bottom)
        return (top / bottom).astype(BF16)

    def attend_low(r, first, count):
        def one(u, carry):
            p = lax.rem(u, 2)
            for group, heads in ((0, 4), (1, 2)):
                at = 128 * group
                ob[u, :, at:at + 128] = group_attend(
                    qkv[u, :, at:at + 128],
                    qkv[u, :, 256 + at:384 + at],
                    qkv[u, :, 512 + at:640 + at],
                    heads,
                    t_low[r, pl.ds(p * 6 + 4 * group, heads)],
                )
            return carry

        lax.fori_loop(first, first + count, one, 0)

    def project_low(first, count):
        even = ob[first:first + count, 0:48, :].reshape(count * 48, 256)
        odd = ob[first:first + count, 48:96, :].reshape(count * 48, 256)
        att = jnp.dot(even, wp_even[...], preferred_element_type=F32) + jnp.dot(
            odd, wp_odd[...], preferred_element_type=F32
        )
        att = att.astype(BF16).astype(F32).reshape(count, 48, WIDE)
        lo[first:first + count] = (xu[first:first + count] + att).astype(BF16).astype(F32)

    def low_slab(r, jjr, p):
        return lo[8 * r + 2 * (jjr // 6) + p, 8 * (jjr % 6):8 * (jjr % 6) + 8, :]

    def stage_qkv_a():
        qkv_units(0, 6)

    def stage_attend_a():
        attend_low(0, 0, 6)

    def stage_first_end():
        for k in range(3):
            widen(PAIRS + k, 0, 12)
            put_first(PAIRS + k)
        qkv_units(6, 2)
        attend_low(0, 6, 2)

    def stage_project_a():
        project_low(0, 8)

    def stage_pack_first():
        for jjr in range(PAIRS):
            slab = jnp.where(
                (sub8 >= 2) & (sub8 < 6), low_slab(0, jjr, 1), roll8(low_slab(0, jjr, 0), 4)
            ).astype(BF16)
            if jjr < 3:
                s2_cor[8 * jjr:8 * jjr + 8, :] = slab
            else:
                s2_lat[8 * (jjr - 3):8 * (jjr - 3) + 8, :] = slab

    def stage_second_rows():
        for jj in range(3, PAIRS + 3):
            widen(jj, 12, 3)
            put_second(jj)

    def stage_qkv_b():
        qkv_units(8, 8)

    def stage_second_edge():
        attend_low(1, 8, 2)
        project_low(8, 2)
        for k in range(3):
            for p in range(2):
                at = (2 * k + p) * 8
                s2_lon[at:at + 8, :] = jnp.where(sub8 == 0, low_slab(0, k, p), low_slab(1, k, p)).astype(BF16)
            s2_lon[48 + 8 * k:56 + 8 * k, :] = jnp.where(
                sub8 >= 4, low_slab(0, k, 0), roll8(low_slab(0, k, 1), 4)
            ).astype(BF16)

    def stage_attend_b():
        attend_low(1, 10, 6)

    def stage_project_b():
        project_low(10, 6)

    stage_qkv_a()
    stage_attend_a()

    p1[1].wait_recv()
    stage_first_end()
    stage_project_a()
    stage_pack_first()
    p2[0].start()
    p2[2].start()

    p1[0].wait_recv()
    p1[2].wait_recv()
    stage_second_rows()
    stage_qkv_b()
    stage_second_edge()
    p2[1].start()
    stage_attend_b()
    stage_project_b()

    def stage_gather():
        for col in range(PAIRS):
            jjr = col + 3
            if col < 21:
                halo = r2_lat[8 * col:8 * col + 8, :].astype(F32)
            else:
                k = col - 21
                halo = r2_cor[8 * k:8 * k + 8, :].astype(F32)
                upper = r2_lon[48 + 8 * k:56 + 8 * k, :].astype(F32)
            for p in range(2):
                far = roll8(halo, 4 * p)
                if col < 21:
                    first, second = low_slab(0, jjr, p), low_slab(1, jjr, p)
                    inner = jnp.where(sub8 == 0, first, second)
                else:
                    first = roll8(upper, 4 * p)
                    at = (2 * k + p) * 8
                    inner = r2_lon[at:at + 8, :].astype(F32)
                at = (p * PAIRS + col) * 8
                mi[0, at:at + 8, :] = jnp.where(sub8 == 7, far, inner)
                mi[1, at:at + 8, :] = jnp.where(sub8 >= 6, first, far)

    for copy in p2:
        copy.wait_recv()
    stage_gather()

    def pair_sum(value):
        rows = value.shape[0]
        value = jnp.broadcast_to(value, (rows, 128))
        even = lax.rem(sublanes(rows), 2) == 0
        return value + jnp.where(even, roll8(value, 7), roll8(value, 1))

    def triple(value):
        return jnp.concatenate([value, value, value], axis=1)

    def norm_merge(index, carry):
        rows = pl.ds(pl.multiple_of(index * 48, 48), 48)
        for kind in range(2):
            x = mi[kind, rows, :]
            centre = pair_sum(jnp.sum(x, axis=1, keepdims=True)) / 768
            d = x - triple(centre)
            spread = pair_sum(jnp.sum(d * d, axis=1, keepdims=True)) / 768
            mn[kind, rows, :] = (d * triple(lax.rsqrt(spread + EPSILON))).astype(BF16)
        return carry

    def stage_merge():
        lax.fori_loop(0, 8, norm_merge, 0)
        even_row = lax.rem(sublanes(192), 2) == 0
        for p in range(2):
            rows = slice(192 * p, 192 * p + 192)
            sums = []
            for kind in range(2):
                y0 = jnp.dot(mn[kind, rows, :], wm[0:384, :], preferred_element_type=F32)
                y1 = jnp.dot(mn[kind, rows, :], wm[384:768, :], preferred_element_type=F32)
                sums.append(y0 + roll8(y1, 7) if kind == 0 else roll8(y0, 1) + y1)
            merged = jnp.where(even_row, sums[0], sums[1]).astype(BF16).astype(F32)
            for col in range(PAIRS):
                w, within = col // 12, col % 12
                at = 48 * (within % 2) + 8 * (within // 2)
                mg[2 * p + w, at:at + 8, :] = merged[8 * col:8 * col + 8, :]

    get_wm.wait()
    stage_merge()

    def norm_high(index, carry):
        u, rows = index // 2, pl.ds(pl.multiple_of(lax.rem(index, 2) * 48, 48), 48)
        x = mg[u, rows, :]
        d = x - jnp.sum(x, axis=1, keepdims=True) / 384
        spread = jnp.sum(d * d, axis=1, keepdims=True) / 384
        xh[u, rows, :] = (d * lax.rsqrt(spread + EPSILON)).astype(BF16)
        return carry

    def stage_qkv_high():
        lax.fori_loop(0, 8, norm_high, 0)
        rows = xh[...].reshape(384, 384)
        for part in range(3):
            piece = jnp.dot(rows, wh[:, 384 * part:384 * part + 384], preferred_element_type=F32)
            qh[:, :, 384 * part:384 * part + 384] = piece.astype(BF16).reshape(4, 96, 384)

    get_wh.wait()
    stage_qkv_high()

    def attend_high(u, carry):
        p = u // 2
        for group in range(3):
            at = 128 * group
            oh2[u, :, at:at + 128] = group_attend(
                qh[u, :, at:at + 128],
                qh[u, :, 384 + at:512 + at],
                qh[u, :, 768 + at:896 + at],
                4,
                t_high[pl.ds(p * 12 + 4 * group, 4)],
            )
        return carry

    def stage_attend_high():
        lax.fori_loop(0, 4, attend_high, 0)

    def stage_project_high():
        att = jnp.dot(oh2[...].reshape(384, 384), wph[...], preferred_element_type=F32)
        att = att.astype(BF16).astype(F32).reshape(4, 96, 384)
        res[...] = (mg[...] + att).astype(BF16).astype(F32)

    stage_attend_high()
    get_wph.wait()
    stage_project_high()

    def result(col, p):
        w, within = col // 12, col % 12
        at = 48 * (within % 2) + 8 * (within // 2)
        return res[2 * p + w, at:at + 8, :]

    def own_rows(x, shift):
        return jnp.where(sub8 == (5 + shift) % 8, roll8(x, 3 + shift), roll8(x, 4 + shift))

    def far_rows(x, shift):
        return jnp.where(
            sub8 == shift,
            roll8(x, 4 + shift),
            jnp.where(sub8 == 1 + shift, roll8(x, 3 + shift), roll8(x, 1 + shift)),
        )

    def stage_pack_out():
        for col in range(PAIRS):
            slab = jnp.where(sub8 < 4, far_rows(result(col, 0), 0), far_rows(result(col, 1), 4)).astype(BF16)
            if col < 18:
                s3_lat[8 * col:8 * col + 8, :] = slab
            else:
                k = col - 18
                s3_cor[8 * k:8 * k + 8, :] = slab
                s3_lon[8 * k:8 * k + 8, :] = jnp.where(
                    (sub8 >= 3) & (sub8 < 6), own_rows(result(col, 0), 0), own_rows(result(col, 1), 4)
                ).astype(BF16)

    def stage_out():
        for target in range(PAIRS):
            for p in range(2):
                if target < 6:
                    first = r3_cor[8 * target:8 * target + 8, :].astype(F32)
                    second = roll8(r3_lon[8 * target:8 * target + 8, :].astype(F32), 4 * p)
                else:
                    k = target - 6
                    first = r3_lat[8 * k:8 * k + 8, :].astype(F32)
                    second = own_rows(result(k, p), 0)
                whole = jnp.where(sub8 < 3, roll8(first, 4 * p), second).astype(BF16)
                out_ref[p, :, target * WIDE:(target + 1) * WIDE] = whole[0:6, :]

    stage_pack_out()
    for copy in p3:
        copy.start()
    for copy in p3:
        copy.wait_recv()
    stage_out()
    for copy in p1 + p2 + p3:
        copy.wait_send()


def solution(mesh):
    lat_total, lon_total = mesh.shape["lat"], mesh.shape["lon"]

    def step(fields, qkv_low, proj_low, merge_proj, qkv_high, proj_high, bias_low, bias_high):
        def vmem(*shape, dtype=BF16):
            return pltpu.VMEM(shape, dtype)

        halo = [vmem(176, WIDE), vmem(80, WIDE), vmem(32, WIDE)]
        last_halo = [vmem(144, WIDE), vmem(48, WIDE), vmem(48, WIDE)]
        return pl.pallas_call(
            functools.partial(kernel, lat_total=lat_total, lon_total=lon_total),
            out_shape=jax.ShapeDtypeStruct((2, 6, PAIRS * WIDE), BF16),
            in_specs=[pl.BlockSpec(memory_space=pl.ANY)] * 8,
            out_specs=pl.BlockSpec(memory_space=pltpu.VMEM),
            scratch_shapes=[
                vmem(15, 2, (PAIRS + 3) * WIDE),
                vmem((PAIRS + 3) * 3, 32, 128, dtype=F32),
                vmem(192, 576),
                vmem(192, 192),
                vmem(768, 384),
                vmem(384, 1152),
                vmem(384, 384),
                vmem(1, 6, 2, NPOS, dtype=F32),
                vmem(1, 12, 1, NPOS, dtype=F32),
                vmem(256, 768),
                vmem(256, 768),
                vmem(256, 384),
                vmem(256, 384),
                vmem(384, 256, dtype=F32),
                vmem(512, 128, dtype=F32),
                vmem(512, 128, dtype=F32),
                vmem(2, 12, 96, 128, dtype=F32),
                vmem(24, 96, 128, dtype=F32),
                vmem(16, 48, WIDE, dtype=F32),
                vmem(16, 48, WIDE),
                vmem(16, 96, 768),
                vmem(16, 96, 256),
                vmem(16, 48, WIDE, dtype=F32),
                *halo, *halo, *last_halo, *last_halo,
                vmem(2, 384, WIDE, dtype=F32),
                vmem(2, 384, WIDE),
                vmem(4, 96, WIDE, dtype=F32),
                vmem(4, 96, WIDE),
                vmem(4, 96, 3 * WIDE),
                vmem(4, 96, WIDE),
                vmem(4, 96, WIDE, dtype=F32),
                pltpu.SemaphoreType.DMA((9,)),
                pltpu.SemaphoreType.DMA((9,)),
                pltpu.SemaphoreType.DMA((9,)),
            ],
            compiler_params=pltpu.CompilerParams(
                collective_id=0, has_side_effects=True, vmem_limit_bytes=62 * 1024 * 1024
            ),
            name="block",
        )(
            fields.transpose(1, 0, 2),
            qkv_low,
            proj_low,
            merge_proj,
            qkv_high,
            proj_high,
            bias_low.transpose(0, 2, 1, 3),
            bias_high.transpose(0, 2, 1, 3),
        )

    return jax.shard_map(
        step,
        mesh=mesh,
        in_specs=(
            P(None, "lat", "lon"),
            P(),
            P(),
            P(),
            P(),
            P(),
            P(None, "lat", None, None),
            P(None, "lat", None, None),
        ),
        out_specs=P(None, "lat", "lon"),
        check_vma=False,
    )
```

```python
import functools

import jax
import jax.numpy as jnp
from jax import lax
from jax.experimental import pallas as pl
from jax.experimental.pallas import tpu as pltpu
from jax.sharding import PartitionSpec as P

MESH = pl.DeviceIdType.MESH
F32 = jnp.float32
BF16 = jnp.bfloat16

EPSILON = 1e-05
NEG = -1e30
SCALE = 32 ** (-0.5)
NPOS = 3312
HALF = 828
PAIRS = 24
WIDE = 384
PLACES = ((3, 4, 5, 6, 7, 0), (1, 2, 3, 4, 5, 6), (7, 0, 2, 4, 6, 1))
TABLE_ROWS = ((0, 16), (16, 16), (32, 32))


def sublanes(rows):
    return lax.rem(lax.broadcasted_iota(jnp.int32, (rows, 1), 0), 8)


def roll8(value, shift):
    shift %= 8
    if shift == 0:
        return value
    rows, cols = value.shape
    if rows == 8:
        return pltpu.roll(value, shift, 0)
    return pltpu.roll(value.reshape(rows // 8, 8, cols), shift, 1).reshape(rows, cols)


def kernel(
    fields_hbm, qkv_low_hbm, proj_low_hbm, merge_hbm, qkv_high_hbm, proj_high_hbm, bias_low_hbm,
    bias_high_hbm,
    out_ref,
    fields, flat, wl, wp, wm, wh, wph, bl, bh,
    w_even, w_odd, wp_even, wp_odd,
    tabs, strip_e, strip_o, t_low, t_high,
    xu, xn, qkv, ob, lo,
    s2_lat, s2_lon, s2_cor, r2_lat, r2_lon, r2_cor,
    s3_near, s3_lat, s3_lon, s3_cor, r3_near, r3_lat, r3_lon, r3_cor,
    mi, mn, mg, xh, qh, oh2, res,
    local_sem, send_sem, recv_sem,
    *, lat_total, lon_total,
):
    lat = lax.axis_index("lat")
    lon = lax.axis_index("lon")
    lat_prev = lax.rem(lat + lat_total - 1, lat_total)
    lat_next = lax.rem(lat + 1, lat_total)
    lon_prev = lax.rem(lon + lon_total - 1, lon_total)
    lon_next = lax.rem(lon + 1, lon_total)
    before = ((lat_prev, lon), (lat, lon_prev), (lat_prev, lon_prev))
    after = ((lat_next, lon), (lat, lon_next), (lat_next, lon_next))

    def device(place):
        return {"lat": place[0], "lon": place[1]}

    barrier = pltpu.get_barrier_semaphore()
    for place in before + after:
        pl.semaphore_signal(barrier, inc=1, device_id=device(place), device_id_type=MESH)

    def fetch(source, target, index):
        copy = pltpu.make_async_copy(source, target, local_sem.at[index])
        copy.start()
        return copy

    get_fields = fetch(fields_hbm, fields.at[0:12, :, 0:PAIRS * WIDE], 0)
    get_bl = fetch(bias_low_hbm, bl, 1)
    get_bh = fetch(bias_high_hbm, bh, 2)
    get_wl = fetch(qkv_low_hbm, wl, 4)
    get_wp = fetch(proj_low_hbm, wp, 5)
    get_wm = fetch(merge_hbm, wm, 6)
    get_wh = fetch(qkv_high_hbm, wh, 7)
    get_wph = fetch(proj_high_hbm, wph, 8)

    def remote(source, target, index, place):
        return pltpu.make_async_remote_copy(
            src_ref=source,
            dst_ref=target,
            send_sem=send_sem.at[index],
            recv_sem=recv_sem.at[index],
            device_id=device(place),
            device_id_type=MESH,
        )

    inner, edge = pl.ds(3 * WIDE, 21 * WIDE), pl.ds(0, 3 * WIDE)
    beyond = pl.ds(PAIRS * WIDE, 3 * WIDE)
    p1 = (
        remote(fields_hbm.at[0:3, :, inner], fields.at[12:15, :, inner], 0, before[0]),
        remote(fields_hbm.at[3:12, :, edge], fields.at[3:12, :, beyond], 1, before[1]),
        remote(fields_hbm.at[0:3, :, edge], fields.at[12:15, :, beyond], 2, before[2]),
    )
    p2 = (
        remote(s2_lat, r2_lat, 3, before[0]),
        remote(s2_lon, r2_lon, 4, before[1]),
        remote(s2_cor, r2_cor, 5, before[2]),
    )
    p3 = (
        remote(s3_near, r3_near, 9, after[0]),
        remote(s3_lat, r3_lat, 6, after[0]),
        remote(s3_lon, r3_lon, 7, after[1]),
        remote(s3_cor, r3_cor, 8, after[2]),
    )

    sub8 = sublanes(8)
    pl.semaphore_wait(barrier, 6)
    for copy in p1:
        copy.start()

    def put_unit(r, jjr, p, part, slab):
        u = 8 * r + 2 * (jjr // 6) + p
        xu[u, 8 * (jjr % 6):8 * (jjr % 6) + 8, 128 * part:128 * part + 128] = slab

    def widen(jj, first, count):
        for part in range(3):
            at = jj * WIDE + 128 * part
            flat[3 * jj + part, 2 * first:2 * (first + count), :] = (
                fields[first:first + count, :, at:at + 128].astype(F32).reshape(2 * count, 128)
            )

    def put_first(jj):
        for part in range(3):
            for p in range(2):
                upper = flat[3 * jj + part, pl.ds(p, 8, stride=2), :]
                lower = flat[3 * jj + part, pl.ds(16 + p, 8, stride=2), :]
                put_unit(0, jj - 3, p, part, jnp.where(sub8 >= 3, upper, lower))

    def put_second(jj):
        for part in range(3):
            for p in range(2):
                put_unit(1, jj - 3, p, part, flat[3 * jj + part, pl.ds(16 + p, 8, stride=2), :])

    def stage_own():
        flat[:, 24:32, :] = jnp.zeros_like(flat[:, 24:32, :])
        for jj in range(3, PAIRS):
            widen(jj, 0, 12)
            put_first(jj)

    get_fields.wait()
    stage_own()

    def stage_pad():
        w_even[...] = jnp.zeros_like(w_even)
        w_odd[...] = jnp.zeros_like(w_odd)
        wp_even[...] = jnp.zeros_like(wp_even)
        wp_odd[...] = jnp.zeros_like(wp_odd)
        strip_e[...] = jnp.zeros_like(strip_e)
        strip_o[...] = jnp.zeros_like(strip_o)
        tabs[...] = jnp.zeros_like(tabs)
        for part in range(3):
            piece = wl[:, 192 * part:192 * part + 192]
            w_even[0:192, 256 * part:256 * part + 192] = piece
            w_odd[64:256, 256 * part:256 * part + 192] = piece
        wp_even[0:192, 0:192] = wp[...]
        wp_odd[0:192, 192:384] = wp[...]

    get_wl.wait()
    get_wp.wait()
    stage_pad()

    def one_hot(kind):
        wide = lax.broadcasted_iota(jnp.int32, (8, 256), 1)
        within = lax.rem(wide, 128)
        step, place = within // 8, lax.rem(within, 8)
        offset = jnp.where(wide < 128, 2 * step - 10, 2 * step - 11)
        entry = jnp.full((8, 256), -1, jnp.int32)
        for ib in range(6):
            entry = jnp.where(place == PLACES[kind][ib], 23 * ib + 11 - offset, entry)
        entry = jnp.where(step < jnp.where(wide < 128, 11, 12), entry, -1)
        row = lax.broadcasted_iota(jnp.int32, (256, 256), 0)
        return jnp.where(row == entry[0:1, :], 1.0, 0.0).astype(BF16)

    def stage_strips():
        for p in range(2):
            start = 0 if p == 1 else NPOS - HALF
            for ia in range(6):
                source = slice(start + 138 * ia, start + 138 * ia + 138)
                for r in range(2):
                    at = 96 * r + 16 * ia + 8 * p
                    tabs[at:at + 6, 0:138] = bl[0, :, r, source]
                at = 192 + 32 * ia + 16 * p
                tabs[at:at + 12, 0:138] = bh[0, :, 0, source]
        for kind in range(3):
            first, count = TABLE_ROWS[kind]
            wide = tabs[6 * first:6 * (first + count), :]
            high = wide.astype(BF16)
            rest = wide - high.astype(F32)
            middle = rest.astype(BF16)
            low = (rest - middle.astype(F32)).astype(BF16)
            hot = one_hot(kind)
            spread = jnp.dot(high, hot, preferred_element_type=F32)
            spread = spread + jnp.dot(middle, hot, preferred_element_type=F32)
            spread = spread + jnp.dot(low, hot, preferred_element_type=F32)
            for ia in range(6):
                piece = spread[count * ia:count * (ia + 1)]
                where = pl.ds(first * 8 + PLACES[kind][ia], count, stride=8)
                strip_e[where, :] = piece[:, 0:128]
                strip_o[where, :] = piece[:, 128:256]

    get_bl.wait()
    get_bh.wait()
    stage_strips()

    lane = lax.broadcasted_iota(jnp.int32, (8, 128), 1)
    row8 = lax.broadcasted_iota(jnp.int32, (8, 128), 0)
    key8 = lax.rem(lane, 8)
    last = lat == lat_total - 1

    def any_of(value, options):
        hit = value == options[0]
        for option in options[1:]:
            hit = hit | (value == option)
        return hit

    def mask_of(kind):
        places = PLACES[kind]
        mask = jnp.where((lane < 96) & any_of(key8, places), 0.0, NEG)
        if kind > 0:
            differ = jnp.where(any_of(row8, places[3:]), 1, 0) != jnp.where(any_of(key8, places[3:]), 1, 0)
            mask = jnp.where(differ & last, NEG, mask)
        return mask

    def turn(value, shift):
        return pltpu.roll(value, shift, 1) if shift else value

    def build_tables(kind, target):
        mask = mask_of(kind)
        first, count = TABLE_ROWS[kind]
        stride = count // 2
        heads = 12 if kind == 2 else 6

        def one(p, carry):
            for head in range(heads):
                at = pl.multiple_of((first + p * stride + head) * 8, 8)
                even = strip_e[pl.ds(at, 8), :]
                odd = strip_o[pl.ds(at, 8), :]
                for parity in range(2):
                    left, right = (even, odd) if parity == 0 else (odd, even)
                    for k in range(6):
                        tile = jnp.where(
                            lane < 48,
                            turn(left, (128 - (5 - k) * 8) % 128),
                            turn(right, 8 * k + 8 * parity),
                        )
                        row = 48 * parity + 8 * k
                        target[p * heads + head, row:row + 8, :] = tile + mask
            return carry

        lax.fori_loop(0, 2, one, 0)

    def stage_tables_first():
        build_tables(0, t_low.at[0])

    def stage_tables_second():
        build_tables(1, t_low.at[1])

    def stage_tables_high():
        build_tables(2, t_high)

    stage_tables_first()

    wide_lane = lax.broadcasted_iota(jnp.int32, (1, 128), 1)
    low_half = wide_lane < 64
    head_masks = [
        jnp.where(wide_lane // 32 == h, 1.0, 0.0).astype(BF16) for h in range(4)
    ]
    ones = jnp.ones((128, 128), BF16)
    zeros32 = jnp.zeros((32, 128), BF16)

    def norm_unit(u):
        x = xu[u]
        x0, x1, x2 = x[:, 0:128], x[:, 128:256], x[:, 256:384]
        me = jnp.sum(x0 + jnp.where(low_half, x1, 0.0), axis=1, keepdims=True) / 192
        mo = jnp.sum(x2 + jnp.where(low_half, 0.0, x1), axis=1, keepdims=True) / 192
        d0, d1, d2 = x0 - me, x1 - jnp.where(low_half, me, mo), x2 - mo
        q1 = d1 * d1
        ve = jnp.sum(d0 * d0 + jnp.where(low_half, q1, 0.0), axis=1, keepdims=True) / 192
        vo = jnp.sum(d2 * d2 + jnp.where(low_half, 0.0, q1), axis=1, keepdims=True) / 192
        re, ro = lax.rsqrt(ve + EPSILON), lax.rsqrt(vo + EPSILON)
        xn[u, :, 0:128] = (d0 * re).astype(BF16)
        xn[u, :, 128:256] = (d1 * jnp.where(low_half, re, ro)).astype(BF16)
        xn[u, :, 256:384] = (d2 * ro).astype(BF16)

    def qkv_units(first, count):
        for u in range(first, first + count):
            norm_unit(u)
        for parity, weight in ((0, w_even), (1, w_odd)):
            rows = xn[first:first + count, :, 128 * parity:128 * parity + 256].reshape(count * 48, 256)
            for part in range(3):
                piece = jnp.dot(rows, weight[:, 256 * part:256 * part + 256], preferred_element_type=F32)
                qkv[first:first + count, 48 * parity:48 * parity + 48, 256 * part:256 * part + 256] = (
                    piece.astype(BF16).reshape(count, 48, 256)
                )

    def group_attend(q, k, v, heads, table):
        stack = jnp.concatenate([q * head_masks[h] for h in range(heads)], axis=0)
        keys = jnp.concatenate([k, zeros32], axis=0)
        scores = lax.dot_general(stack, keys, (((1,), (1,)), ((), ())), preferred_element_type=F32)
        scores = scores * SCALE + table.reshape(heads * 96, 128)
        weights = jnp.exp(scores - jnp.max(scores, axis=1, keepdims=True)).astype(BF16)
        values = jnp.concatenate([jnp.concatenate([v, zeros32], axis=0), ones], axis=1)
        mixed = jnp.dot(weights, values, preferred_element_type=F32)
        top, bottom = mixed[0:96, 0:128], mixed[0:96, 128:256]
        for h in range(1, heads):
            own = wide_lane // 32 == h
            top = jnp.where(own, mixed[96 * h:96 * h + 96, 0:128], top)
            bottom = jnp.where(own, mixed[96 * h:96 * h + 96, 128:256], bottom)
        return (top / bottom).astype(BF16)

    def attend_low(r, first, count):
        def one(pair, carry):
            for p in range(2):
                u = 2 * pair + p
                for group, heads in ((0, 4), (1, 2)):
                    at = 128 * group
                    ob[u, :, at:at + 128] = group_attend(
                        qkv[u, :, at:at + 128],
                        qkv[u, :, 256 + at:384 + at],
                        qkv[u, :, 512 + at:640 + at],
                        heads,
                        t_low[r, p * 6 + 4 * group:p * 6 + 4 * group + heads],
                    )
            return carry

        if count == 2:
            one(first // 2, 0)
        else:
            lax.fori_loop(first // 2, (first + count) // 2, one, 0)

    def project_low(first, count):
        even = ob[first:first + count, 0:48, :].reshape(count * 48, 256)
        odd = ob[first:first + count, 48:96, :].reshape(count * 48, 256)
        att = jnp.dot(even, wp_even[...], preferred_element_type=F32) + jnp.dot(
            odd, wp_odd[...], preferred_element_type=F32
        )
        att = att.astype(BF16).astype(F32).reshape(count, 48, WIDE)
        lo[first:first + count] = (xu[first:first + count] + att).astype(BF16).astype(F32)

    def low_slab(r, jjr, p):
        return lo[8 * r + 2 * (jjr // 6) + p, 8 * (jjr % 6):8 * (jjr % 6) + 8, :]

    def stage_qkv_a():
        qkv_units(0, 6)

    def stage_attend_a():
        attend_low(0, 0, 6)

    def stage_first_end():
        for k in range(3):
            widen(PAIRS + k, 0, 12)
            put_first(PAIRS + k)
        qkv_units(6, 2)
        attend_low(0, 6, 2)

    def stage_project_a():
        project_low(0, 8)

    def stage_pack_first():
        for jjr in range(PAIRS):
            slab = jnp.where(
                (sub8 >= 2) & (sub8 < 6), low_slab(0, jjr, 1), roll8(low_slab(0, jjr, 0), 4)
            ).astype(BF16)
            if jjr < 3:
                s2_cor[8 * jjr:8 * jjr + 8, :] = slab
            else:
                s2_lat[8 * (jjr - 3):8 * (jjr - 3) + 8, :] = slab

    def stage_second_rows():
        for jj in range(3, PAIRS + 3):
            widen(jj, 12, 3)
            put_second(jj)

    def stage_qkv_b():
        qkv_units(8, 8)

    def stage_second_edge():
        attend_low(1, 8, 2)
        project_low(8, 2)
        for k in range(3):
            for p in range(2):
                at = (2 * k + p) * 8
                s2_lon[at:at + 8, :] = jnp.where(sub8 == 0, low_slab(0, k, p), low_slab(1, k, p)).astype(BF16)
            s2_lon[48 + 8 * k:56 + 8 * k, :] = jnp.where(
                sub8 >= 4, low_slab(0, k, 0), roll8(low_slab(0, k, 1), 4)
            ).astype(BF16)

    def stage_attend_b():
        attend_low(1, 10, 6)

    def stage_project_b():
        project_low(10, 6)

    stage_qkv_a()
    stage_attend_a()

    p1[1].wait_recv()
    stage_first_end()
    stage_project_a()
    stage_pack_first()
    p2[0].start()
    p2[2].start()
    stage_tables_second()

    p1[0].wait_recv()
    p1[2].wait_recv()
    stage_second_rows()
    stage_qkv_b()
    stage_second_edge()
    p2[1].start()
    stage_attend_b()
    stage_project_b()
    stage_tables_high()

    def stage_gather():
        for col in range(PAIRS):
            jjr = col + 3
            if col < 21:
                halo = r2_lat[8 * col:8 * col + 8, :].astype(F32)
            else:
                k = col - 21
                halo = r2_cor[8 * k:8 * k + 8, :].astype(F32)
                upper = r2_lon[48 + 8 * k:56 + 8 * k, :].astype(F32)
            for p in range(2):
                far = roll8(halo, 4 * p)
                if col < 21:
                    first, second = low_slab(0, jjr, p), low_slab(1, jjr, p)
                    inner = jnp.where(sub8 == 0, first, second)
                else:
                    first = roll8(upper, 4 * p)
                    at = (2 * k + p) * 8
                    inner = r2_lon[at:at + 8, :].astype(F32)
                at = (p * PAIRS + col) * 8
                mi[0, at:at + 8, :] = jnp.where(sub8 == 7, far, inner)
                mi[1, at:at + 8, :] = jnp.where(sub8 >= 6, first, far)

    for copy in p2:
        copy.wait_recv()
    stage_gather()

    def pair_sum(value):
        rows = value.shape[0]
        value = jnp.broadcast_to(value, (rows, 128))
        even = lax.rem(sublanes(rows), 2) == 0
        return value + jnp.where(even, roll8(value, 7), roll8(value, 1))

    def triple(value):
        return jnp.concatenate([value, value, value], axis=1)

    def norm_merge(index):
        rows = slice(index * 48, index * 48 + 48)
        for kind in range(2):
            x = mi[kind, rows, :]
            centre = pair_sum(jnp.sum(x, axis=1, keepdims=True)) / 768
            d = x - triple(centre)
            spread = pair_sum(jnp.sum(d * d, axis=1, keepdims=True)) / 768
            mn[kind, rows, :] = (d * triple(lax.rsqrt(spread + EPSILON))).astype(BF16)

    def stage_merge():
        for index in range(8):
            norm_merge(index)
        even_row = lax.rem(sublanes(192), 2) == 0
        for p in range(2):
            rows = slice(192 * p, 192 * p + 192)
            sums = []
            for kind in range(2):
                y0 = jnp.dot(mn[kind, rows, :], wm[0:384, :], preferred_element_type=F32)
                y1 = jnp.dot(mn[kind, rows, :], wm[384:768, :], preferred_element_type=F32)
                sums.append(y0 + roll8(y1, 7) if kind == 0 else roll8(y0, 1) + y1)
            merged = jnp.where(even_row, sums[0], sums[1]).astype(BF16).astype(F32)
            for col in range(PAIRS):
                w, within = col // 12, col % 12
                at = 48 * (within % 2) + 8 * (within // 2)
                mg[2 * w + p, at:at + 8, :] = merged[8 * col:8 * col + 8, :]

    get_wm.wait()
    stage_merge()

    def norm_high(u):
        x = mg[u]
        d = x - jnp.sum(x, axis=1, keepdims=True) / 384
        spread = jnp.sum(d * d, axis=1, keepdims=True) / 384
        xh[u] = (d * lax.rsqrt(spread + EPSILON)).astype(BF16)

    def stage_qkv_high():
        for u in range(4):
            norm_high(u)
        rows = xh[...].reshape(384, 384)
        for part in range(3):
            piece = jnp.dot(rows, wh[:, 384 * part:384 * part + 384], preferred_element_type=F32)
            qh[:, :, 384 * part:384 * part + 384] = piece.astype(BF16).reshape(4, 96, 384)

    get_wh.wait()
    stage_qkv_high()

    def attend_high(w):
        for u in (2 * w, 2 * w + 1):
            p = u % 2
            for group in range(3):
                at = 128 * group
                oh2[u, :, at:at + 128] = group_attend(
                    qh[u, :, at:at + 128],
                    qh[u, :, 384 + at:512 + at],
                    qh[u, :, 768 + at:896 + at],
                    4,
                    t_high[p * 12 + 4 * group:p * 12 + 4 * group + 4],
                )
        units = slice(2 * w, 2 * w + 2)
        att = jnp.dot(oh2[units].reshape(192, 384), wph[...], preferred_element_type=F32)
        att = att.astype(BF16).astype(F32).reshape(2, 96, 384)
        res[units] = (mg[units] + att).astype(BF16).astype(F32)

    def result(col, p):
        w, within = col // 12, col % 12
        at = 48 * (within % 2) + 8 * (within // 2)
        return res[2 * w + p, at:at + 8, :]

    def own_rows(x, shift):
        return jnp.where(sub8 == (5 + shift) % 8, roll8(x, 3 + shift), roll8(x, 4 + shift))

    def far_rows(x, shift):
        return jnp.where(
            sub8 == shift,
            roll8(x, 4 + shift),
            jnp.where(sub8 == 1 + shift, roll8(x, 3 + shift), roll8(x, 1 + shift)),
        )

    def pack_out(w):
        for col in range(12 * w, 12 * w + 12):
            slab = jnp.where(sub8 < 4, far_rows(result(col, 0), 0), far_rows(result(col, 1), 4)).astype(BF16)
            if col < 12:
                s3_near[8 * col:8 * col + 8, :] = slab
            elif col < 18:
                k = col - 12
                s3_lat[8 * k:8 * k + 8, :] = slab
            else:
                k = col - 18
                s3_cor[8 * k:8 * k + 8, :] = slab
                s3_lon[8 * k:8 * k + 8, :] = jnp.where(
                    (sub8 >= 3) & (sub8 < 6), own_rows(result(col, 0), 0), own_rows(result(col, 1), 4)
                ).astype(BF16)

    def put_out(target):
        for p in range(2):
            if target < 6:
                first = r3_cor[8 * target:8 * target + 8, :].astype(F32)
                second = roll8(r3_lon[8 * target:8 * target + 8, :].astype(F32), 4 * p)
            else:
                k = target - 6
                received, k = (r3_near, k) if k < 12 else (r3_lat, k - 12)
                first = received[8 * k:8 * k + 8, :].astype(F32)
                second = own_rows(result(target - 6, p), 0)
            whole = jnp.where(sub8 < 3, roll8(first, 4 * p), second)
            for part in range(3):
                flat[3 * target + part, pl.ds(p, 8, stride=2), :] = whole[:, 128 * part:128 * part + 128]
        for part in range(3):
            at = target * WIDE + 128 * part
            out_ref[:, :, at:at + 128] = flat[3 * target + part, 0:12, :].reshape(6, 2, 128).astype(BF16)

    def stage_high_first():
        attend_high(0)
        pack_out(0)

    def stage_high_second():
        attend_high(1)
        pack_out(1)

    def stage_out_first():
        for target in range(6, 18):
            put_out(target)

    def stage_out_second():
        for target in (*range(6), *range(18, PAIRS)):
            put_out(target)

    get_wph.wait()
    stage_high_first()
    p3[0].start()
    stage_high_second()
    p3[1].start()
    p3[2].start()
    p3[3].start()
    p3[0].wait_recv()
    stage_out_first()
    p3[1].wait_recv()
    p3[2].wait_recv()
    p3[3].wait_recv()
    stage_out_second()
    for copy in p1 + p2 + p3:
        copy.wait_send()


def solution(mesh):
    lat_total, lon_total = mesh.shape["lat"], mesh.shape["lon"]

    def step(fields, qkv_low, proj_low, merge_proj, qkv_high, proj_high, bias_low, bias_high):
        def vmem(*shape, dtype=BF16):
            return pltpu.VMEM(shape, dtype)

        halo = [vmem(176, WIDE), vmem(80, WIDE), vmem(32, WIDE)]
        last_halo = [vmem(96, WIDE), vmem(48, WIDE), vmem(48, WIDE), vmem(48, WIDE)]
        return pl.pallas_call(
            functools.partial(kernel, lat_total=lat_total, lon_total=lon_total),
            out_shape=jax.ShapeDtypeStruct((6, 2, PAIRS * WIDE), BF16),
            in_specs=[pl.BlockSpec(memory_space=pl.ANY)] * 8,
            out_specs=pl.BlockSpec(memory_space=pltpu.VMEM),
            scratch_shapes=[
                vmem(15, 2, (PAIRS + 3) * WIDE),
                vmem((PAIRS + 3) * 3, 32, 128, dtype=F32),
                vmem(192, 576),
                vmem(192, 192),
                vmem(768, 384),
                vmem(384, 1152),
                vmem(384, 384),
                vmem(1, 6, 2, NPOS, dtype=F32),
                vmem(1, 12, 1, NPOS, dtype=F32),
                vmem(256, 768),
                vmem(256, 768),
                vmem(256, 384),
                vmem(256, 384),
                vmem(384, 256, dtype=F32),
                vmem(512, 128, dtype=F32),
                vmem(512, 128, dtype=F32),
                vmem(2, 12, 96, 128, dtype=F32),
                vmem(24, 96, 128, dtype=F32),
                vmem(16, 48, WIDE, dtype=F32),
                vmem(16, 48, WIDE),
                vmem(16, 96, 768),
                vmem(16, 96, 256),
                vmem(16, 48, WIDE, dtype=F32),
                *halo, *halo, *last_halo, *last_halo,
                vmem(2, 384, WIDE, dtype=F32),
                vmem(2, 384, WIDE),
                vmem(4, 96, WIDE, dtype=F32),
                vmem(4, 96, WIDE),
                vmem(4, 96, 3 * WIDE),
                vmem(4, 96, WIDE),
                vmem(4, 96, WIDE, dtype=F32),
                pltpu.SemaphoreType.DMA((10,)),
                pltpu.SemaphoreType.DMA((10,)),
                pltpu.SemaphoreType.DMA((10,)),
            ],
            compiler_params=pltpu.CompilerParams(
                collective_id=0, has_side_effects=True, vmem_limit_bytes=62 * 1024 * 1024
            ),
            name="block",
        )(
            fields.transpose(1, 0, 2),
            qkv_low,
            proj_low,
            merge_proj,
            qkv_high,
            proj_high,
            bias_low.transpose(0, 2, 1, 3),
            bias_high.transpose(0, 2, 1, 3),
        ).transpose(1, 0, 2)

    return jax.shard_map(
        step,
        mesh=mesh,
        in_specs=(
            P(None, "lat", "lon"),
            P(),
            P(),
            P(),
            P(),
            P(),
            P(None, "lat", None, None),
            P(None, "lat", None, None),
        ),
        out_specs=P(None, "lat", "lon"),
        check_vma=False,
    )
```

```python
import functools

import jax
import jax.numpy as jnp
from jax import lax
from jax.experimental import pallas as pl
from jax.experimental.pallas import tpu as pltpu
from jax.sharding import PartitionSpec as P

MESH = pl.DeviceIdType.MESH
F32 = jnp.float32
BF16 = jnp.bfloat16

EPSILON = 1e-05
NEG = -1e30
SCALE = 32 ** (-0.5)
NPOS = 3312
HALF = 828
PAIRS = 24
WIDE = 384
PLACES = ((3, 4, 5, 6, 7, 0), (1, 2, 3, 4, 5, 6), (7, 0, 2, 4, 6, 1))
TABLE_ROWS = ((0, 16), (16, 16), (32, 32))


def sublanes(rows):
    return lax.rem(lax.broadcasted_iota(jnp.int32, (rows, 1), 0), 8)


def roll8(value, shift):
    shift %= 8
    if shift == 0:
        return value
    rows, cols = value.shape
    if rows == 8:
        return pltpu.roll(value, shift, 0)
    return pltpu.roll(value.reshape(rows // 8, 8, cols), shift, 1).reshape(rows, cols)


def kernel(
    fields_hbm, qkv_low_hbm, proj_low_hbm, merge_hbm, qkv_high_hbm, proj_high_hbm, bias_low_hbm,
    bias_high_hbm,
    out_ref,
    fields, flat, wl, wp, wm, wh, wph, bl, bh,
    w_even, w_odd, wp_even, wp_odd,
    tabs, strip_e, strip_o, t_low, t_high,
    xu, xn, qkv, ob, lo,
    s2_lat, s2_lon, s2_cor, r2_lat, r2_lon, r2_cor,
    s3_near, s3_lat, s3_lon, s3_cor, r3_near, r3_lat, r3_lon, r3_cor,
    mi, mn, mg, xh, qh, oh2, res,
    local_sem, send_sem, recv_sem,
    *, lat_total, lon_total,
):
    lat = lax.axis_index("lat")
    lon = lax.axis_index("lon")
    lat_prev = lax.rem(lat + lat_total - 1, lat_total)
    lat_next = lax.rem(lat + 1, lat_total)
    lon_prev = lax.rem(lon + lon_total - 1, lon_total)
    lon_next = lax.rem(lon + 1, lon_total)
    before = ((lat_prev, lon), (lat, lon_prev), (lat_prev, lon_prev))
    after = ((lat_next, lon), (lat, lon_next), (lat_next, lon_next))

    def device(place):
        return {"lat": place[0], "lon": place[1]}

    barrier = pltpu.get_barrier_semaphore()
    for place in after:
        pl.semaphore_signal(barrier, inc=1, device_id=device(place), device_id_type=MESH)

    def fetch(source, target, index):
        copy = pltpu.make_async_copy(source, target, local_sem.at[index])
        copy.start()
        return copy

    get_fields = fetch(fields_hbm, fields.at[0:12, :, 0:PAIRS * WIDE], 0)
    get_bl = fetch(bias_low_hbm, bl, 1)
    get_bh = fetch(bias_high_hbm, bh, 2)
    get_wl = fetch(qkv_low_hbm, wl, 4)
    get_wp = fetch(proj_low_hbm, wp, 5)
    get_wm = fetch(merge_hbm, wm, 6)
    get_wh = fetch(qkv_high_hbm, wh, 7)
    get_wph = fetch(proj_high_hbm, wph, 8)

    def remote(source, target, index, place):
        return pltpu.make_async_remote_copy(
            src_ref=source,
            dst_ref=target,
            send_sem=send_sem.at[index],
            recv_sem=recv_sem.at[index],
            device_id=device(place),
            device_id_type=MESH,
        )

    inner, edge = pl.ds(3 * WIDE, 21 * WIDE), pl.ds(0, 3 * WIDE)
    beyond = pl.ds(PAIRS * WIDE, 3 * WIDE)
    p1 = (
        remote(fields_hbm.at[0:3, :, inner], fields.at[12:15, :, inner], 0, before[0]),
        remote(fields_hbm.at[3:12, :, edge], fields.at[3:12, :, beyond], 1, before[1]),
        remote(fields_hbm.at[0:3, :, edge], fields.at[12:15, :, beyond], 2, before[2]),
    )
    p2 = (
        remote(s2_lat, r2_lat, 3, before[0]),
        remote(s2_lon, r2_lon, 4, before[1]),
        remote(s2_cor, r2_cor, 5, before[2]),
    )
    p3 = (
        remote(s3_near, r3_near, 9, after[0]),
        remote(s3_lat, r3_lat, 6, after[0]),
        remote(s3_lon, r3_lon, 7, after[1]),
        remote(s3_cor, r3_cor, 8, after[2]),
    )

    sub8 = sublanes(8)
    pl.semaphore_wait(barrier, 3)
    for copy in p1:
        copy.start()

    def put_unit(r, jjr, p, part, slab):
        u = 8 * r + 2 * (jjr // 6) + p
        xu[u, 8 * (jjr % 6):8 * (jjr % 6) + 8, 128 * part:128 * part + 128] = slab

    def widen(jj, first, count):
        for part in range(3):
            at = jj * WIDE + 128 * part
            flat[3 * jj + part, 2 * first:2 * (first + count), :] = (
                fields[first:first + count, :, at:at + 128].astype(F32).reshape(2 * count, 128)
            )

    def put_first(jj):
        for part in range(3):
            for p in range(2):
                upper = flat[3 * jj + part, pl.ds(p, 8, stride=2), :]
                lower = flat[3 * jj + part, pl.ds(16 + p, 8, stride=2), :]
                put_unit(0, jj - 3, p, part, jnp.where(sub8 >= 3, upper, lower))

    def put_second(jj):
        for part in range(3):
            for p in range(2):
                put_unit(1, jj - 3, p, part, flat[3 * jj + part, pl.ds(16 + p, 8, stride=2), :])

    def stage_own():
        flat[:, 24:32, :] = jnp.zeros_like(flat[:, 24:32, :])
        for jj in range(3, PAIRS):
            widen(jj, 0, 12)
            put_first(jj)

    get_fields.wait()
    stage_own()

    def stage_pad():
        w_even[...] = jnp.zeros_like(w_even)
        w_odd[...] = jnp.zeros_like(w_odd)
        wp_even[...] = jnp.zeros_like(wp_even)
        wp_odd[...] = jnp.zeros_like(wp_odd)
        strip_e[...] = jnp.zeros_like(strip_e)
        strip_o[...] = jnp.zeros_like(strip_o)
        tabs[...] = jnp.zeros_like(tabs)
        for part in range(3):
            piece = wl[:, 192 * part:192 * part + 192]
            w_even[0:192, 256 * part:256 * part + 192] = piece
            w_odd[64:256, 256 * part:256 * part + 192] = piece
        wp_even[0:192, 0:192] = wp[...]
        wp_odd[0:192, 192:384] = wp[...]

    get_wl.wait()
    get_wp.wait()
    stage_pad()

    def one_hot(kind):
        wide = lax.broadcasted_iota(jnp.int32, (8, 256), 1)
        within = lax.rem(wide, 128)
        step, place = within // 8, lax.rem(within, 8)
        offset = jnp.where(wide < 128, 2 * step - 10, 2 * step - 11)
        entry = jnp.full((8, 256), -1, jnp.int32)
        for ia in range(6):
            entry = jnp.where(place == PLACES[kind][ia], 23 * ia + 11 + offset, entry)
        entry = jnp.where(step < jnp.where(wide < 128, 11, 12), entry, -1)
        row = lax.broadcasted_iota(jnp.int32, (256, 256), 0)
        return jnp.where(row == entry[0:1, :], 1.0, 0.0).astype(BF16)

    def stage_strips():
        for p in range(2):
            start = 0 if p == 1 else NPOS - HALF
            for ia in range(6):
                for ib in range(6):
                    source = slice(start + 138 * ia + 23 * ib, start + 138 * ia + 23 * ib + 23)
                    target = slice(23 * ia, 23 * ia + 23)
                    for r in range(2):
                        at = 96 * r + 16 * ib + 8 * p
                        tabs[at:at + 6, target] = bl[0, :, r, source]
                    at = 192 + 32 * ib + 16 * p
                    tabs[at:at + 12, target] = bh[0, :, 0, source]
        for kind in range(3):
            first, count = TABLE_ROWS[kind]
            wide = tabs[6 * first:6 * (first + count), :]
            high = wide.astype(BF16)
            rest = wide - high.astype(F32)
            middle = rest.astype(BF16)
            low = (rest - middle.astype(F32)).astype(BF16)
            hot = one_hot(kind)
            spread = jnp.dot(high, hot, preferred_element_type=F32)
            spread = spread + jnp.dot(middle, hot, preferred_element_type=F32)
            spread = spread + jnp.dot(low, hot, preferred_element_type=F32)
            for ib in range(6):
                piece = spread[count * ib:count * (ib + 1)]
                where = pl.ds(first * 8 + PLACES[kind][ib], count, stride=8)
                strip_e[where, :] = piece[:, 0:128]
                strip_o[where, :] = piece[:, 128:256]

    get_bl.wait()
    get_bh.wait()
    stage_strips()

    lane = lax.broadcasted_iota(jnp.int32, (8, 128), 1)
    row8 = lax.broadcasted_iota(jnp.int32, (8, 128), 0)
    lane8 = lax.rem(lane, 8)
    last = lat == lat_total - 1

    def any_of(value, options):
        hit = value == options[0]
        for option in options[1:]:
            hit = hit | (value == option)
        return hit

    def mask_of(kind):
        places = PLACES[kind]
        mask = jnp.where(any_of(row8, places), 0.0, NEG)
        if kind > 0:
            differ = jnp.where(any_of(row8, places[3:]), 1, 0) != jnp.where(any_of(lane8, places[3:]), 1, 0)
            mask = jnp.where(differ & last, NEG, mask)
        return mask

    def turn(value, shift):
        return pltpu.roll(value, shift, 1) if shift else value

    def build_tables(kind, target):
        mask = mask_of(kind)
        first, count = TABLE_ROWS[kind]
        stride = count // 2
        heads = 12 if kind == 2 else 6

        def one(p, carry):
            for head in range(heads):
                at = pl.multiple_of((first + p * stride + head) * 8, 8)
                even = strip_e[pl.ds(at, 8), :]
                odd = strip_o[pl.ds(at, 8), :]
                for parity in range(2):
                    left, right = (even, odd) if parity == 0 else (odd, even)
                    for k in range(6):
                        tile = jnp.where(
                            lane < 48,
                            turn(left, (128 - (5 - k) * 8) % 128),
                            turn(right, 8 * k + 8 * parity),
                        )
                        row = 48 * parity + 8 * k
                        target[p * heads + head, row:row + 8, :] = tile + mask
            return carry

        lax.fori_loop(0, 2, one, 0)

    def stage_tables_first():
        build_tables(0, t_low.at[0])

    def stage_tables_second():
        build_tables(1, t_low.at[1])

    def stage_tables_high():
        build_tables(2, t_high)

    stage_tables_first()

    wide_lane = lax.broadcasted_iota(jnp.int32, (1, 128), 1)
    low_half = wide_lane < 64
    head_masks = [
        jnp.where(wide_lane // 32 == h, 1.0, 0.0).astype(BF16) for h in range(4)
    ]
    ones = jnp.ones((16, 96), BF16)

    def norm_unit(u):
        x = xu[u]
        x0, x1, x2 = x[:, 0:128], x[:, 128:256], x[:, 256:384]
        me = jnp.sum(x0 + jnp.where(low_half, x1, 0.0), axis=1, keepdims=True) / 192
        mo = jnp.sum(x2 + jnp.where(low_half, 0.0, x1), axis=1, keepdims=True) / 192
        d0, d1, d2 = x0 - me, x1 - jnp.where(low_half, me, mo), x2 - mo
        q1 = d1 * d1
        ve = jnp.sum(d0 * d0 + jnp.where(low_half, q1, 0.0), axis=1, keepdims=True) / 192
        vo = jnp.sum(d2 * d2 + jnp.where(low_half, 0.0, q1), axis=1, keepdims=True) / 192
        re, ro = lax.rsqrt(ve + EPSILON), lax.rsqrt(vo + EPSILON)
        xn[u, :, 0:128] = (d0 * re).astype(BF16)
        xn[u, :, 128:256] = (d1 * jnp.where(low_half, re, ro)).astype(BF16)
        xn[u, :, 256:384] = (d2 * ro).astype(BF16)

    def qkv_units(first, count):
        for u in range(first, first + count):
            norm_unit(u)
        for parity, weight in ((0, w_even), (1, w_odd)):
            rows = xn[first:first + count, :, 128 * parity:128 * parity + 256].reshape(count * 48, 256)
            for part in range(3):
                piece = jnp.dot(rows, weight[:, 256 * part:256 * part + 256], preferred_element_type=F32)
                qkv[first:first + count, 48 * parity:48 * parity + 48, 256 * part:256 * part + 256] = (
                    piece.astype(BF16).reshape(count, 48, 256)
                )

    def group_attend(q, k, v, heads, table):
        stack = jnp.concatenate([k * head_masks[h] for h in range(heads)], axis=0)
        scores = lax.dot_general(stack, q, (((1,), (1,)), ((), ())), preferred_element_type=F32)
        scores = scores.reshape(heads, 96, 96) * SCALE + table
        weights = jnp.exp(scores - jnp.max(scores, axis=1, keepdims=True)).astype(BF16)
        turned = v.T
        mixed = []
        for h in range(heads):
            values = jnp.concatenate([turned[32 * h:32 * h + 32], ones], axis=0)
            sums = jnp.dot(values, weights[h], preferred_element_type=F32)
            mixed.append(sums[0:32] / sums[32:33])
        if heads < 4:
            mixed.append(jnp.zeros((128 - 32 * heads, 96), F32))
        return jnp.concatenate(mixed, axis=0).T.astype(BF16)

    def attend_low(r, first, count):
        def one(pair, carry):
            for p in range(2):
                u = 2 * pair + p
                for group, heads in ((0, 4), (1, 2)):
                    at = 128 * group
                    ob[u, :, at:at + 128] = group_attend(
                        qkv[u, :, at:at + 128],
                        qkv[u, :, 256 + at:384 + at],
                        qkv[u, :, 512 + at:640 + at],
                        heads,
                        t_low[r, p * 6 + 4 * group:p * 6 + 4 * group + heads, :, 0:96],
                    )
            return carry

        if count == 2:
            one(first // 2, 0)
        else:
            lax.fori_loop(first // 2, (first + count) // 2, one, 0)

    def project_low(first, count):
        even = ob[first:first + count, 0:48, :].reshape(count * 48, 256)
        odd = ob[first:first + count, 48:96, :].reshape(count * 48, 256)
        att = jnp.dot(even, wp_even[...], preferred_element_type=F32) + jnp.dot(
            odd, wp_odd[...], preferred_element_type=F32
        )
        att = att.astype(BF16).astype(F32).reshape(count, 48, WIDE)
        lo[first:first + count] = (xu[first:first + count] + att).astype(BF16).astype(F32)

    def low_slab(r, jjr, p):
        return lo[8 * r + 2 * (jjr // 6) + p, 8 * (jjr % 6):8 * (jjr % 6) + 8, :]

    def stage_qkv_a():
        qkv_units(0, 6)

    def stage_attend_a():
        attend_low(0, 0, 6)

    def stage_first_end():
        for k in range(3):
            widen(PAIRS + k, 0, 12)
            put_first(PAIRS + k)
        qkv_units(6, 2)
        attend_low(0, 6, 2)

    def stage_project_a():
        project_low(0, 8)

    def stage_pack_first():
        for jjr in range(PAIRS):
            slab = jnp.where(
                (sub8 >= 2) & (sub8 < 6), low_slab(0, jjr, 1), roll8(low_slab(0, jjr, 0), 4)
            ).astype(BF16)
            if jjr < 3:
                s2_cor[8 * jjr:8 * jjr + 8, :] = slab
            else:
                s2_lat[8 * (jjr - 3):8 * (jjr - 3) + 8, :] = slab

    def stage_second_rows():
        for jj in range(3, PAIRS + 3):
            widen(jj, 12, 3)
            put_second(jj)

    def stage_qkv_b():
        qkv_units(8, 8)

    def stage_second_edge():
        attend_low(1, 8, 2)
        project_low(8, 2)
        for k in range(3):
            for p in range(2):
                at = (2 * k + p) * 8
                s2_lon[at:at + 8, :] = jnp.where(sub8 == 0, low_slab(0, k, p), low_slab(1, k, p)).astype(BF16)
            s2_lon[48 + 8 * k:56 + 8 * k, :] = jnp.where(
                sub8 >= 4, low_slab(0, k, 0), roll8(low_slab(0, k, 1), 4)
            ).astype(BF16)

    def stage_attend_b():
        attend_low(1, 10, 6)

    def stage_project_b():
        project_low(10, 6)

    stage_qkv_a()
    stage_attend_a()

    p1[1].wait_recv()
    stage_first_end()
    stage_project_a()
    stage_pack_first()
    p2[0].start()
    p2[2].start()
    stage_tables_second()

    p1[0].wait_recv()
    p1[2].wait_recv()
    stage_second_rows()
    stage_qkv_b()
    stage_second_edge()
    p2[1].start()
    stage_attend_b()
    stage_project_b()
    stage_tables_high()

    def stage_gather():
        for col in range(PAIRS):
            jjr = col + 3
            if col < 21:
                halo = r2_lat[8 * col:8 * col + 8, :].astype(F32)
            else:
                k = col - 21
                halo = r2_cor[8 * k:8 * k + 8, :].astype(F32)
                upper = r2_lon[48 + 8 * k:56 + 8 * k, :].astype(F32)
            for p in range(2):
                far = roll8(halo, 4 * p)
                if col < 21:
                    first, second = low_slab(0, jjr, p), low_slab(1, jjr, p)
                    inner = jnp.where(sub8 == 0, first, second)
                else:
                    first = roll8(upper, 4 * p)
                    at = (2 * k + p) * 8
                    inner = r2_lon[at:at + 8, :].astype(F32)
                at = (p * PAIRS + col) * 8
                mi[0, at:at + 8, :] = jnp.where(sub8 == 7, far, inner)
                mi[1, at:at + 8, :] = jnp.where(sub8 >= 6, first, far)

    for copy in p2:
        copy.wait_recv()
    stage_gather()

    def pair_sum(value):
        rows = value.shape[0]
        value = jnp.broadcast_to(value, (rows, 128))
        even = lax.rem(sublanes(rows), 2) == 0
        return value + jnp.where(even, roll8(value, 7), roll8(value, 1))

    def triple(value):
        return jnp.concatenate([value, value, value], axis=1)

    def norm_merge(index):
        rows = slice(index * 48, index * 48 + 48)
        for kind in range(2):
            x = mi[kind, rows, :]
            centre = pair_sum(jnp.sum(x, axis=1, keepdims=True)) / 768
            d = x - triple(centre)
            spread = pair_sum(jnp.sum(d * d, axis=1, keepdims=True)) / 768
            mn[kind, rows, :] = (d * triple(lax.rsqrt(spread + EPSILON))).astype(BF16)

    def stage_merge():
        for index in range(8):
            norm_merge(index)
        even_row = lax.rem(sublanes(192), 2) == 0
        for p in range(2):
            rows = slice(192 * p, 192 * p + 192)
            sums = []
            for kind in range(2):
                y0 = jnp.dot(mn[kind, rows, :], wm[0:384, :], preferred_element_type=F32)
                y1 = jnp.dot(mn[kind, rows, :], wm[384:768, :], preferred_element_type=F32)
                sums.append(y0 + roll8(y1, 7) if kind == 0 else roll8(y0, 1) + y1)
            merged = jnp.where(even_row, sums[0], sums[1]).astype(BF16).astype(F32)
            for col in range(PAIRS):
                w, within = col // 12, col % 12
                at = 48 * (within % 2) + 8 * (within // 2)
                mg[2 * w + p, at:at + 8, :] = merged[8 * col:8 * col + 8, :]

    get_wm.wait()
    stage_merge()

    def norm_high(u):
        x = mg[u]
        d = x - jnp.sum(x, axis=1, keepdims=True) / 384
        spread = jnp.sum(d * d, axis=1, keepdims=True) / 384
        xh[u] = (d * lax.rsqrt(spread + EPSILON)).astype(BF16)

    def stage_qkv_high():
        for u in range(4):
            norm_high(u)
        rows = xh[...].reshape(384, 384)
        for part in range(3):
            piece = jnp.dot(rows, wh[:, 384 * part:384 * part + 384], preferred_element_type=F32)
            qh[:, :, 384 * part:384 * part + 384] = piece.astype(BF16).reshape(4, 96, 384)

    get_wh.wait()
    stage_qkv_high()

    def attend_high(w):
        for u in (2 * w, 2 * w + 1):
            p = u % 2
            for group in range(3):
                at = 128 * group
                oh2[u, :, at:at + 128] = group_attend(
                    qh[u, :, at:at + 128],
                    qh[u, :, 384 + at:512 + at],
                    qh[u, :, 768 + at:896 + at],
                    4,
                    t_high[p * 12 + 4 * group:p * 12 + 4 * group + 4, :, 0:96],
                )
        units = slice(2 * w, 2 * w + 2)
        att = jnp.dot(oh2[units].reshape(192, 384), wph[...], preferred_element_type=F32)
        att = att.astype(BF16).astype(F32).reshape(2, 96, 384)
        res[units] = (mg[units] + att).astype(BF16).astype(F32)

    def result(col, p):
        w, within = col // 12, col % 12
        at = 48 * (within % 2) + 8 * (within // 2)
        return res[2 * w + p, at:at + 8, :]

    def own_rows(x, shift):
        return jnp.where(sub8 == (5 + shift) % 8, roll8(x, 3 + shift), roll8(x, 4 + shift))

    def far_rows(x, shift):
        return jnp.where(
            sub8 == shift,
            roll8(x, 4 + shift),
            jnp.where(sub8 == 1 + shift, roll8(x, 3 + shift), roll8(x, 1 + shift)),
        )

    def pack_out(w):
        for col in range(12 * w, 12 * w + 12):
            slab = jnp.where(sub8 < 4, far_rows(result(col, 0), 0), far_rows(result(col, 1), 4)).astype(BF16)
            if col < 12:
                s3_near[8 * col:8 * col + 8, :] = slab
            elif col < 18:
                k = col - 12
                s3_lat[8 * k:8 * k + 8, :] = slab
            else:
                k = col - 18
                s3_cor[8 * k:8 * k + 8, :] = slab
                s3_lon[8 * k:8 * k + 8, :] = jnp.where(
                    (sub8 >= 3) & (sub8 < 6), own_rows(result(col, 0), 0), own_rows(result(col, 1), 4)
                ).astype(BF16)

    def put_out(target):
        for p in range(2):
            if target < 6:
                first = r3_cor[8 * target:8 * target + 8, :].astype(F32)
                second = roll8(r3_lon[8 * target:8 * target + 8, :].astype(F32), 4 * p)
            else:
                k = target - 6
                received, k = (r3_near, k) if k < 12 else (r3_lat, k - 12)
                first = received[8 * k:8 * k + 8, :].astype(F32)
                second = own_rows(result(target - 6, p), 0)
            whole = jnp.where(sub8 < 3, roll8(first, 4 * p), second)
            for part in range(3):
                flat[3 * target + part, pl.ds(p, 8, stride=2), :] = whole[:, 128 * part:128 * part + 128]
        for part in range(3):
            at = target * WIDE + 128 * part
            out_ref[:, :, at:at + 128] = flat[3 * target + part, 0:12, :].reshape(6, 2, 128).astype(BF16)

    def stage_high_first():
        attend_high(0)
        pack_out(0)

    def stage_high_second():
        attend_high(1)
        pack_out(1)

    def stage_out_first():
        for target in range(6, 18):
            put_out(target)

    def stage_out_second():
        for target in (*range(6), *range(18, PAIRS)):
            put_out(target)

    get_wph.wait()
    stage_high_first()
    p3[0].start()
    stage_high_second()
    p3[1].start()
    p3[2].start()
    p3[3].start()
    p3[0].wait_recv()
    stage_out_first()
    p3[1].wait_recv()
    p3[2].wait_recv()
    p3[3].wait_recv()
    stage_out_second()
    for copy in p1 + p2 + p3:
        copy.wait_send()


def solution(mesh):
    lat_total, lon_total = mesh.shape["lat"], mesh.shape["lon"]

    def step(fields, qkv_low, proj_low, merge_proj, qkv_high, proj_high, bias_low, bias_high):
        def vmem(*shape, dtype=BF16):
            return pltpu.VMEM(shape, dtype)

        operands = (
            fields.transpose(1, 0, 2),
            qkv_low,
            proj_low,
            merge_proj,
            qkv_high,
            proj_high,
            bias_low.transpose(0, 2, 1, 3),
            bias_high.transpose(0, 2, 1, 3),
        )
        operands = [pltpu.with_memory_space_constraint(operand, pltpu.HBM) for operand in operands]
        halo = [vmem(176, WIDE), vmem(80, WIDE), vmem(32, WIDE)]
        last_halo = [vmem(96, WIDE), vmem(48, WIDE), vmem(48, WIDE), vmem(48, WIDE)]
        return pl.pallas_call(
            functools.partial(kernel, lat_total=lat_total, lon_total=lon_total),
            out_shape=jax.ShapeDtypeStruct((6, 2, PAIRS * WIDE), BF16),
            in_specs=[pl.BlockSpec(memory_space=pl.ANY)] * 8,
            out_specs=pl.BlockSpec(memory_space=pltpu.VMEM),
            scratch_shapes=[
                vmem(15, 2, (PAIRS + 3) * WIDE),
                vmem((PAIRS + 3) * 3, 32, 128, dtype=F32),
                vmem(192, 576),
                vmem(192, 192),
                vmem(768, 384),
                vmem(384, 1152),
                vmem(384, 384),
                vmem(1, 6, 2, NPOS, dtype=F32),
                vmem(1, 12, 1, NPOS, dtype=F32),
                vmem(256, 768),
                vmem(256, 768),
                vmem(256, 384),
                vmem(256, 384),
                vmem(384, 256, dtype=F32),
                vmem(512, 128, dtype=F32),
                vmem(512, 128, dtype=F32),
                vmem(2, 12, 96, 128, dtype=F32),
                vmem(24, 96, 128, dtype=F32),
                vmem(16, 48, WIDE, dtype=F32),
                vmem(16, 48, WIDE),
                vmem(16, 96, 768),
                vmem(16, 96, 256),
                vmem(16, 48, WIDE, dtype=F32),
                *halo, *halo, *last_halo, *last_halo,
                vmem(2, 384, WIDE, dtype=F32),
                vmem(2, 384, WIDE),
                vmem(4, 96, WIDE, dtype=F32),
                vmem(4, 96, WIDE),
                vmem(4, 96, 3 * WIDE),
                vmem(4, 96, WIDE),
                vmem(4, 96, WIDE, dtype=F32),
                pltpu.SemaphoreType.DMA((10,)),
                pltpu.SemaphoreType.DMA((10,)),
                pltpu.SemaphoreType.DMA((10,)),
            ],
            compiler_params=pltpu.CompilerParams(
                collective_id=0, has_side_effects=True, vmem_limit_bytes=28 * 1024 * 1024
            ),
            name="block",
        )(*operands).transpose(1, 0, 2)

    return jax.shard_map(
        step,
        mesh=mesh,
        in_specs=(
            P(None, "lat", "lon"),
            P(),
            P(),
            P(),
            P(),
            P(),
            P(None, "lat", None, None),
            P(None, "lat", None, None),
        ),
        out_specs=P(None, "lat", "lon"),
        check_vma=False,
    )
```

```python
import functools

import jax
import jax.numpy as jnp
from jax import lax
from jax.experimental import pallas as pl
from jax.experimental.pallas import tpu as pltpu
from jax.sharding import PartitionSpec as P

MESH = pl.DeviceIdType.MESH
F32 = jnp.float32
BF16 = jnp.bfloat16

EPSILON = 1e-05
NEG = -1e30
SCALE = 32 ** (-0.5)
NPOS = 3312
HALF = 828
PAIRS = 24
WIDE = 384
PLACES = ((3, 4, 5, 6, 7, 0), (1, 2, 3, 4, 5, 6), (7, 0, 2, 4, 6, 1))
TABLE_ROWS = ((0, 16), (16, 16), (32, 32))


def sublanes(rows):
    return lax.rem(lax.broadcasted_iota(jnp.int32, (rows, 1), 0), 8)


def roll8(value, shift):
    shift %= 8
    if shift == 0:
        return value
    rows, cols = value.shape
    if rows == 8:
        return pltpu.roll(value, shift, 0)
    return pltpu.roll(value.reshape(rows // 8, 8, cols), shift, 1).reshape(rows, cols)


def kernel(
    fields_hbm, qkv_low_hbm, proj_low_hbm, merge_hbm, qkv_high_hbm, proj_high_hbm, bias_low_hbm,
    bias_high_hbm,
    out_ref,
    fields, flat, wl, wp, wm, wh, wph, bl, bh,
    w_even, w_odd, wp_even, wp_odd,
    tabs, strip_e, strip_o, t_low, t_high,
    xu, xn, qkv, ob, lo,
    s2_lat, s2_lon, s2_cor, r2_lat, r2_lon, r2_cor,
    s3_near, s3_lat, s3_lon, s3_cor, r3_near, r3_lat, r3_lon, r3_cor,
    mi, mn, mg, xh, qh, oh2, res,
    local_sem, send_sem, recv_sem,
    *, lat_total, lon_total,
):
    lat = lax.axis_index("lat")
    lon = lax.axis_index("lon")
    lat_prev = lax.rem(lat + lat_total - 1, lat_total)
    lat_next = lax.rem(lat + 1, lat_total)
    lon_prev = lax.rem(lon + lon_total - 1, lon_total)
    lon_next = lax.rem(lon + 1, lon_total)
    before = ((lat_prev, lon), (lat, lon_prev), (lat_prev, lon_prev))
    after = ((lat_next, lon), (lat, lon_next), (lat_next, lon_next))

    def device(place):
        return {"lat": place[0], "lon": place[1]}

    barrier = pltpu.get_barrier_semaphore()
    for place in after:
        pl.semaphore_signal(barrier, inc=1, device_id=device(place), device_id_type=MESH)

    def fetch(source, target, index):
        copy = pltpu.make_async_copy(source, target, local_sem.at[index])
        copy.start()
        return copy

    get_fields = fetch(fields_hbm, fields.at[0:12, :, 0:PAIRS * WIDE], 0)
    get_bl = fetch(bias_low_hbm, bl, 1)
    get_bh = fetch(bias_high_hbm, bh, 2)
    get_wl = fetch(qkv_low_hbm, wl, 4)
    get_wp = fetch(proj_low_hbm, wp, 5)
    get_wm = fetch(merge_hbm, wm, 6)
    get_wh = fetch(qkv_high_hbm, wh, 7)
    get_wph = fetch(proj_high_hbm, wph, 8)

    def remote(source, target, index, place):
        return pltpu.make_async_remote_copy(
            src_ref=source,
            dst_ref=target,
            send_sem=send_sem.at[index],
            recv_sem=recv_sem.at[index],
            device_id=device(place),
            device_id_type=MESH,
        )

    inner, edge = pl.ds(3 * WIDE, 21 * WIDE), pl.ds(0, 3 * WIDE)
    beyond = pl.ds(PAIRS * WIDE, 3 * WIDE)
    p1 = (
        remote(fields_hbm.at[0:3, :, inner], fields.at[12:15, :, inner], 0, before[0]),
        remote(fields_hbm.at[3:12, :, edge], fields.at[3:12, :, beyond], 1, before[1]),
        remote(fields_hbm.at[0:3, :, edge], fields.at[12:15, :, beyond], 2, before[2]),
    )
    p2 = (
        remote(s2_lat, r2_lat, 3, before[0]),
        remote(s2_lon, r2_lon, 4, before[1]),
        remote(s2_cor, r2_cor, 5, before[2]),
    )
    p3 = (
        remote(s3_near, r3_near, 9, after[0]),
        remote(s3_lat, r3_lat, 6, after[0]),
        remote(s3_lon, r3_lon, 7, after[1]),
        remote(s3_cor, r3_cor, 8, after[2]),
    )

    sub8 = sublanes(8)
    pl.semaphore_wait(barrier, 3)
    for copy in p1:
        copy.start()

    def put_unit(r, jjr, p, part, slab):
        u = 8 * r + 2 * (jjr // 6) + p
        xu[u, 8 * (jjr % 6):8 * (jjr % 6) + 8, 128 * part:128 * part + 128] = slab

    def widen(jj, first, count):
        for part in range(3):
            at = jj * WIDE + 128 * part
            flat[3 * jj + part, 2 * first:2 * (first + count), :] = (
                fields[first:first + count, :, at:at + 128].astype(F32).reshape(2 * count, 128)
            )

    def put_first(jj):
        for part in range(3):
            for p in range(2):
                upper = flat[3 * jj + part, pl.ds(p, 8, stride=2), :]
                lower = flat[3 * jj + part, pl.ds(16 + p, 8, stride=2), :]
                put_unit(0, jj - 3, p, part, jnp.where(sub8 >= 3, upper, lower))

    def put_second(jj):
        for part in range(3):
            for p in range(2):
                put_unit(1, jj - 3, p, part, flat[3 * jj + part, pl.ds(16 + p, 8, stride=2), :])

    def stage_own():
        flat[:, 24:32, :] = jnp.zeros_like(flat[:, 24:32, :])
        for jj in range(3, PAIRS):
            widen(jj, 0, 12)
            put_first(jj)

    get_fields.wait()
    stage_own()

    def stage_pad():
        w_even[...] = jnp.zeros_like(w_even)
        w_odd[...] = jnp.zeros_like(w_odd)
        wp_even[...] = jnp.zeros_like(wp_even)
        wp_odd[...] = jnp.zeros_like(wp_odd)
        strip_e[...] = jnp.zeros_like(strip_e)
        strip_o[...] = jnp.zeros_like(strip_o)
        tabs[...] = jnp.zeros_like(tabs)
        for part in range(3):
            piece = wl[:, 192 * part:192 * part + 192]
            w_even[0:192, 256 * part:256 * part + 192] = piece
            w_odd[64:256, 256 * part:256 * part + 192] = piece
        wp_even[0:192, 0:192] = wp[...]
        wp_odd[0:192, 192:384] = wp[...]

    get_wl.wait()
    get_wp.wait()
    stage_pad()

    def one_hot(kind):
        wide = lax.broadcasted_iota(jnp.int32, (8, 256), 1)
        within = lax.rem(wide, 128)
        step, place = within // 8, lax.rem(within, 8)
        offset = jnp.where(wide < 128, 2 * step - 10, 2 * step - 11)
        entry = jnp.full((8, 256), -1, jnp.int32)
        for ia in range(6):
            entry = jnp.where(place == PLACES[kind][ia], 23 * ia + 11 + offset, entry)
        entry = jnp.where(step < jnp.where(wide < 128, 11, 12), entry, -1)
        row = lax.broadcasted_iota(jnp.int32, (256, 256), 0)
        return jnp.where(row == entry[0:1, :], 1.0, 0.0).astype(BF16)

    def build_strips(kinds):
        for p in range(2):
            start = 0 if p == 1 else NPOS - HALF
            for ia in range(6):
                for ib in range(6):
                    source = slice(start + 138 * ia + 23 * ib, start + 138 * ia + 23 * ib + 23)
                    target = slice(23 * ia, 23 * ia + 23)
                    for kind in kinds:
                        if kind < 2:
                            at = 96 * kind + 16 * ib + 8 * p
                            tabs[at:at + 6, target] = bl[0, :, kind, source]
                        else:
                            at = 192 + 32 * ib + 16 * p
                            tabs[at:at + 12, target] = bh[0, :, 0, source]
        for kind in kinds:
            first, count = TABLE_ROWS[kind]
            wide = tabs[6 * first:6 * (first + count), :]
            high = wide.astype(BF16)
            rest = wide - high.astype(F32)
            middle = rest.astype(BF16)
            low = (rest - middle.astype(F32)).astype(BF16)
            hot = one_hot(kind)
            spread = jnp.dot(high, hot, preferred_element_type=F32)
            spread = spread + jnp.dot(middle, hot, preferred_element_type=F32)
            spread = spread + jnp.dot(low, hot, preferred_element_type=F32)
            for ib in range(6):
                piece = spread[count * ib:count * (ib + 1)]
                where = pl.ds(first * 8 + PLACES[kind][ib], count, stride=8)
                strip_e[where, :] = piece[:, 0:128]
                strip_o[where, :] = piece[:, 128:256]


    lane = lax.broadcasted_iota(jnp.int32, (8, 128), 1)
    row8 = lax.broadcasted_iota(jnp.int32, (8, 128), 0)
    lane8 = lax.rem(lane, 8)
    last = lat == lat_total - 1

    def any_of(value, options):
        hit = value == options[0]
        for option in options[1:]:
            hit = hit | (value == option)
        return hit

    def mask_of(kind):
        places = PLACES[kind]
        mask = jnp.where(any_of(row8, places), 0.0, NEG)
        if kind > 0:
            differ = jnp.where(any_of(row8, places[3:]), 1, 0) != jnp.where(any_of(lane8, places[3:]), 1, 0)
            mask = jnp.where(differ & last, NEG, mask)
        return mask

    def turn(value, shift):
        return pltpu.roll(value, shift, 1) if shift else value

    def build_tables(kind, target):
        mask = mask_of(kind)
        first, count = TABLE_ROWS[kind]
        stride = count // 2
        heads = 12 if kind == 2 else 6

        def one(p, carry):
            for head in range(heads):
                at = pl.multiple_of((first + p * stride + head) * 8, 8)
                even = strip_e[pl.ds(at, 8), :]
                odd = strip_o[pl.ds(at, 8), :]
                for parity in range(2):
                    left, right = (even, odd) if parity == 0 else (odd, even)
                    for k in range(6):
                        tile = jnp.where(
                            lane < 48,
                            turn(left, (128 - (5 - k) * 8) % 128),
                            turn(right, 8 * k + 8 * parity),
                        )
                        row = 48 * parity + 8 * k
                        target[p * heads + head, row:row + 8, :] = tile + mask
            return carry

        lax.fori_loop(0, 2, one, 0)

    def stage_tables_low():
        build_strips((0, 1))
        build_tables(0, t_low.at[0])
        build_tables(1, t_low.at[1])

    def stage_tables_high():
        build_strips((2,))
        build_tables(2, t_high)

    get_bl.wait()
    stage_tables_low()

    wide_lane = lax.broadcasted_iota(jnp.int32, (1, 128), 1)
    low_half = wide_lane < 64
    head_masks = [
        jnp.where(wide_lane // 32 == h, 1.0, 0.0).astype(BF16) for h in range(4)
    ]
    ones = jnp.ones((16, 96), BF16)

    def norm_unit(u):
        x = xu[u]
        x0, x1, x2 = x[:, 0:128], x[:, 128:256], x[:, 256:384]
        me = jnp.sum(x0 + jnp.where(low_half, x1, 0.0), axis=1, keepdims=True) / 192
        mo = jnp.sum(x2 + jnp.where(low_half, 0.0, x1), axis=1, keepdims=True) / 192
        d0, d1, d2 = x0 - me, x1 - jnp.where(low_half, me, mo), x2 - mo
        q1 = d1 * d1
        ve = jnp.sum(d0 * d0 + jnp.where(low_half, q1, 0.0), axis=1, keepdims=True) / 192
        vo = jnp.sum(d2 * d2 + jnp.where(low_half, 0.0, q1), axis=1, keepdims=True) / 192
        re, ro = lax.rsqrt(ve + EPSILON), lax.rsqrt(vo + EPSILON)
        xn[u, :, 0:128] = (d0 * re).astype(BF16)
        xn[u, :, 128:256] = (d1 * jnp.where(low_half, re, ro)).astype(BF16)
        xn[u, :, 256:384] = (d2 * ro).astype(BF16)

    def qkv_units(first, count):
        for u in range(first, first + count):
            norm_unit(u)
        for parity, weight in ((0, w_even), (1, w_odd)):
            rows = xn[first:first + count, :, 128 * parity:128 * parity + 256].reshape(count * 48, 256)
            for part in range(3):
                piece = jnp.dot(rows, weight[:, 256 * part:256 * part + 256], preferred_element_type=F32)
                qkv[first:first + count, 48 * parity:48 * parity + 48, 256 * part:256 * part + 256] = (
                    piece.astype(BF16).reshape(count, 48, 256)
                )

    def group_attend(q, k, v, heads, table):
        stack = jnp.concatenate([k * head_masks[h] for h in range(heads)], axis=0)
        scores = lax.dot_general(stack, q, (((1,), (1,)), ((), ())), preferred_element_type=F32)
        scores = scores.reshape(heads, 96, 96) * SCALE + table
        weights = jnp.exp(scores - jnp.max(scores, axis=1, keepdims=True)).astype(BF16)
        turned = v.T
        mixed = []
        for h in range(heads):
            values = jnp.concatenate([turned[32 * h:32 * h + 32], ones], axis=0)
            sums = jnp.dot(values, weights[h], preferred_element_type=F32)
            mixed.append(sums[0:32] / sums[32:33])
        if heads < 4:
            mixed.append(jnp.zeros((128 - 32 * heads, 96), F32))
        return jnp.concatenate(mixed, axis=0).T.astype(BF16)

    def attend_low(r, first, count):
        def one(pair, carry):
            for p in range(2):
                u = 2 * pair + p
                for group, heads in ((0, 4), (1, 2)):
                    at = 128 * group
                    ob[u, :, at:at + 128] = group_attend(
                        qkv[u, :, at:at + 128],
                        qkv[u, :, 256 + at:384 + at],
                        qkv[u, :, 512 + at:640 + at],
                        heads,
                        t_low[r, p * 6 + 4 * group:p * 6 + 4 * group + heads, :, 0:96],
                    )
            return carry

        if count == 2:
            one(first // 2, 0)
        else:
            lax.fori_loop(first // 2, (first + count) // 2, one, 0)


    def project_low(first, count):
        even = ob[first:first + count, 0:48, :].reshape(count * 48, 256)
        odd = ob[first:first + count, 48:96, :].reshape(count * 48, 256)
        att = jnp.dot(even, wp_even[...], preferred_element_type=F32) + jnp.dot(
            odd, wp_odd[...], preferred_element_type=F32
        )
        att = att.astype(BF16).astype(F32).reshape(count, 48, WIDE)
        lo[first:first + count] = (xu[first:first + count] + att).astype(BF16).astype(F32)

    def low_slab(r, jjr, p):
        return lo[8 * r + 2 * (jjr // 6) + p, 8 * (jjr % 6):8 * (jjr % 6) + 8, :]

    def stage_qkv_a():
        qkv_units(0, 6)

    def stage_attend_a():
        attend_low(0, 0, 6)

    def stage_edges():
        for k in range(3):
            widen(PAIRS + k, 0, 12)
            put_first(PAIRS + k)
        for jj in range(3, PAIRS + 3):
            widen(jj, 12, 3)
            put_second(jj)
        qkv_units(6, 4)
        attend_low(0, 6, 2)
        attend_low(1, 8, 2)
        project_low(0, 10)

    def stage_pack_low():
        for jjr in range(PAIRS):
            slab = jnp.where(
                (sub8 >= 2) & (sub8 < 6), low_slab(0, jjr, 1), roll8(low_slab(0, jjr, 0), 4)
            ).astype(BF16)
            if jjr < 3:
                s2_cor[8 * jjr:8 * jjr + 8, :] = slab
            else:
                s2_lat[8 * (jjr - 3):8 * (jjr - 3) + 8, :] = slab
        for k in range(3):
            for p in range(2):
                at = (2 * k + p) * 8
                s2_lon[at:at + 8, :] = jnp.where(sub8 == 0, low_slab(0, k, p), low_slab(1, k, p)).astype(BF16)
            s2_lon[48 + 8 * k:56 + 8 * k, :] = jnp.where(
                sub8 >= 4, low_slab(0, k, 0), roll8(low_slab(0, k, 1), 4)
            ).astype(BF16)

    def stage_qkv_b():
        qkv_units(10, 6)

    def stage_attend_b():
        attend_low(1, 10, 6)

    def stage_project_b():
        project_low(10, 6)

    stage_qkv_a()
    stage_attend_a()

    for copy in p1:
        copy.wait_recv()
    stage_edges()
    stage_pack_low()
    for copy in p2:
        copy.start()
    stage_qkv_b()
    stage_attend_b()
    stage_project_b()
    get_bh.wait()
    stage_tables_high()

    def gather(w):
        for col in range(12 * w, 12 * w + 12):
            jjr = col + 3
            if col < 21:
                halo = r2_lat[8 * col:8 * col + 8, :].astype(F32)
            else:
                k = col - 21
                halo = r2_cor[8 * k:8 * k + 8, :].astype(F32)
                upper = r2_lon[48 + 8 * k:56 + 8 * k, :].astype(F32)
            for p in range(2):
                far = roll8(halo, 4 * p)
                if col < 21:
                    first, second = low_slab(0, jjr, p), low_slab(1, jjr, p)
                    inner = jnp.where(sub8 == 0, first, second)
                else:
                    first = roll8(upper, 4 * p)
                    at = (2 * k + p) * 8
                    inner = r2_lon[at:at + 8, :].astype(F32)
                at = ((2 * w + p) * 12 + col % 12) * 8
                mi[0, at:at + 8, :] = jnp.where(sub8 == 7, far, inner)
                mi[1, at:at + 8, :] = jnp.where(sub8 >= 6, first, far)

    def pair_sum(value):
        rows = value.shape[0]
        value = jnp.broadcast_to(value, (rows, 128))
        even = lax.rem(sublanes(rows), 2) == 0
        return value + jnp.where(even, roll8(value, 7), roll8(value, 1))

    def triple(value):
        return jnp.concatenate([value, value, value], axis=1)

    def norm_merge(index):
        rows = slice(index * 48, index * 48 + 48)
        for kind in range(2):
            x = mi[kind, rows, :]
            centre = pair_sum(jnp.sum(x, axis=1, keepdims=True)) / 768
            d = x - triple(centre)
            spread = pair_sum(jnp.sum(d * d, axis=1, keepdims=True)) / 768
            mn[kind, rows, :] = (d * triple(lax.rsqrt(spread + EPSILON))).astype(BF16)

    even_row = lax.rem(sublanes(192), 2) == 0

    def merge(w):
        for index in range(4 * w, 4 * w + 4):
            norm_merge(index)
        rows = slice(192 * w, 192 * w + 192)
        sums = []
        for kind in range(2):
            y0 = jnp.dot(mn[kind, rows, :], wm[0:384, :], preferred_element_type=F32)
            y1 = jnp.dot(mn[kind, rows, :], wm[384:768, :], preferred_element_type=F32)
            sums.append(y0 + roll8(y1, 7) if kind == 0 else roll8(y0, 1) + y1)
        merged = jnp.where(even_row, sums[0], sums[1]).astype(BF16).astype(F32)
        for p in range(2):
            for col in range(12):
                at, source = 48 * (col % 2) + 8 * (col // 2), (12 * p + col) * 8
                mg[2 * w + p, at:at + 8, :] = merged[source:source + 8, :]

    def norm_high(u):
        x = mg[u]
        d = x - jnp.sum(x, axis=1, keepdims=True) / 384
        spread = jnp.sum(d * d, axis=1, keepdims=True) / 384
        xh[u] = (d * lax.rsqrt(spread + EPSILON)).astype(BF16)

    def qkv_high_units(w):
        units = slice(2 * w, 2 * w + 2)
        for u in (2 * w, 2 * w + 1):
            norm_high(u)
        rows = xh[units].reshape(192, 384)
        for part in range(3):
            piece = jnp.dot(rows, wh[:, 384 * part:384 * part + 384], preferred_element_type=F32)
            qh[units, :, 384 * part:384 * part + 384] = piece.astype(BF16).reshape(2, 96, 384)

    def attend_high(w):
        for u in (2 * w, 2 * w + 1):
            p = u % 2
            for group in range(3):
                at = 128 * group
                oh2[u, :, at:at + 128] = group_attend(
                    qh[u, :, at:at + 128],
                    qh[u, :, 384 + at:512 + at],
                    qh[u, :, 768 + at:896 + at],
                    4,
                    t_high[p * 12 + 4 * group:p * 12 + 4 * group + 4, :, 0:96],
                )
        units = slice(2 * w, 2 * w + 2)
        att = jnp.dot(oh2[units].reshape(192, 384), wph[...], preferred_element_type=F32)
        att = att.astype(BF16).astype(F32).reshape(2, 96, 384)
        res[units] = (mg[units] + att).astype(BF16).astype(F32)

    def result(col, p):
        w, within = col // 12, col % 12
        at = 48 * (within % 2) + 8 * (within // 2)
        return res[2 * w + p, at:at + 8, :]

    def own_rows(x, shift):
        return jnp.where(sub8 == (5 + shift) % 8, roll8(x, 3 + shift), roll8(x, 4 + shift))

    def far_rows(x, shift):
        return jnp.where(
            sub8 == shift,
            roll8(x, 4 + shift),
            jnp.where(sub8 == 1 + shift, roll8(x, 3 + shift), roll8(x, 1 + shift)),
        )

    def pack_out(w):
        for col in range(12 * w, 12 * w + 12):
            slab = jnp.where(sub8 < 4, far_rows(result(col, 0), 0), far_rows(result(col, 1), 4)).astype(BF16)
            if col < 12:
                s3_near[8 * col:8 * col + 8, :] = slab
            elif col < 18:
                k = col - 12
                s3_lat[8 * k:8 * k + 8, :] = slab
            else:
                k = col - 18
                s3_cor[8 * k:8 * k + 8, :] = slab
                s3_lon[8 * k:8 * k + 8, :] = jnp.where(
                    (sub8 >= 3) & (sub8 < 6), own_rows(result(col, 0), 0), own_rows(result(col, 1), 4)
                ).astype(BF16)

    def put_out(target):
        for p in range(2):
            if target < 6:
                first = r3_cor[8 * target:8 * target + 8, :].astype(F32)
                second = roll8(r3_lon[8 * target:8 * target + 8, :].astype(F32), 4 * p)
            else:
                k = target - 6
                received, k = (r3_near, k) if k < 12 else (r3_lat, k - 12)
                first = received[8 * k:8 * k + 8, :].astype(F32)
                second = own_rows(result(target - 6, p), 0)
            whole = jnp.where(sub8 < 3, roll8(first, 4 * p), second)
            for part in range(3):
                flat[3 * target + part, pl.ds(p, 8, stride=2), :] = whole[:, 128 * part:128 * part + 128]
        for part in range(3):
            at = target * WIDE + 128 * part
            out_ref[:, :, at:at + 128] = flat[3 * target + part, 0:12, :].reshape(6, 2, 128).astype(BF16)

    def level_high(w):
        gather(w)
        merge(w)
        qkv_high_units(w)
        attend_high(w)
        pack_out(w)

    def stage_high_first():
        level_high(0)

    def stage_high_second():
        level_high(1)

    def stage_out_first():
        for target in range(6, 18):
            put_out(target)

    def stage_out_second():
        for target in (*range(6), *range(18, PAIRS)):
            put_out(target)

    get_wm.wait()
    get_wh.wait()
    get_wph.wait()
    p2[0].wait_recv()
    stage_high_first()
    p3[0].start()
    p2[1].wait_recv()
    p2[2].wait_recv()
    stage_high_second()
    p3[1].start()
    p3[2].start()
    p3[3].start()
    p3[0].wait_recv()
    stage_out_first()
    p3[1].wait_recv()
    p3[2].wait_recv()
    p3[3].wait_recv()
    stage_out_second()
    for copy in p1 + p2 + p3:
        copy.wait_send()


def solution(mesh):
    lat_total, lon_total = mesh.shape["lat"], mesh.shape["lon"]

    def step(fields, qkv_low, proj_low, merge_proj, qkv_high, proj_high, bias_low, bias_high):
        def vmem(*shape, dtype=BF16):
            return pltpu.VMEM(shape, dtype)

        operands = (
            fields.transpose(1, 0, 2),
            qkv_low,
            proj_low,
            merge_proj,
            qkv_high,
            proj_high,
            bias_low.transpose(0, 2, 1, 3),
            bias_high.transpose(0, 2, 1, 3),
        )
        operands = [pltpu.with_memory_space_constraint(operand, pltpu.HBM) for operand in operands]
        halo = [vmem(176, WIDE), vmem(80, WIDE), vmem(32, WIDE)]
        last_halo = [vmem(96, WIDE), vmem(48, WIDE), vmem(48, WIDE), vmem(48, WIDE)]
        return pl.pallas_call(
            functools.partial(kernel, lat_total=lat_total, lon_total=lon_total),
            out_shape=jax.ShapeDtypeStruct((6, 2, PAIRS * WIDE), BF16),
            in_specs=[pl.BlockSpec(memory_space=pl.ANY)] * 8,
            out_specs=pl.BlockSpec(memory_space=pltpu.VMEM),
            scratch_shapes=[
                vmem(15, 2, (PAIRS + 3) * WIDE),
                vmem((PAIRS + 3) * 3, 32, 128, dtype=F32),
                vmem(192, 576),
                vmem(192, 192),
                vmem(768, 384),
                vmem(384, 1152),
                vmem(384, 384),
                vmem(1, 6, 2, NPOS, dtype=F32),
                vmem(1, 12, 1, NPOS, dtype=F32),
                vmem(256, 768),
                vmem(256, 768),
                vmem(256, 384),
                vmem(256, 384),
                vmem(384, 256, dtype=F32),
                vmem(512, 128, dtype=F32),
                vmem(512, 128, dtype=F32),
                vmem(2, 12, 96, 128, dtype=F32),
                vmem(24, 96, 128, dtype=F32),
                vmem(16, 48, WIDE, dtype=F32),
                vmem(16, 48, WIDE),
                vmem(16, 96, 768),
                vmem(16, 96, 256),
                vmem(16, 48, WIDE, dtype=F32),
                *halo, *halo, *last_halo, *last_halo,
                vmem(2, 384, WIDE, dtype=F32),
                vmem(2, 384, WIDE),
                vmem(4, 96, WIDE, dtype=F32),
                vmem(4, 96, WIDE),
                vmem(4, 96, 3 * WIDE),
                vmem(4, 96, WIDE),
                vmem(4, 96, WIDE, dtype=F32),
                pltpu.SemaphoreType.DMA((10,)),
                pltpu.SemaphoreType.DMA((10,)),
                pltpu.SemaphoreType.DMA((10,)),
            ],
            compiler_params=pltpu.CompilerParams(
                collective_id=0, has_side_effects=True, vmem_limit_bytes=28 * 1024 * 1024
            ),
            name="block",
        )(*operands).transpose(1, 0, 2)

    return jax.shard_map(
        step,
        mesh=mesh,
        in_specs=(
            P(None, "lat", "lon"),
            P(),
            P(),
            P(),
            P(),
            P(),
            P(None, "lat", None, None),
            P(None, "lat", None, None),
        ),
        out_specs=P(None, "lat", "lon"),
        check_vma=False,
    )
```

```python
import functools

import jax
import jax.numpy as jnp
from jax import lax
from jax.experimental import pallas as pl
from jax.experimental.pallas import tpu as pltpu
from jax.sharding import PartitionSpec as P

MESH = pl.DeviceIdType.MESH
F32 = jnp.float32
BF16 = jnp.bfloat16

EPSILON = 1e-05
NEG = -1e30
SCALE = 32 ** (-0.5)
NPOS = 3312
HALF = 828
PAIRS = 24
WIDE = 384
PLACES = ((3, 4, 5, 6, 7, 0), (1, 2, 3, 4, 5, 6), (7, 0, 2, 4, 6, 1))
TABLE_ROWS = ((0, 16), (16, 16), (32, 32))


def sublanes(rows):
    return lax.rem(lax.broadcasted_iota(jnp.int32, (rows, 1), 0), 8)


def roll8(value, shift):
    shift %= 8
    if shift == 0:
        return value
    rows, cols = value.shape
    if rows == 8:
        return pltpu.roll(value, shift, 0)
    return pltpu.roll(value.reshape(rows // 8, 8, cols), shift, 1).reshape(rows, cols)


def kernel(
    fields_hbm, qkv_low_hbm, proj_low_hbm, merge_hbm, qkv_high_hbm, proj_high_hbm, bias_low_hbm,
    bias_high_hbm,
    out_ref,
    fields, flat, wl, wp, wm, wh, wph, bl, bh,
    w_even, w_odd, wp_even, wp_odd,
    tabs, strip_e, strip_o, t_low, t_high,
    xu, xn, qkv, ob, lo,
    s2_lat, s2_lon, s2_cor, r2_lat, r2_lon, r2_cor,
    s3_near, s3_lat, s3_lon, s3_cor, r3_near, r3_lat, r3_lon, r3_cor,
    mi, mn, mg, xh, qh, oh2, res,
    local_sem, send_sem, recv_sem,
    *, lat_total, lon_total,
):
    lat = lax.axis_index("lat")
    lon = lax.axis_index("lon")
    lat_prev = lax.rem(lat + lat_total - 1, lat_total)
    lat_next = lax.rem(lat + 1, lat_total)
    lon_prev = lax.rem(lon + lon_total - 1, lon_total)
    lon_next = lax.rem(lon + 1, lon_total)
    before = ((lat_prev, lon), (lat, lon_prev), (lat_prev, lon_prev))
    after = ((lat_next, lon), (lat, lon_next), (lat_next, lon_next))

    def device(place):
        return {"lat": place[0], "lon": place[1]}

    barrier = pltpu.get_barrier_semaphore()
    for place in after:
        pl.semaphore_signal(barrier, inc=1, device_id=device(place), device_id_type=MESH)

    def fetch(source, target, index):
        copy = pltpu.make_async_copy(source, target, local_sem.at[index])
        copy.start()
        return copy

    get_fields = fetch(fields_hbm, fields.at[0:12, :, 0:PAIRS * WIDE], 0)
    get_bl = fetch(bias_low_hbm, bl, 1)
    get_bh = fetch(bias_high_hbm, bh, 2)
    get_wl = fetch(qkv_low_hbm, wl, 4)
    get_wp = fetch(proj_low_hbm, wp, 5)
    get_wm = fetch(merge_hbm, wm, 6)
    get_wh = fetch(qkv_high_hbm, wh, 7)
    get_wph = fetch(proj_high_hbm, wph, 8)

    def remote(source, target, index, place):
        return pltpu.make_async_remote_copy(
            src_ref=source,
            dst_ref=target,
            send_sem=send_sem.at[index],
            recv_sem=recv_sem.at[index],
            device_id=device(place),
            device_id_type=MESH,
        )

    inner, edge = pl.ds(3 * WIDE, 21 * WIDE), pl.ds(0, 3 * WIDE)
    beyond = pl.ds(PAIRS * WIDE, 3 * WIDE)
    p1 = (
        remote(fields_hbm.at[0:3, :, inner], fields.at[12:15, :, inner], 0, before[0]),
        remote(fields_hbm.at[3:12, :, edge], fields.at[3:12, :, beyond], 1, before[1]),
        remote(fields_hbm.at[0:3, :, edge], fields.at[12:15, :, beyond], 2, before[2]),
    )
    p2 = (
        remote(s2_lat, r2_lat, 3, before[0]),
        remote(s2_lon, r2_lon, 4, before[1]),
        remote(s2_cor, r2_cor, 5, before[2]),
    )
    p3 = (
        remote(s3_near, r3_near, 9, after[0]),
        remote(s3_lat, r3_lat, 6, after[0]),
        remote(s3_lon, r3_lon, 7, after[1]),
        remote(s3_cor, r3_cor, 8, after[2]),
    )

    sub8 = sublanes(8)
    pl.semaphore_wait(barrier, 3)
    for copy in p1:
        copy.start()

    def put_unit(r, jjr, p, part, slab):
        u = 8 * r + 2 * (jjr // 6) + p
        xu[u, 8 * (jjr % 6):8 * (jjr % 6) + 8, 128 * part:128 * part + 128] = slab

    def widen(jj, first, count):
        for part in range(3):
            at = jj * WIDE + 128 * part
            flat[3 * jj + part, 2 * first:2 * (first + count), :] = (
                fields[first:first + count, :, at:at + 128].astype(F32).reshape(2 * count, 128)
            )

    def put_first(jj):
        for part in range(3):
            for p in range(2):
                upper = flat[3 * jj + part, pl.ds(p, 8, stride=2), :]
                lower = flat[3 * jj + part, pl.ds(16 + p, 8, stride=2), :]
                put_unit(0, jj - 3, p, part, jnp.where(sub8 >= 3, upper, lower))

    def put_second(jj):
        for part in range(3):
            for p in range(2):
                put_unit(1, jj - 3, p, part, flat[3 * jj + part, pl.ds(16 + p, 8, stride=2), :])

    def stage_own():
        flat[:, 24:32, :] = jnp.zeros_like(flat[:, 24:32, :])
        for jj in range(3, PAIRS):
            widen(jj, 0, 12)
            put_first(jj)

    get_fields.wait()
    stage_own()

    def stage_pad():
        w_even[...] = jnp.zeros_like(w_even)
        w_odd[...] = jnp.zeros_like(w_odd)
        wp_even[...] = jnp.zeros_like(wp_even)
        wp_odd[...] = jnp.zeros_like(wp_odd)
        strip_e[...] = jnp.zeros_like(strip_e)
        strip_o[...] = jnp.zeros_like(strip_o)
        tabs[...] = jnp.zeros_like(tabs)
        for part in range(3):
            piece = wl[:, 192 * part:192 * part + 192]
            w_even[0:192, 256 * part:256 * part + 192] = piece
            w_odd[64:256, 256 * part:256 * part + 192] = piece
        wp_even[0:192, 0:192] = wp[...]
        wp_odd[0:192, 192:384] = wp[...]

    get_wl.wait()
    get_wp.wait()
    stage_pad()

    def one_hot(kind):
        wide = lax.broadcasted_iota(jnp.int32, (8, 256), 1)
        within = lax.rem(wide, 128)
        step, place = within // 8, lax.rem(within, 8)
        offset = jnp.where(wide < 128, 2 * step - 10, 2 * step - 11)
        entry = jnp.full((8, 256), -1, jnp.int32)
        for ia in range(6):
            entry = jnp.where(place == PLACES[kind][ia], 23 * ia + 11 + offset, entry)
        entry = jnp.where(step < jnp.where(wide < 128, 11, 12), entry, -1)
        row = lax.broadcasted_iota(jnp.int32, (256, 256), 0)
        return jnp.where(row == entry[0:1, :], 1.0, 0.0).astype(BF16)

    def build_strips(kinds):
        for p in range(2):
            start = 0 if p == 1 else NPOS - HALF
            for ia in range(6):
                for ib in range(6):
                    source = slice(start + 138 * ia + 23 * ib, start + 138 * ia + 23 * ib + 23)
                    target = slice(23 * ia, 23 * ia + 23)
                    for kind in kinds:
                        if kind < 2:
                            at = 96 * kind + 16 * ib + 8 * p
                            tabs[at:at + 6, target] = bl[0, :, kind, source]
                        else:
                            at = 192 + 32 * ib + 16 * p
                            tabs[at:at + 12, target] = bh[0, :, 0, source]
        for kind in kinds:
            first, count = TABLE_ROWS[kind]
            wide = tabs[6 * first:6 * (first + count), :]
            high = wide.astype(BF16)
            rest = wide - high.astype(F32)
            middle = rest.astype(BF16)
            low = (rest - middle.astype(F32)).astype(BF16)
            hot = one_hot(kind)
            spread = jnp.dot(high, hot, preferred_element_type=F32)
            spread = spread + jnp.dot(middle, hot, preferred_element_type=F32)
            spread = spread + jnp.dot(low, hot, preferred_element_type=F32)
            for ib in range(6):
                piece = spread[count * ib:count * (ib + 1)]
                where = pl.ds(first * 8 + PLACES[kind][ib], count, stride=8)
                strip_e[where, :] = piece[:, 0:128]
                strip_o[where, :] = piece[:, 128:256]


    lane = lax.broadcasted_iota(jnp.int32, (8, 128), 1)
    row8 = lax.broadcasted_iota(jnp.int32, (8, 128), 0)
    lane8 = lax.rem(lane, 8)
    last = lat == lat_total - 1

    def any_of(value, options):
        hit = value == options[0]
        for option in options[1:]:
            hit = hit | (value == option)
        return hit

    def mask_of(kind):
        places = PLACES[kind]
        mask = jnp.where(any_of(row8, places), 0.0, NEG)
        if kind > 0:
            differ = jnp.where(any_of(row8, places[3:]), 1, 0) != jnp.where(any_of(lane8, places[3:]), 1, 0)
            mask = jnp.where(differ & last, NEG, mask)
        return mask

    def turn(value, shift):
        return pltpu.roll(value, shift, 1) if shift else value

    def build_tables(kind, target):
        mask = mask_of(kind)
        first, count = TABLE_ROWS[kind]
        stride = count // 2
        heads = 12 if kind == 2 else 6

        def one(p, carry):
            for head in range(heads):
                at = pl.multiple_of((first + p * stride + head) * 8, 8)
                even = strip_e[pl.ds(at, 8), :]
                odd = strip_o[pl.ds(at, 8), :]
                for parity in range(2):
                    left, right = (even, odd) if parity == 0 else (odd, even)
                    for k in range(6):
                        tile = jnp.where(
                            lane < 48,
                            turn(left, (128 - (5 - k) * 8) % 128),
                            turn(right, 8 * k + 8 * parity),
                        )
                        row = 48 * parity + 8 * k
                        target[p * heads + head, row:row + 8, :] = tile + mask
            return carry

        lax.fori_loop(0, 2, one, 0)

    def stage_tables_low():
        build_strips((0, 1))
        build_tables(0, t_low.at[0])

    def stage_tables_second():
        build_tables(1, t_low.at[1])

    def stage_tables_high():
        build_strips((2,))
        build_tables(2, t_high)

    get_bl.wait()
    stage_tables_low()

    wide_lane = lax.broadcasted_iota(jnp.int32, (1, 128), 1)
    low_half = wide_lane < 64
    head_masks = [
        jnp.where(wide_lane // 32 == h, 1.0, 0.0).astype(BF16) for h in range(4)
    ]
    ones = jnp.ones((16, 96), BF16)

    def norm_unit(u):
        x = xu[u]
        x0, x1, x2 = x[:, 0:128], x[:, 128:256], x[:, 256:384]
        me = jnp.sum(x0 + jnp.where(low_half, x1, 0.0), axis=1, keepdims=True) / 192
        mo = jnp.sum(x2 + jnp.where(low_half, 0.0, x1), axis=1, keepdims=True) / 192
        d0, d1, d2 = x0 - me, x1 - jnp.where(low_half, me, mo), x2 - mo
        q1 = d1 * d1
        ve = jnp.sum(d0 * d0 + jnp.where(low_half, q1, 0.0), axis=1, keepdims=True) / 192
        vo = jnp.sum(d2 * d2 + jnp.where(low_half, 0.0, q1), axis=1, keepdims=True) / 192
        re, ro = lax.rsqrt(ve + EPSILON), lax.rsqrt(vo + EPSILON)
        xn[u, :, 0:128] = (d0 * re).astype(BF16)
        xn[u, :, 128:256] = (d1 * jnp.where(low_half, re, ro)).astype(BF16)
        xn[u, :, 256:384] = (d2 * ro).astype(BF16)

    def qkv_units(first, count):
        for u in range(first, first + count):
            norm_unit(u)
        for parity, weight in ((0, w_even), (1, w_odd)):
            rows = xn[first:first + count, :, 128 * parity:128 * parity + 256].reshape(count * 48, 256)
            for part in range(3):
                piece = jnp.dot(rows, weight[:, 256 * part:256 * part + 256], preferred_element_type=F32)
                qkv[first:first + count, 48 * parity:48 * parity + 48, 256 * part:256 * part + 256] = (
                    piece.astype(BF16).reshape(count, 48, 256)
                )

    def group_attend(q, k, v, heads, table):
        stack = jnp.concatenate([k * head_masks[h] for h in range(heads)], axis=0)
        scores = lax.dot_general(stack, q, (((1,), (1,)), ((), ())), preferred_element_type=F32)
        scores = scores.reshape(heads, 96, 96) * SCALE + table
        weights = jnp.exp(scores - jnp.max(scores, axis=1, keepdims=True)).astype(BF16)
        turned = v.T
        mixed = []
        for h in range(heads):
            values = jnp.concatenate([turned[32 * h:32 * h + 32], ones], axis=0)
            sums = jnp.dot(values, weights[h], preferred_element_type=F32)
            mixed.append(sums[0:32] / sums[32:33])
        if heads < 4:
            mixed.append(jnp.zeros((128 - 32 * heads, 96), F32))
        return jnp.concatenate(mixed, axis=0).T.astype(BF16)

    def attend_low(r, first, count):
        def one(pair, carry):
            for p in range(2):
                u = 2 * pair + p
                for group, heads in ((0, 4), (1, 2)):
                    at = 128 * group
                    ob[u, :, at:at + 128] = group_attend(
                        qkv[u, :, at:at + 128],
                        qkv[u, :, 256 + at:384 + at],
                        qkv[u, :, 512 + at:640 + at],
                        heads,
                        t_low[r, p * 6 + 4 * group:p * 6 + 4 * group + heads, :, 0:96],
                    )
            return carry

        if count == 2:
            one(first // 2, 0)
        else:
            lax.fori_loop(first // 2, (first + count) // 2, one, 0)


    def project_low(first, count):
        even = ob[first:first + count, 0:48, :].reshape(count * 48, 256)
        odd = ob[first:first + count, 48:96, :].reshape(count * 48, 256)
        att = jnp.dot(even, wp_even[...], preferred_element_type=F32) + jnp.dot(
            odd, wp_odd[...], preferred_element_type=F32
        )
        att = att.astype(BF16).astype(F32).reshape(count, 48, WIDE)
        lo[first:first + count] = (xu[first:first + count] + att).astype(BF16).astype(F32)

    def low_slab(r, jjr, p):
        return lo[8 * r + 2 * (jjr // 6) + p, 8 * (jjr % 6):8 * (jjr % 6) + 8, :]

    def stage_qkv_a():
        qkv_units(0, 6)

    def stage_attend_a():
        attend_low(0, 0, 6)

    def stage_first_end():
        for k in range(3):
            widen(PAIRS + k, 0, 12)
            put_first(PAIRS + k)
        qkv_units(6, 2)
        attend_low(0, 6, 2)
        project_low(0, 8)
        for jjr in range(PAIRS):
            slab = jnp.where(
                (sub8 >= 2) & (sub8 < 6), low_slab(0, jjr, 1), roll8(low_slab(0, jjr, 0), 4)
            ).astype(BF16)
            if jjr < 3:
                s2_cor[8 * jjr:8 * jjr + 8, :] = slab
            else:
                s2_lat[8 * (jjr - 3):8 * (jjr - 3) + 8, :] = slab

    def stage_second_edge():
        for jj in range(3, PAIRS + 3):
            widen(jj, 12, 3)
            put_second(jj)
        qkv_units(8, 2)
        attend_low(1, 8, 2)
        project_low(8, 2)
        for k in range(3):
            for p in range(2):
                at = (2 * k + p) * 8
                s2_lon[at:at + 8, :] = jnp.where(sub8 == 0, low_slab(0, k, p), low_slab(1, k, p)).astype(BF16)
            s2_lon[48 + 8 * k:56 + 8 * k, :] = jnp.where(
                sub8 >= 4, low_slab(0, k, 0), roll8(low_slab(0, k, 1), 4)
            ).astype(BF16)

    def stage_qkv_b():
        qkv_units(10, 6)

    def stage_attend_b():
        attend_low(1, 10, 6)

    def stage_project_b():
        project_low(10, 6)

    stage_qkv_a()
    stage_attend_a()

    p1[1].wait_recv()
    stage_first_end()
    p2[0].start()
    p2[2].start()
    stage_tables_second()
    p1[0].wait_recv()
    p1[2].wait_recv()
    stage_second_edge()
    p2[1].start()
    stage_qkv_b()
    stage_attend_b()
    stage_project_b()
    get_bh.wait()
    stage_tables_high()

    def gather(w):
        for col in range(12 * w, 12 * w + 12):
            jjr = col + 3
            if col < 21:
                halo = r2_lat[8 * col:8 * col + 8, :].astype(F32)
            else:
                k = col - 21
                halo = r2_cor[8 * k:8 * k + 8, :].astype(F32)
                upper = r2_lon[48 + 8 * k:56 + 8 * k, :].astype(F32)
            for p in range(2):
                far = roll8(halo, 4 * p)
                if col < 21:
                    first, second = low_slab(0, jjr, p), low_slab(1, jjr, p)
                    inner = jnp.where(sub8 == 0, first, second)
                else:
                    first = roll8(upper, 4 * p)
                    at = (2 * k + p) * 8
                    inner = r2_lon[at:at + 8, :].astype(F32)
                at = ((2 * w + p) * 12 + col % 12) * 8
                mi[0, at:at + 8, :] = jnp.where(sub8 == 7, far, inner)
                mi[1, at:at + 8, :] = jnp.where(sub8 >= 6, first, far)

    def pair_sum(value):
        rows = value.shape[0]
        value = jnp.broadcast_to(value, (rows, 128))
        even = lax.rem(sublanes(rows), 2) == 0
        return value + jnp.where(even, roll8(value, 7), roll8(value, 1))

    def triple(value):
        return jnp.concatenate([value, value, value], axis=1)

    def norm_merge(index):
        rows = slice(index * 48, index * 48 + 48)
        for kind in range(2):
            x = mi[kind, rows, :]
            centre = pair_sum(jnp.sum(x, axis=1, keepdims=True)) / 768
            d = x - triple(centre)
            spread = pair_sum(jnp.sum(d * d, axis=1, keepdims=True)) / 768
            mn[kind, rows, :] = (d * triple(lax.rsqrt(spread + EPSILON))).astype(BF16)

    even_row = lax.rem(sublanes(192), 2) == 0

    def merge(w):
        for index in range(4 * w, 4 * w + 4):
            norm_merge(index)
        rows = slice(192 * w, 192 * w + 192)
        sums = []
        for kind in range(2):
            y0 = jnp.dot(mn[kind, rows, :], wm[0:384, :], preferred_element_type=F32)
            y1 = jnp.dot(mn[kind, rows, :], wm[384:768, :], preferred_element_type=F32)
            sums.append(y0 + roll8(y1, 7) if kind == 0 else roll8(y0, 1) + y1)
        merged = jnp.where(even_row, sums[0], sums[1]).astype(BF16).astype(F32)
        for p in range(2):
            for col in range(12):
                at, source = 48 * (col % 2) + 8 * (col // 2), (12 * p + col) * 8
                mg[2 * w + p, at:at + 8, :] = merged[source:source + 8, :]

    def norm_high(u):
        x = mg[u]
        d = x - jnp.sum(x, axis=1, keepdims=True) / 384
        spread = jnp.sum(d * d, axis=1, keepdims=True) / 384
        xh[u] = (d * lax.rsqrt(spread + EPSILON)).astype(BF16)

    def qkv_high_units(w):
        units = slice(2 * w, 2 * w + 2)
        for u in (2 * w, 2 * w + 1):
            norm_high(u)
        rows = xh[units].reshape(192, 384)
        for part in range(3):
            piece = jnp.dot(rows, wh[:, 384 * part:384 * part + 384], preferred_element_type=F32)
            qh[units, :, 384 * part:384 * part + 384] = piece.astype(BF16).reshape(2, 96, 384)

    def attend_high(w):
        for u in (2 * w, 2 * w + 1):
            p = u % 2
            for group in range(3):
                at = 128 * group
                oh2[u, :, at:at + 128] = group_attend(
                    qh[u, :, at:at + 128],
                    qh[u, :, 384 + at:512 + at],
                    qh[u, :, 768 + at:896 + at],
                    4,
                    t_high[p * 12 + 4 * group:p * 12 + 4 * group + 4, :, 0:96],
                )
        units = slice(2 * w, 2 * w + 2)
        att = jnp.dot(oh2[units].reshape(192, 384), wph[...], preferred_element_type=F32)
        att = att.astype(BF16).astype(F32).reshape(2, 96, 384)
        res[units] = (mg[units] + att).astype(BF16).astype(F32)

    def result(col, p):
        w, within = col // 12, col % 12
        at = 48 * (within % 2) + 8 * (within // 2)
        return res[2 * w + p, at:at + 8, :]

    def own_rows(x, shift):
        return jnp.where(sub8 == (5 + shift) % 8, roll8(x, 3 + shift), roll8(x, 4 + shift))

    def far_rows(x, shift):
        return jnp.where(
            sub8 == shift,
            roll8(x, 4 + shift),
            jnp.where(sub8 == 1 + shift, roll8(x, 3 + shift), roll8(x, 1 + shift)),
        )

    def pack_out(w):
        for col in range(12 * w, 12 * w + 12):
            slab = jnp.where(sub8 < 4, far_rows(result(col, 0), 0), far_rows(result(col, 1), 4)).astype(BF16)
            if col < 12:
                s3_near[8 * col:8 * col + 8, :] = slab
            elif col < 18:
                k = col - 12
                s3_lat[8 * k:8 * k + 8, :] = slab
            else:
                k = col - 18
                s3_cor[8 * k:8 * k + 8, :] = slab
                s3_lon[8 * k:8 * k + 8, :] = jnp.where(
                    (sub8 >= 3) & (sub8 < 6), own_rows(result(col, 0), 0), own_rows(result(col, 1), 4)
                ).astype(BF16)

    def put_out(target):
        for p in range(2):
            if target < 6:
                first = r3_cor[8 * target:8 * target + 8, :].astype(F32)
                second = roll8(r3_lon[8 * target:8 * target + 8, :].astype(F32), 4 * p)
            else:
                k = target - 6
                received, k = (r3_near, k) if k < 12 else (r3_lat, k - 12)
                first = received[8 * k:8 * k + 8, :].astype(F32)
                second = own_rows(result(target - 6, p), 0)
            whole = jnp.where(sub8 < 3, roll8(first, 4 * p), second)
            for part in range(3):
                flat[3 * target + part, pl.ds(p, 8, stride=2), :] = whole[:, 128 * part:128 * part + 128]
        for part in range(3):
            at = target * WIDE + 128 * part
            out_ref[:, :, at:at + 128] = flat[3 * target + part, 0:12, :].reshape(6, 2, 128).astype(BF16)

    def level_high(w):
        gather(w)
        merge(w)
        qkv_high_units(w)
        attend_high(w)
        pack_out(w)

    def stage_high_first():
        level_high(0)

    def stage_high_second():
        level_high(1)

    def stage_out_first():
        for target in range(6, 18):
            put_out(target)

    def stage_out_second():
        for target in (*range(6), *range(18, PAIRS)):
            put_out(target)

    get_wm.wait()
    get_wh.wait()
    get_wph.wait()
    p2[0].wait_recv()
    stage_high_first()
    p3[0].start()
    p2[1].wait_recv()
    p2[2].wait_recv()
    stage_high_second()
    p3[1].start()
    p3[2].start()
    p3[3].start()
    p3[0].wait_recv()
    stage_out_first()
    p3[1].wait_recv()
    p3[2].wait_recv()
    p3[3].wait_recv()
    stage_out_second()
    for copy in p1 + p2 + p3:
        copy.wait_send()


def solution(mesh):
    lat_total, lon_total = mesh.shape["lat"], mesh.shape["lon"]

    def step(fields, qkv_low, proj_low, merge_proj, qkv_high, proj_high, bias_low, bias_high):
        def vmem(*shape, dtype=BF16):
            return pltpu.VMEM(shape, dtype)

        operands = (
            fields.transpose(1, 0, 2),
            qkv_low,
            proj_low,
            merge_proj,
            qkv_high,
            proj_high,
            bias_low.transpose(0, 2, 1, 3),
            bias_high.transpose(0, 2, 1, 3),
        )
        operands = [pltpu.with_memory_space_constraint(operand, pltpu.HBM) for operand in operands]
        halo = [vmem(176, WIDE), vmem(80, WIDE), vmem(32, WIDE)]
        last_halo = [vmem(96, WIDE), vmem(48, WIDE), vmem(48, WIDE), vmem(48, WIDE)]
        return pl.pallas_call(
            functools.partial(kernel, lat_total=lat_total, lon_total=lon_total),
            out_shape=jax.ShapeDtypeStruct((6, 2, PAIRS * WIDE), BF16),
            in_specs=[pl.BlockSpec(memory_space=pl.ANY)] * 8,
            out_specs=pl.BlockSpec(memory_space=pltpu.VMEM),
            scratch_shapes=[
                vmem(15, 2, (PAIRS + 3) * WIDE),
                vmem((PAIRS + 3) * 3, 32, 128, dtype=F32),
                vmem(192, 576),
                vmem(192, 192),
                vmem(768, 384),
                vmem(384, 1152),
                vmem(384, 384),
                vmem(1, 6, 2, NPOS, dtype=F32),
                vmem(1, 12, 1, NPOS, dtype=F32),
                vmem(256, 768),
                vmem(256, 768),
                vmem(256, 384),
                vmem(256, 384),
                vmem(384, 256, dtype=F32),
                vmem(512, 128, dtype=F32),
                vmem(512, 128, dtype=F32),
                vmem(2, 12, 96, 128, dtype=F32),
                vmem(24, 96, 128, dtype=F32),
                vmem(16, 48, WIDE, dtype=F32),
                vmem(16, 48, WIDE),
                vmem(16, 96, 768),
                vmem(16, 96, 256),
                vmem(16, 48, WIDE, dtype=F32),
                *halo, *halo, *last_halo, *last_halo,
                vmem(2, 384, WIDE, dtype=F32),
                vmem(2, 384, WIDE),
                vmem(4, 96, WIDE, dtype=F32),
                vmem(4, 96, WIDE),
                vmem(4, 96, 3 * WIDE),
                vmem(4, 96, WIDE),
                vmem(4, 96, WIDE, dtype=F32),
                pltpu.SemaphoreType.DMA((10,)),
                pltpu.SemaphoreType.DMA((10,)),
                pltpu.SemaphoreType.DMA((10,)),
            ],
            compiler_params=pltpu.CompilerParams(
                collective_id=0, has_side_effects=True, vmem_limit_bytes=28 * 1024 * 1024
            ),
            name="block",
        )(*operands).transpose(1, 0, 2)

    return jax.shard_map(
        step,
        mesh=mesh,
        in_specs=(
            P(None, "lat", "lon"),
            P(),
            P(),
            P(),
            P(),
            P(),
            P(None, "lat", None, None),
            P(None, "lat", None, None),
        ),
        out_specs=P(None, "lat", "lon"),
        check_vma=False,
    )
```

```python
import functools

import jax
import jax.numpy as jnp
from jax import lax
from jax.experimental import pallas as pl
from jax.experimental.pallas import tpu as pltpu
from jax.sharding import PartitionSpec as P

MESH = pl.DeviceIdType.MESH
F32 = jnp.float32
BF16 = jnp.bfloat16

EPSILON = 1e-05
NEG = -1e30
SCALE = 32 ** (-0.5)
NPOS = 3312
HALF = 828
PAIRS = 24
WIDE = 384
PLACES = ((3, 4, 5, 6, 7, 0), (1, 2, 3, 4, 5, 6), (7, 0, 2, 4, 6, 1))
TABLE_ROWS = ((0, 16), (16, 16), (32, 32))


def sublanes(rows):
    return lax.rem(lax.broadcasted_iota(jnp.int32, (rows, 1), 0), 8)


def roll8(value, shift):
    shift %= 8
    if shift == 0:
        return value
    rows, cols = value.shape
    if rows == 8:
        return pltpu.roll(value, shift, 0)
    return pltpu.roll(value.reshape(rows // 8, 8, cols), shift, 1).reshape(rows, cols)


def kernel(
    fields_hbm, qkv_low_hbm, proj_low_hbm, merge_hbm, qkv_high_hbm, proj_high_hbm, bias_low_hbm,
    bias_high_hbm,
    out_ref,
    fields, flat, wl, wp, wm, wh, wph, bl, bh,
    w_even, w_odd, wp_even, wp_odd,
    raw, tabs, strip_e, strip_o, t_low, t_high,
    xu, xn, qkv, ob, lo,
    s2_lat, s2_lon, s2_cor, r2_lat, r2_lon, r2_cor,
    s3_near, s3_lat, s3_lon, s3_cor, r3_near, r3_lat, r3_lon, r3_cor,
    mi, mn, mg, xh, qh, oh2, res,
    local_sem, send_sem, recv_sem,
    *, lat_total, lon_total,
):
    lat = lax.axis_index("lat")
    lon = lax.axis_index("lon")
    lat_prev = lax.rem(lat + lat_total - 1, lat_total)
    lat_next = lax.rem(lat + 1, lat_total)
    lon_prev = lax.rem(lon + lon_total - 1, lon_total)
    lon_next = lax.rem(lon + 1, lon_total)
    before = ((lat_prev, lon), (lat, lon_prev), (lat_prev, lon_prev))
    after = ((lat_next, lon), (lat, lon_next), (lat_next, lon_next))

    def device(place):
        return {"lat": place[0], "lon": place[1]}

    barrier = pltpu.get_barrier_semaphore()
    for place in after:
        pl.semaphore_signal(barrier, inc=1, device_id=device(place), device_id_type=MESH)

    def fetch(source, target, index):
        copy = pltpu.make_async_copy(source, target, local_sem.at[index])
        copy.start()
        return copy

    get_fields = fetch(fields_hbm, fields.at[0:12, :, 0:PAIRS * WIDE], 0)
    get_bl = fetch(bias_low_hbm, bl, 1)
    get_bh = fetch(bias_high_hbm, bh, 2)
    get_wl = fetch(qkv_low_hbm, wl, 4)
    get_wp = fetch(proj_low_hbm, wp, 5)
    get_wm = fetch(merge_hbm, wm, 6)
    get_wh = fetch(qkv_high_hbm, wh, 7)
    get_wph = fetch(proj_high_hbm, wph, 8)

    def remote(source, target, index, place):
        return pltpu.make_async_remote_copy(
            src_ref=source,
            dst_ref=target,
            send_sem=send_sem.at[index],
            recv_sem=recv_sem.at[index],
            device_id=device(place),
            device_id_type=MESH,
        )

    inner, edge = pl.ds(3 * WIDE, 21 * WIDE), pl.ds(0, 3 * WIDE)
    beyond = pl.ds(PAIRS * WIDE, 3 * WIDE)
    p1 = (
        remote(fields_hbm.at[0:3, :, inner], fields.at[12:15, :, inner], 0, before[0]),
        remote(fields_hbm.at[3:12, :, edge], fields.at[3:12, :, beyond], 1, before[1]),
        remote(fields_hbm.at[0:3, :, edge], fields.at[12:15, :, beyond], 2, before[2]),
    )
    p2 = (
        remote(s2_lat, r2_lat, 3, before[0]),
        remote(s2_lon, r2_lon, 4, before[1]),
        remote(s2_cor, r2_cor, 5, before[2]),
    )
    p3 = (
        remote(s3_near, r3_near, 9, after[0]),
        remote(s3_lat, r3_lat, 6, after[0]),
        remote(s3_lon, r3_lon, 7, after[1]),
        remote(s3_cor, r3_cor, 8, after[2]),
    )

    sub8 = sublanes(8)
    pl.semaphore_wait(barrier, 3)
    for copy in p1:
        copy.start()

    def put_unit(r, jjr, p, part, slab):
        u = 8 * r + 2 * (jjr // 6) + p
        xu[u, 8 * (jjr % 6):8 * (jjr % 6) + 8, 128 * part:128 * part + 128] = slab

    def widen(jj, first, count):
        for part in range(3):
            at = jj * WIDE + 128 * part
            flat[3 * jj + part, 2 * first:2 * (first + count), :] = (
                fields[first:first + count, :, at:at + 128].astype(F32).reshape(2 * count, 128)
            )

    def put_first(jj):
        for part in range(3):
            for p in range(2):
                upper = flat[3 * jj + part, pl.ds(p, 8, stride=2), :]
                lower = flat[3 * jj + part, pl.ds(16 + p, 8, stride=2), :]
                put_unit(0, jj - 3, p, part, jnp.where(sub8 >= 3, upper, lower))

    def put_second(jj):
        for part in range(3):
            for p in range(2):
                put_unit(1, jj - 3, p, part, flat[3 * jj + part, pl.ds(16 + p, 8, stride=2), :])

    def stage_own():
        flat[:, 24:32, :] = jnp.zeros_like(flat[:, 24:32, :])
        for jj in range(3, PAIRS):
            widen(jj, 0, 12)
            put_first(jj)

    get_fields.wait()
    stage_own()

    def stage_pad():
        w_even[...] = jnp.zeros_like(w_even)
        w_odd[...] = jnp.zeros_like(w_odd)
        wp_even[...] = jnp.zeros_like(wp_even)
        wp_odd[...] = jnp.zeros_like(wp_odd)
        strip_e[...] = jnp.zeros_like(strip_e)
        strip_o[...] = jnp.zeros_like(strip_o)
        tabs[...] = jnp.zeros_like(tabs)
        raw[...] = jnp.zeros_like(raw)
        for part in range(3):
            piece = wl[:, 192 * part:192 * part + 192]
            w_even[0:192, 256 * part:256 * part + 192] = piece
            w_odd[64:256, 256 * part:256 * part + 192] = piece
        wp_even[0:192, 0:192] = wp[...]
        wp_odd[0:192, 192:384] = wp[...]

    get_wl.wait()
    get_wp.wait()
    stage_pad()

    def one_hot(kind):
        wide = lax.broadcasted_iota(jnp.int32, (8, 256), 1)
        within = lax.rem(wide, 128)
        step, place = within // 8, lax.rem(within, 8)
        offset = jnp.where(wide < 128, 2 * step - 10, 2 * step - 11)
        entry = jnp.full((8, 256), -1, jnp.int32)
        for ia in range(6):
            entry = jnp.where(place == PLACES[kind][ia], 23 * ia + 11 + offset, entry)
        entry = jnp.where(step < jnp.where(wide < 128, 11, 12), entry, -1)
        row = lax.broadcasted_iota(jnp.int32, (256, 256), 0)
        return jnp.where(row == entry[0:1, :], 1.0, 0.0).astype(BF16)

    def build_strips(kinds):
        for kind in kinds:
            first, count = TABLE_ROWS[kind]
            for p in range(2):
                start = 0 if p == 1 else NPOS - HALF
                at = first + p * (count // 2)
                if kind < 2:
                    raw[at:at + 6, 0:HALF] = bl[0, :, kind, start:start + HALF]
                else:
                    raw[at:at + 12, 0:HALF] = bh[0, :, 0, start:start + HALF]
            for ia in range(6):
                for ib in range(6):
                    source, at = 138 * ia + 23 * ib, 6 * first + count * ib
                    tabs[at:at + count, 23 * ia:23 * ia + 23] = raw[first:first + count, source:source + 23]
        for kind in kinds:
            first, count = TABLE_ROWS[kind]
            wide = tabs[6 * first:6 * (first + count), :]
            high = wide.astype(BF16)
            rest = wide - high.astype(F32)
            middle = rest.astype(BF16)
            low = (rest - middle.astype(F32)).astype(BF16)
            hot = one_hot(kind)
            spread = jnp.dot(high, hot, preferred_element_type=F32)
            spread = spread + jnp.dot(middle, hot, preferred_element_type=F32)
            spread = spread + jnp.dot(low, hot, preferred_element_type=F32)
            for ib in range(6):
                piece = spread[count * ib:count * (ib + 1)]
                where = pl.ds(first * 8 + PLACES[kind][ib], count, stride=8)
                strip_e[where, :] = piece[:, 0:128]
                strip_o[where, :] = piece[:, 128:256]


    lane = lax.broadcasted_iota(jnp.int32, (8, 128), 1)
    row8 = lax.broadcasted_iota(jnp.int32, (8, 128), 0)
    lane8 = lax.rem(lane, 8)
    last = lat == lat_total - 1

    def any_of(value, options):
        hit = value == options[0]
        for option in options[1:]:
            hit = hit | (value == option)
        return hit

    def mask_of(kind):
        places = PLACES[kind]
        mask = jnp.where(any_of(row8, places), 0.0, NEG)
        if kind > 0:
            differ = jnp.where(any_of(row8, places[3:]), 1, 0) != jnp.where(any_of(lane8, places[3:]), 1, 0)
            mask = jnp.where(differ & last, NEG, mask)
        return mask

    def turn(value, shift):
        return pltpu.roll(value, shift, 1) if shift else value

    def build_tables(kind, target):
        mask = mask_of(kind)
        first, count = TABLE_ROWS[kind]
        stride = count // 2
        heads = 12 if kind == 2 else 6

        def one(p, carry):
            for head in range(heads):
                at = pl.multiple_of((first + p * stride + head) * 8, 8)
                even = strip_e[pl.ds(at, 8), :]
                odd = strip_o[pl.ds(at, 8), :]
                for parity in range(2):
                    left, right = (even, odd) if parity == 0 else (odd, even)
                    for k in range(6):
                        tile = jnp.where(
                            lane < 48,
                            turn(left, (128 - (5 - k) * 8) % 128),
                            turn(right, 8 * k + 8 * parity),
                        )
                        row = 48 * parity + 8 * k
                        target[p * heads + head, row:row + 8, :] = tile + mask
            return carry

        lax.fori_loop(0, 2, one, 0)

    def stage_tables_low():
        build_strips((0, 1))
        build_tables(0, t_low.at[0])

    def stage_tables_second():
        build_tables(1, t_low.at[1])

    def stage_tables_high():
        build_strips((2,))
        build_tables(2, t_high)

    get_bl.wait()
    stage_tables_low()

    wide_lane = lax.broadcasted_iota(jnp.int32, (1, 128), 1)
    low_half = wide_lane < 64
    head_masks = [
        jnp.where(wide_lane // 32 == h, 1.0, 0.0).astype(BF16) for h in range(4)
    ]
    ones = jnp.ones((16, 96), BF16)

    def norm_unit(u):
        x = xu[u]
        x0, x1, x2 = x[:, 0:128], x[:, 128:256], x[:, 256:384]
        me = jnp.sum(x0 + jnp.where(low_half, x1, 0.0), axis=1, keepdims=True) / 192
        mo = jnp.sum(x2 + jnp.where(low_half, 0.0, x1), axis=1, keepdims=True) / 192
        d0, d1, d2 = x0 - me, x1 - jnp.where(low_half, me, mo), x2 - mo
        q1 = d1 * d1
        ve = jnp.sum(d0 * d0 + jnp.where(low_half, q1, 0.0), axis=1, keepdims=True) / 192
        vo = jnp.sum(d2 * d2 + jnp.where(low_half, 0.0, q1), axis=1, keepdims=True) / 192
        re, ro = lax.rsqrt(ve + EPSILON), lax.rsqrt(vo + EPSILON)
        xn[u, :, 0:128] = (d0 * re).astype(BF16)
        xn[u, :, 128:256] = (d1 * jnp.where(low_half, re, ro)).astype(BF16)
        xn[u, :, 256:384] = (d2 * ro).astype(BF16)

    def qkv_units(first, count):
        for u in range(first, first + count):
            norm_unit(u)
        for parity, weight in ((0, w_even), (1, w_odd)):
            rows = xn[first:first + count, :, 128 * parity:128 * parity + 256].reshape(count * 48, 256)
            for part in range(3):
                piece = jnp.dot(rows, weight[:, 256 * part:256 * part + 256], preferred_element_type=F32)
                qkv[first:first + count, 48 * parity:48 * parity + 48, 256 * part:256 * part + 256] = (
                    piece.astype(BF16).reshape(count, 48, 256)
                )

    def group_attend(q, k, v, heads, table):
        stack = jnp.concatenate([k * head_masks[h] for h in range(heads)], axis=0)
        scores = lax.dot_general(stack, q, (((1,), (1,)), ((), ())), preferred_element_type=F32)
        scores = scores.reshape(heads, 96, 96) * SCALE + table
        weights = jnp.exp(scores - jnp.max(scores, axis=1, keepdims=True)).astype(BF16)
        turned = v.T
        mixed = []
        for h in range(heads):
            values = jnp.concatenate([turned[32 * h:32 * h + 32], ones], axis=0)
            sums = jnp.dot(values, weights[h], preferred_element_type=F32)
            mixed.append(sums[0:32] / sums[32:33])
        if heads < 4:
            mixed.append(jnp.zeros((128 - 32 * heads, 96), F32))
        return jnp.concatenate(mixed, axis=0).T.astype(BF16)

    def attend_low(r, first, count):
        def one(pair, carry):
            for p in range(2):
                u = 2 * pair + p
                for group, heads in ((0, 4), (1, 2)):
                    at = 128 * group
                    ob[u, :, at:at + 128] = group_attend(
                        qkv[u, :, at:at + 128],
                        qkv[u, :, 256 + at:384 + at],
                        qkv[u, :, 512 + at:640 + at],
                        heads,
                        t_low[r, p * 6 + 4 * group:p * 6 + 4 * group + heads, :, 0:96],
                    )
            return carry

        if count == 2:
            one(first // 2, 0)
        else:
            lax.fori_loop(first // 2, (first + count) // 2, one, 0)


    def project_low(first, count):
        even = ob[first:first + count, 0:48, :].reshape(count * 48, 256)
        odd = ob[first:first + count, 48:96, :].reshape(count * 48, 256)
        att = jnp.dot(even, wp_even[...], preferred_element_type=F32) + jnp.dot(
            odd, wp_odd[...], preferred_element_type=F32
        )
        att = att.astype(BF16).astype(F32).reshape(count, 48, WIDE)
        lo[first:first + count] = (xu[first:first + count] + att).astype(BF16).astype(F32)

    def low_slab(r, jjr, p):
        return lo[8 * r + 2 * (jjr // 6) + p, 8 * (jjr % 6):8 * (jjr % 6) + 8, :]

    def stage_qkv_a():
        qkv_units(0, 6)

    def stage_attend_a():
        attend_low(0, 0, 6)

    def stage_first_end():
        for k in range(3):
            widen(PAIRS + k, 0, 12)
            put_first(PAIRS + k)
        qkv_units(6, 2)
        attend_low(0, 6, 2)
        project_low(0, 8)
        for jjr in range(PAIRS):
            slab = jnp.where(
                (sub8 >= 2) & (sub8 < 6), low_slab(0, jjr, 1), roll8(low_slab(0, jjr, 0), 4)
            ).astype(BF16)
            if jjr < 3:
                s2_cor[8 * jjr:8 * jjr + 8, :] = slab
            else:
                s2_lat[8 * (jjr - 3):8 * (jjr - 3) + 8, :] = slab

    def stage_second_edge():
        for jj in range(3, PAIRS + 3):
            widen(jj, 12, 3)
            put_second(jj)
        qkv_units(8, 2)
        attend_low(1, 8, 2)
        project_low(8, 2)
        for k in range(3):
            for p in range(2):
                at = (2 * k + p) * 8
                s2_lon[at:at + 8, :] = jnp.where(sub8 == 0, low_slab(0, k, p), low_slab(1, k, p)).astype(BF16)
            s2_lon[48 + 8 * k:56 + 8 * k, :] = jnp.where(
                sub8 >= 4, low_slab(0, k, 0), roll8(low_slab(0, k, 1), 4)
            ).astype(BF16)

    def stage_qkv_b():
        qkv_units(10, 6)

    def stage_attend_b():
        attend_low(1, 10, 6)

    def stage_project_b():
        project_low(10, 6)

    stage_qkv_a()
    stage_attend_a()

    p1[1].wait_recv()
    stage_first_end()
    p2[0].start()
    p2[2].start()
    stage_tables_second()
    p1[0].wait_recv()
    p1[2].wait_recv()
    stage_second_edge()
    p2[1].start()
    stage_qkv_b()
    stage_attend_b()
    stage_project_b()
    get_bh.wait()
    stage_tables_high()

    def gather(w):
        for col in range(12 * w, 12 * w + 12):
            jjr = col + 3
            if col < 21:
                halo = r2_lat[8 * col:8 * col + 8, :].astype(F32)
            else:
                k = col - 21
                halo = r2_cor[8 * k:8 * k + 8, :].astype(F32)
                upper = r2_lon[48 + 8 * k:56 + 8 * k, :].astype(F32)
            for p in range(2):
                far = roll8(halo, 4 * p)
                if col < 21:
                    first, second = low_slab(0, jjr, p), low_slab(1, jjr, p)
                    inner = jnp.where(sub8 == 0, first, second)
                else:
                    first = roll8(upper, 4 * p)
                    at = (2 * k + p) * 8
                    inner = r2_lon[at:at + 8, :].astype(F32)
                at = ((2 * w + p) * 12 + col % 12) * 8
                mi[0, at:at + 8, :] = jnp.where(sub8 == 7, far, inner)
                mi[1, at:at + 8, :] = jnp.where(sub8 >= 6, first, far)

    def pair_sum(value):
        rows = value.shape[0]
        value = jnp.broadcast_to(value, (rows, 128))
        even = lax.rem(sublanes(rows), 2) == 0
        return value + jnp.where(even, roll8(value, 7), roll8(value, 1))

    def triple(value):
        return jnp.concatenate([value, value, value], axis=1)

    def norm_merge(index):
        rows = slice(index * 48, index * 48 + 48)
        for kind in range(2):
            x = mi[kind, rows, :]
            centre = pair_sum(jnp.sum(x, axis=1, keepdims=True)) / 768
            d = x - triple(centre)
            spread = pair_sum(jnp.sum(d * d, axis=1, keepdims=True)) / 768
            mn[kind, rows, :] = (d * triple(lax.rsqrt(spread + EPSILON))).astype(BF16)

    even_row = lax.rem(sublanes(192), 2) == 0

    def merge(w):
        for index in range(4 * w, 4 * w + 4):
            norm_merge(index)
        rows = slice(192 * w, 192 * w + 192)
        sums = []
        for kind in range(2):
            y0 = jnp.dot(mn[kind, rows, :], wm[0:384, :], preferred_element_type=F32)
            y1 = jnp.dot(mn[kind, rows, :], wm[384:768, :], preferred_element_type=F32)
            sums.append(y0 + roll8(y1, 7) if kind == 0 else roll8(y0, 1) + y1)
        merged = jnp.where(even_row, sums[0], sums[1]).astype(BF16).astype(F32)
        for p in range(2):
            for col in range(12):
                at, source = 48 * (col % 2) + 8 * (col // 2), (12 * p + col) * 8
                mg[2 * w + p, at:at + 8, :] = merged[source:source + 8, :]

    def norm_high(u):
        x = mg[u]
        d = x - jnp.sum(x, axis=1, keepdims=True) / 384
        spread = jnp.sum(d * d, axis=1, keepdims=True) / 384
        xh[u] = (d * lax.rsqrt(spread + EPSILON)).astype(BF16)

    def qkv_high_units(w):
        units = slice(2 * w, 2 * w + 2)
        for u in (2 * w, 2 * w + 1):
            norm_high(u)
        rows = xh[units].reshape(192, 384)
        for part in range(3):
            piece = jnp.dot(rows, wh[:, 384 * part:384 * part + 384], preferred_element_type=F32)
            qh[units, :, 384 * part:384 * part + 384] = piece.astype(BF16).reshape(2, 96, 384)

    def attend_high(w):
        for u in (2 * w, 2 * w + 1):
            p = u % 2
            for group in range(3):
                at = 128 * group
                oh2[u, :, at:at + 128] = group_attend(
                    qh[u, :, at:at + 128],
                    qh[u, :, 384 + at:512 + at],
                    qh[u, :, 768 + at:896 + at],
                    4,
                    t_high[p * 12 + 4 * group:p * 12 + 4 * group + 4, :, 0:96],
                )
        units = slice(2 * w, 2 * w + 2)
        att = jnp.dot(oh2[units].reshape(192, 384), wph[...], preferred_element_type=F32)
        att = att.astype(BF16).astype(F32).reshape(2, 96, 384)
        res[units] = (mg[units] + att).astype(BF16).astype(F32)

    def result(col, p):
        w, within = col // 12, col % 12
        at = 48 * (within % 2) + 8 * (within // 2)
        return res[2 * w + p, at:at + 8, :]

    def own_rows(x, shift):
        return jnp.where(sub8 == (5 + shift) % 8, roll8(x, 3 + shift), roll8(x, 4 + shift))

    def far_rows(x, shift):
        return jnp.where(
            sub8 == shift,
            roll8(x, 4 + shift),
            jnp.where(sub8 == 1 + shift, roll8(x, 3 + shift), roll8(x, 1 + shift)),
        )

    def pack_out(w):
        for col in range(12 * w, 12 * w + 12):
            slab = jnp.where(sub8 < 4, far_rows(result(col, 0), 0), far_rows(result(col, 1), 4)).astype(BF16)
            if col < 12:
                s3_near[8 * col:8 * col + 8, :] = slab
            elif col < 18:
                k = col - 12
                s3_lat[8 * k:8 * k + 8, :] = slab
            else:
                k = col - 18
                s3_cor[8 * k:8 * k + 8, :] = slab
                s3_lon[8 * k:8 * k + 8, :] = jnp.where(
                    (sub8 >= 3) & (sub8 < 6), own_rows(result(col, 0), 0), own_rows(result(col, 1), 4)
                ).astype(BF16)

    def put_out(target):
        for p in range(2):
            if target < 6:
                first = r3_cor[8 * target:8 * target + 8, :].astype(F32)
                second = roll8(r3_lon[8 * target:8 * target + 8, :].astype(F32), 4 * p)
            else:
                k = target - 6
                received, k = (r3_near, k) if k < 12 else (r3_lat, k - 12)
                first = received[8 * k:8 * k + 8, :].astype(F32)
                second = own_rows(result(target - 6, p), 0)
            whole = jnp.where(sub8 < 3, roll8(first, 4 * p), second)
            for part in range(3):
                flat[3 * target + part, pl.ds(p, 8, stride=2), :] = whole[:, 128 * part:128 * part + 128]
        for part in range(3):
            at = target * WIDE + 128 * part
            out_ref[:, :, at:at + 128] = flat[3 * target + part, 0:12, :].reshape(6, 2, 128).astype(BF16)

    def level_high(w):
        gather(w)
        merge(w)
        qkv_high_units(w)
        attend_high(w)
        pack_out(w)

    def stage_high_first():
        level_high(0)

    def stage_high_second():
        level_high(1)

    def stage_out_first():
        for target in range(6, 18):
            put_out(target)

    def stage_out_second():
        for target in (*range(6), *range(18, PAIRS)):
            put_out(target)

    get_wm.wait()
    get_wh.wait()
    get_wph.wait()
    p2[0].wait_recv()
    stage_high_first()
    p3[0].start()
    p2[1].wait_recv()
    p2[2].wait_recv()
    stage_high_second()
    p3[1].start()
    p3[2].start()
    p3[3].start()
    p3[0].wait_recv()
    stage_out_first()
    p3[1].wait_recv()
    p3[2].wait_recv()
    p3[3].wait_recv()
    stage_out_second()
    for copy in p1 + p2 + p3:
        copy.wait_send()


def solution(mesh):
    lat_total, lon_total = mesh.shape["lat"], mesh.shape["lon"]

    def step(fields, qkv_low, proj_low, merge_proj, qkv_high, proj_high, bias_low, bias_high):
        def vmem(*shape, dtype=BF16):
            return pltpu.VMEM(shape, dtype)

        operands = (
            fields.transpose(1, 0, 2),
            qkv_low,
            proj_low,
            merge_proj,
            qkv_high,
            proj_high,
            bias_low.transpose(0, 2, 1, 3),
            bias_high.transpose(0, 2, 1, 3),
        )
        operands = [pltpu.with_memory_space_constraint(operand, pltpu.HBM) for operand in operands]
        halo = [vmem(176, WIDE), vmem(80, WIDE), vmem(32, WIDE)]
        last_halo = [vmem(96, WIDE), vmem(48, WIDE), vmem(48, WIDE), vmem(48, WIDE)]
        return pl.pallas_call(
            functools.partial(kernel, lat_total=lat_total, lon_total=lon_total),
            out_shape=jax.ShapeDtypeStruct((6, 2, PAIRS * WIDE), BF16),
            in_specs=[pl.BlockSpec(memory_space=pl.ANY)] * 8,
            out_specs=pl.BlockSpec(memory_space=pltpu.VMEM),
            scratch_shapes=[
                vmem(15, 2, (PAIRS + 3) * WIDE),
                vmem((PAIRS + 3) * 3, 32, 128, dtype=F32),
                vmem(192, 576),
                vmem(192, 192),
                vmem(768, 384),
                vmem(384, 1152),
                vmem(384, 384),
                vmem(1, 6, 2, NPOS, dtype=F32),
                vmem(1, 12, 1, NPOS, dtype=F32),
                vmem(256, 768),
                vmem(256, 768),
                vmem(256, 384),
                vmem(256, 384),
                vmem(64, 896, dtype=F32),
                vmem(384, 256, dtype=F32),
                vmem(512, 128, dtype=F32),
                vmem(512, 128, dtype=F32),
                vmem(2, 12, 96, 128, dtype=F32),
                vmem(24, 96, 128, dtype=F32),
                vmem(16, 48, WIDE, dtype=F32),
                vmem(16, 48, WIDE),
                vmem(16, 96, 768),
                vmem(16, 96, 256),
                vmem(16, 48, WIDE, dtype=F32),
                *halo, *halo, *last_halo, *last_halo,
                vmem(2, 384, WIDE, dtype=F32),
                vmem(2, 384, WIDE),
                vmem(4, 96, WIDE, dtype=F32),
                vmem(4, 96, WIDE),
                vmem(4, 96, 3 * WIDE),
                vmem(4, 96, WIDE),
                vmem(4, 96, WIDE, dtype=F32),
                pltpu.SemaphoreType.DMA((10,)),
                pltpu.SemaphoreType.DMA((10,)),
                pltpu.SemaphoreType.DMA((10,)),
            ],
            compiler_params=pltpu.CompilerParams(
                collective_id=0, has_side_effects=True, vmem_limit_bytes=28 * 1024 * 1024
            ),
            name="block",
        )(*operands).transpose(1, 0, 2)

    return jax.shard_map(
        step,
        mesh=mesh,
        in_specs=(
            P(None, "lat", "lon"),
            P(),
            P(),
            P(),
            P(),
            P(),
            P(None, "lat", None, None),
            P(None, "lat", None, None),
        ),
        out_specs=P(None, "lat", "lon"),
        check_vma=False,
    )
```

```python
import functools

import jax
import jax.numpy as jnp
from jax import lax
from jax.experimental import pallas as pl
from jax.experimental.pallas import tpu as pltpu
from jax.sharding import PartitionSpec as P

MESH = pl.DeviceIdType.MESH
F32 = jnp.float32
BF16 = jnp.bfloat16

EPSILON = 1e-05
NEG = -1e30
SCALE = 32 ** (-0.5)
NPOS = 3312
HALF = 828
PAIRS = 24
WIDE = 384
PLACES = ((3, 4, 5, 6, 7, 0), (1, 2, 3, 4, 5, 6), (7, 0, 2, 4, 6, 1))
TABLE_ROWS = ((0, 16), (16, 16), (32, 32))


def sublanes(rows):
    return lax.rem(lax.broadcasted_iota(jnp.int32, (rows, 1), 0), 8)


def roll8(value, shift):
    shift %= 8
    if shift == 0:
        return value
    rows, cols = value.shape
    if rows == 8:
        return pltpu.roll(value, shift, 0)
    return pltpu.roll(value.reshape(rows // 8, 8, cols), shift, 1).reshape(rows, cols)


def kernel(
    fields_hbm, qkv_low_hbm, proj_low_hbm, merge_hbm, qkv_high_hbm, proj_high_hbm, bias_low_hbm,
    bias_high_hbm,
    out_ref,
    fields, flat, wl, wp, wm, wh, wph, bl, bh,
    w_even, w_odd, wp_even, wp_odd,
    raw, tabs, strip_e, strip_o, t_low, t_high,
    xu, xn, qkv, ob, lo,
    s2_lat, s2_lon, s2_cor, r2_lat, r2_lon, r2_cor,
    s3_near, s3_lat, s3_lon, s3_cor, r3_near, r3_lat, r3_lon, r3_cor,
    mi, mn, mg, xh, qh, oh2, res,
    local_sem, send_sem, recv_sem,
    *, lat_total, lon_total,
):
    lat = lax.axis_index("lat")
    lon = lax.axis_index("lon")
    lat_prev = lax.rem(lat + lat_total - 1, lat_total)
    lat_next = lax.rem(lat + 1, lat_total)
    lon_prev = lax.rem(lon + lon_total - 1, lon_total)
    lon_next = lax.rem(lon + 1, lon_total)
    before = ((lat_prev, lon), (lat, lon_prev), (lat_prev, lon_prev))
    after = ((lat_next, lon), (lat, lon_next), (lat_next, lon_next))

    def device(place):
        return {"lat": place[0], "lon": place[1]}

    barrier = pltpu.get_barrier_semaphore()
    for place in after:
        pl.semaphore_signal(barrier, inc=1, device_id=device(place), device_id_type=MESH)

    def fetch(source, target, index):
        copy = pltpu.make_async_copy(source, target, local_sem.at[index])
        copy.start()
        return copy

    get_fields = fetch(fields_hbm, fields.at[0:12, :, 0:PAIRS * WIDE], 0)
    get_bl = fetch(bias_low_hbm, bl, 1)
    get_bh = fetch(bias_high_hbm, bh, 2)
    get_wl = fetch(qkv_low_hbm, wl, 4)
    get_wp = fetch(proj_low_hbm, wp, 5)
    get_wm = fetch(merge_hbm, wm, 6)
    get_wh = fetch(qkv_high_hbm, wh, 7)
    get_wph = fetch(proj_high_hbm, wph, 8)

    def remote(source, target, index, place):
        return pltpu.make_async_remote_copy(
            src_ref=source,
            dst_ref=target,
            send_sem=send_sem.at[index],
            recv_sem=recv_sem.at[index],
            device_id=device(place),
            device_id_type=MESH,
        )

    inner, edge = pl.ds(3 * WIDE, 21 * WIDE), pl.ds(0, 3 * WIDE)
    beyond = pl.ds(PAIRS * WIDE, 3 * WIDE)
    p1 = (
        remote(fields_hbm.at[0:3, :, inner], fields.at[12:15, :, inner], 0, before[0]),
        remote(fields_hbm.at[3:12, :, edge], fields.at[3:12, :, beyond], 1, before[1]),
        remote(fields_hbm.at[0:3, :, edge], fields.at[12:15, :, beyond], 2, before[2]),
    )
    p2 = (
        remote(s2_lat, r2_lat, 3, before[0]),
        remote(s2_lon, r2_lon, 4, before[1]),
        remote(s2_cor, r2_cor, 5, before[2]),
    )
    p3 = (
        remote(s3_near, r3_near, 9, after[0]),
        remote(s3_lat, r3_lat, 6, after[0]),
        remote(s3_lon, r3_lon, 7, after[1]),
        remote(s3_cor, r3_cor, 8, after[2]),
    )

    sub8 = sublanes(8)
    pl.semaphore_wait(barrier, 3)
    for copy in p1:
        copy.start()

    def put_unit(r, jjr, p, part, slab):
        u = 8 * r + 2 * (jjr // 6) + p
        xu[u, 8 * (jjr % 6):8 * (jjr % 6) + 8, 128 * part:128 * part + 128] = slab

    def widen(jj, first, count):
        for part in range(3):
            at = jj * WIDE + 128 * part
            flat[3 * jj + part, 2 * first:2 * (first + count), :] = (
                fields[first:first + count, :, at:at + 128].astype(F32).reshape(2 * count, 128)
            )

    def put_first(jj):
        for part in range(3):
            for p in range(2):
                upper = flat[3 * jj + part, pl.ds(p, 8, stride=2), :]
                lower = flat[3 * jj + part, pl.ds(16 + p, 8, stride=2), :]
                put_unit(0, jj - 3, p, part, jnp.where(sub8 >= 3, upper, lower))

    def put_second(jj):
        for part in range(3):
            for p in range(2):
                put_unit(1, jj - 3, p, part, flat[3 * jj + part, pl.ds(16 + p, 8, stride=2), :])

    def stage_own():
        flat[:, 24:32, :] = jnp.zeros_like(flat[:, 24:32, :])
        for jj in range(3, PAIRS):
            widen(jj, 0, 12)
            put_first(jj)

    get_fields.wait()
    stage_own()

    def stage_pad():
        w_even[...] = jnp.zeros_like(w_even)
        w_odd[...] = jnp.zeros_like(w_odd)
        wp_even[...] = jnp.zeros_like(wp_even)
        wp_odd[...] = jnp.zeros_like(wp_odd)
        strip_e[...] = jnp.zeros_like(strip_e)
        strip_o[...] = jnp.zeros_like(strip_o)
        tabs[...] = jnp.zeros_like(tabs)
        raw[...] = jnp.zeros_like(raw)
        for part in range(3):
            piece = wl[:, 192 * part:192 * part + 192]
            w_even[0:192, 256 * part:256 * part + 192] = piece
            w_odd[64:256, 256 * part:256 * part + 192] = piece
        wp_even[0:192, 0:192] = wp[...]
        wp_odd[0:192, 192:384] = wp[...]

    get_wl.wait()
    get_wp.wait()
    stage_pad()

    def one_hot(kind):
        wide = lax.broadcasted_iota(jnp.int32, (8, 256), 1)
        within = lax.rem(wide, 128)
        step, place = within // 8, lax.rem(within, 8)
        offset = jnp.where(wide < 128, 2 * step - 10, 2 * step - 11)
        entry = jnp.full((8, 256), -1, jnp.int32)
        for ia in range(6):
            entry = jnp.where(place == PLACES[kind][ia], 23 * ia + 11 + offset, entry)
        entry = jnp.where(step < jnp.where(wide < 128, 11, 12), entry, -1)
        row = lax.broadcasted_iota(jnp.int32, (256, 256), 0)
        return jnp.where(row == entry[0:1, :], 1.0, 0.0).astype(BF16)

    def build_strips(kinds):
        for kind in kinds:
            first, count = TABLE_ROWS[kind]
            for p in range(2):
                start = 0 if p == 1 else NPOS - HALF
                at = first + p * (count // 2)
                if kind < 2:
                    raw[at:at + 6, 0:HALF] = bl[0, :, kind, start:start + HALF]
                else:
                    raw[at:at + 12, 0:HALF] = bh[0, :, 0, start:start + HALF]
            for ia in range(6):
                for ib in range(6):
                    source, at = 138 * ia + 23 * ib, 6 * first + count * ib
                    tabs[at:at + count, 23 * ia:23 * ia + 23] = raw[first:first + count, source:source + 23]
        for kind in kinds:
            first, count = TABLE_ROWS[kind]
            wide = tabs[6 * first:6 * (first + count), :]
            high = wide.astype(BF16)
            rest = wide - high.astype(F32)
            middle = rest.astype(BF16)
            low = (rest - middle.astype(F32)).astype(BF16)
            hot = one_hot(kind)
            spread = jnp.dot(high, hot, preferred_element_type=F32)
            spread = spread + jnp.dot(middle, hot, preferred_element_type=F32)
            spread = spread + jnp.dot(low, hot, preferred_element_type=F32)
            for ib in range(6):
                piece = spread[count * ib:count * (ib + 1)]
                where = pl.ds(first * 8 + PLACES[kind][ib], count, stride=8)
                strip_e[where, :] = piece[:, 0:128]
                strip_o[where, :] = piece[:, 128:256]


    lane = lax.broadcasted_iota(jnp.int32, (8, 128), 1)
    row8 = lax.broadcasted_iota(jnp.int32, (8, 128), 0)
    lane8 = lax.rem(lane, 8)
    last = lat == lat_total - 1

    def any_of(value, options):
        hit = value == options[0]
        for option in options[1:]:
            hit = hit | (value == option)
        return hit

    def mask_of(kind):
        places = PLACES[kind]
        mask = jnp.where(any_of(row8, places), 0.0, NEG)
        if kind > 0:
            differ = jnp.where(any_of(row8, places[3:]), 1, 0) != jnp.where(any_of(lane8, places[3:]), 1, 0)
            mask = jnp.where(differ & last, NEG, mask)
        return mask

    def turn(value, shift):
        return pltpu.roll(value, shift, 1) if shift else value

    def build_tables(kind, target):
        mask = mask_of(kind)
        first, count = TABLE_ROWS[kind]
        stride = count // 2
        heads = 12 if kind == 2 else 6

        def one(p, carry):
            for head in range(heads):
                at = pl.multiple_of((first + p * stride + head) * 8, 8)
                even = strip_e[pl.ds(at, 8), :]
                odd = strip_o[pl.ds(at, 8), :]
                for parity in range(2):
                    left, right = (even, odd) if parity == 0 else (odd, even)
                    for k in range(6):
                        tile = jnp.where(
                            lane < 48,
                            turn(left, (128 - (5 - k) * 8) % 128),
                            turn(right, 8 * k + 8 * parity),
                        )
                        row = 48 * parity + 8 * k
                        target[p * heads + head, row:row + 8, :] = tile + mask
            return carry

        lax.fori_loop(0, 2, one, 0)

    def stage_tables_low():
        build_strips((0, 1))
        build_tables(0, t_low.at[0])

    def stage_tables_second():
        build_tables(1, t_low.at[1])

    def stage_tables_high():
        build_strips((2,))
        build_tables(2, t_high)

    get_bl.wait()
    stage_tables_low()

    wide_lane = lax.broadcasted_iota(jnp.int32, (1, 128), 1)
    low_half = wide_lane < 64
    head_masks = [
        jnp.where(wide_lane // 32 == h, 1.0, 0.0).astype(BF16) for h in range(4)
    ]
    ones = jnp.ones((16, 96), BF16)

    def norm_unit(u):
        x = xu[u]
        x0, x1, x2 = x[:, 0:128], x[:, 128:256], x[:, 256:384]
        me = jnp.sum(x0 + jnp.where(low_half, x1, 0.0), axis=1, keepdims=True) / 192
        mo = jnp.sum(x2 + jnp.where(low_half, 0.0, x1), axis=1, keepdims=True) / 192
        d0, d1, d2 = x0 - me, x1 - jnp.where(low_half, me, mo), x2 - mo
        q1 = d1 * d1
        ve = jnp.sum(d0 * d0 + jnp.where(low_half, q1, 0.0), axis=1, keepdims=True) / 192
        vo = jnp.sum(d2 * d2 + jnp.where(low_half, 0.0, q1), axis=1, keepdims=True) / 192
        re, ro = lax.rsqrt(ve + EPSILON), lax.rsqrt(vo + EPSILON)
        xn[u, :, 0:128] = (d0 * re).astype(BF16)
        xn[u, :, 128:256] = (d1 * jnp.where(low_half, re, ro)).astype(BF16)
        xn[u, :, 256:384] = (d2 * ro).astype(BF16)

    def qkv_units(first, count):
        for u in range(first, first + count):
            norm_unit(u)
        for parity, weight in ((0, w_even), (1, w_odd)):
            rows = xn[first:first + count, :, 128 * parity:128 * parity + 256].reshape(count * 48, 256)
            for part in range(3):
                piece = jnp.dot(rows, weight[:, 256 * part:256 * part + 256], preferred_element_type=F32)
                qkv[first:first + count, 48 * parity:48 * parity + 48, 256 * part:256 * part + 256] = (
                    piece.astype(BF16).reshape(count, 48, 256)
                )

    def group_attend(q, k, v, heads, table):
        stack = jnp.concatenate([k * head_masks[h] for h in range(heads)], axis=0)
        scores = lax.dot_general(stack, q, (((1,), (1,)), ((), ())), preferred_element_type=F32)
        scores = scores.reshape(heads, 96, 96) * SCALE + table
        weights = jnp.exp(scores - jnp.max(scores, axis=1, keepdims=True)).astype(BF16)
        turned = v.T
        mixed = []
        for h in range(heads):
            values = jnp.concatenate([turned[32 * h:32 * h + 32], ones], axis=0)
            sums = jnp.dot(values, weights[h], preferred_element_type=F32)
            mixed.append(sums[0:32] / sums[32:33])
        if heads < 4:
            mixed.append(jnp.zeros((128 - 32 * heads, 96), F32))
        return jnp.concatenate(mixed, axis=0).T.astype(BF16)

    def attend_low(r, first, count):
        def one(pair, carry):
            for p in range(2):
                u = 2 * pair + p
                for group, heads in ((0, 4), (1, 2)):
                    at = 128 * group
                    ob[u, :, at:at + 128] = group_attend(
                        qkv[u, :, at:at + 128],
                        qkv[u, :, 256 + at:384 + at],
                        qkv[u, :, 512 + at:640 + at],
                        heads,
                        t_low[r, p * 6 + 4 * group:p * 6 + 4 * group + heads, :, 0:96],
                    )
            return carry

        if count == 2:
            one(first // 2, 0)
        else:
            lax.fori_loop(first // 2, (first + count) // 2, one, 0)


    def project_low(first, count):
        even = ob[first:first + count, 0:48, :].reshape(count * 48, 256)
        odd = ob[first:first + count, 48:96, :].reshape(count * 48, 256)
        att = jnp.dot(even, wp_even[...], preferred_element_type=F32) + jnp.dot(
            odd, wp_odd[...], preferred_element_type=F32
        )
        att = att.astype(BF16).astype(F32).reshape(count, 48, WIDE)
        lo[first:first + count] = (xu[first:first + count] + att).astype(BF16).astype(F32)

    def low_slab(r, jjr, p):
        return lo[8 * r + 2 * (jjr // 6) + p, 8 * (jjr % 6):8 * (jjr % 6) + 8, :]

    def stage_qkv_a():
        qkv_units(0, 6)

    def stage_attend_a():
        attend_low(0, 0, 6)

    def stage_first_end():
        for k in range(3):
            widen(PAIRS + k, 0, 12)
            put_first(PAIRS + k)
        qkv_units(6, 2)
        attend_low(0, 6, 2)
        project_low(0, 8)
        for jjr in range(PAIRS):
            slab = jnp.where(
                (sub8 >= 2) & (sub8 < 6), low_slab(0, jjr, 1), roll8(low_slab(0, jjr, 0), 4)
            ).astype(BF16)
            if jjr < 3:
                s2_cor[8 * jjr:8 * jjr + 8, :] = slab
            else:
                s2_lat[8 * (jjr - 3):8 * (jjr - 3) + 8, :] = slab

    def stage_second_edge():
        for jj in range(3, PAIRS + 3):
            widen(jj, 12, 3)
            put_second(jj)
        qkv_units(8, 2)
        attend_low(1, 8, 2)
        project_low(8, 2)
        for k in range(3):
            for p in range(2):
                at = (2 * k + p) * 8
                s2_lon[at:at + 8, :] = jnp.where(sub8 == 0, low_slab(0, k, p), low_slab(1, k, p)).astype(BF16)
            s2_lon[48 + 8 * k:56 + 8 * k, :] = jnp.where(
                sub8 >= 4, low_slab(0, k, 0), roll8(low_slab(0, k, 1), 4)
            ).astype(BF16)

    def stage_qkv_b():
        qkv_units(10, 6)

    def stage_attend_b():
        attend_low(1, 10, 6)

    def stage_project_b():
        project_low(10, 6)

    stage_qkv_a()
    stage_attend_a()

    stage_tables_second()
    p1[1].wait_recv()
    stage_first_end()
    p2[0].start()
    p2[2].start()
    p1[0].wait_recv()
    p1[2].wait_recv()
    stage_second_edge()
    p2[1].start()
    stage_qkv_b()
    stage_attend_b()
    stage_project_b()
    get_bh.wait()
    stage_tables_high()

    def gather(w):
        for col in range(12 * w, 12 * w + 12):
            jjr = col + 3
            if col < 21:
                halo = r2_lat[8 * col:8 * col + 8, :].astype(F32)
            else:
                k = col - 21
                halo = r2_cor[8 * k:8 * k + 8, :].astype(F32)
                upper = r2_lon[48 + 8 * k:56 + 8 * k, :].astype(F32)
            for p in range(2):
                far = roll8(halo, 4 * p)
                if col < 21:
                    first, second = low_slab(0, jjr, p), low_slab(1, jjr, p)
                    inner = jnp.where(sub8 == 0, first, second)
                else:
                    first = roll8(upper, 4 * p)
                    at = (2 * k + p) * 8
                    inner = r2_lon[at:at + 8, :].astype(F32)
                at = ((2 * w + p) * 12 + col % 12) * 8
                mi[0, at:at + 8, :] = jnp.where(sub8 == 7, far, inner)
                mi[1, at:at + 8, :] = jnp.where(sub8 >= 6, first, far)

    def pair_sum(value):
        rows = value.shape[0]
        value = jnp.broadcast_to(value, (rows, 128))
        even = lax.rem(sublanes(rows), 2) == 0
        return value + jnp.where(even, roll8(value, 7), roll8(value, 1))

    def triple(value):
        return jnp.concatenate([value, value, value], axis=1)

    def norm_merge(index):
        rows = slice(index * 48, index * 48 + 48)
        for kind in range(2):
            x = mi[kind, rows, :]
            centre = pair_sum(jnp.sum(x, axis=1, keepdims=True)) / 768
            d = x - triple(centre)
            spread = pair_sum(jnp.sum(d * d, axis=1, keepdims=True)) / 768
            mn[kind, rows, :] = (d * triple(lax.rsqrt(spread + EPSILON))).astype(BF16)

    even_row = lax.rem(sublanes(192), 2) == 0

    def merge(w):
        for index in range(4 * w, 4 * w + 4):
            norm_merge(index)
        rows = slice(192 * w, 192 * w + 192)
        sums = []
        for kind in range(2):
            y0 = jnp.dot(mn[kind, rows, :], wm[0:384, :], preferred_element_type=F32)
            y1 = jnp.dot(mn[kind, rows, :], wm[384:768, :], preferred_element_type=F32)
            sums.append(y0 + roll8(y1, 7) if kind == 0 else roll8(y0, 1) + y1)
        merged = jnp.where(even_row, sums[0], sums[1]).astype(BF16).astype(F32)
        for p in range(2):
            for col in range(12):
                at, source = 48 * (col % 2) + 8 * (col // 2), (12 * p + col) * 8
                mg[2 * w + p, at:at + 8, :] = merged[source:source + 8, :]

    def norm_high(u):
        x = mg[u]
        d = x - jnp.sum(x, axis=1, keepdims=True) / 384
        spread = jnp.sum(d * d, axis=1, keepdims=True) / 384
        xh[u] = (d * lax.rsqrt(spread + EPSILON)).astype(BF16)

    def qkv_high_units(w):
        units = slice(2 * w, 2 * w + 2)
        for u in (2 * w, 2 * w + 1):
            norm_high(u)
        rows = xh[units].reshape(192, 384)
        for part in range(3):
            piece = jnp.dot(rows, wh[:, 384 * part:384 * part + 384], preferred_element_type=F32)
            qh[units, :, 384 * part:384 * part + 384] = piece.astype(BF16).reshape(2, 96, 384)

    def attend_high(w):
        for u in (2 * w, 2 * w + 1):
            p = u % 2
            for group in range(3):
                at = 128 * group
                oh2[u, :, at:at + 128] = group_attend(
                    qh[u, :, at:at + 128],
                    qh[u, :, 384 + at:512 + at],
                    qh[u, :, 768 + at:896 + at],
                    4,
                    t_high[p * 12 + 4 * group:p * 12 + 4 * group + 4, :, 0:96],
                )
        units = slice(2 * w, 2 * w + 2)
        att = jnp.dot(oh2[units].reshape(192, 384), wph[...], preferred_element_type=F32)
        att = att.astype(BF16).astype(F32).reshape(2, 96, 384)
        res[units] = (mg[units] + att).astype(BF16).astype(F32)

    def result(col, p):
        w, within = col // 12, col % 12
        at = 48 * (within % 2) + 8 * (within // 2)
        return res[2 * w + p, at:at + 8, :]

    def own_rows(x, shift):
        return jnp.where(sub8 == (5 + shift) % 8, roll8(x, 3 + shift), roll8(x, 4 + shift))

    def far_rows(x, shift):
        return jnp.where(
            sub8 == shift,
            roll8(x, 4 + shift),
            jnp.where(sub8 == 1 + shift, roll8(x, 3 + shift), roll8(x, 1 + shift)),
        )

    def pack_out(w):
        for col in range(12 * w, 12 * w + 12):
            slab = jnp.where(sub8 < 4, far_rows(result(col, 0), 0), far_rows(result(col, 1), 4)).astype(BF16)
            if col < 12:
                s3_near[8 * col:8 * col + 8, :] = slab
            elif col < 18:
                k = col - 12
                s3_lat[8 * k:8 * k + 8, :] = slab
            else:
                k = col - 18
                s3_cor[8 * k:8 * k + 8, :] = slab
                s3_lon[8 * k:8 * k + 8, :] = jnp.where(
                    (sub8 >= 3) & (sub8 < 6), own_rows(result(col, 0), 0), own_rows(result(col, 1), 4)
                ).astype(BF16)

    def put_out(target):
        for p in range(2):
            if target < 6:
                first = r3_cor[8 * target:8 * target + 8, :].astype(F32)
                second = roll8(r3_lon[8 * target:8 * target + 8, :].astype(F32), 4 * p)
            else:
                k = target - 6
                received, k = (r3_near, k) if k < 12 else (r3_lat, k - 12)
                first = received[8 * k:8 * k + 8, :].astype(F32)
                second = own_rows(result(target - 6, p), 0)
            whole = jnp.where(sub8 < 3, roll8(first, 4 * p), second)
            for part in range(3):
                flat[3 * target + part, pl.ds(p, 8, stride=2), :] = whole[:, 128 * part:128 * part + 128]
        for part in range(3):
            at = target * WIDE + 128 * part
            out_ref[:, :, at:at + 128] = flat[3 * target + part, 0:12, :].reshape(6, 2, 128).astype(BF16)

    def level_high(w):
        gather(w)
        merge(w)
        qkv_high_units(w)
        attend_high(w)
        pack_out(w)

    def stage_high_first():
        level_high(0)

    def stage_high_second():
        level_high(1)

    def stage_out_first():
        for target in range(6, 18):
            put_out(target)

    def stage_out_second():
        for target in (*range(6), *range(18, PAIRS)):
            put_out(target)

    get_wm.wait()
    get_wh.wait()
    get_wph.wait()
    p2[0].wait_recv()
    stage_high_first()
    p3[0].start()
    p2[1].wait_recv()
    p2[2].wait_recv()
    stage_high_second()
    p3[1].start()
    p3[2].start()
    p3[3].start()
    p3[0].wait_recv()
    stage_out_first()
    p3[1].wait_recv()
    p3[2].wait_recv()
    p3[3].wait_recv()
    stage_out_second()
    for copy in p1 + p2 + p3:
        copy.wait_send()


def solution(mesh):
    lat_total, lon_total = mesh.shape["lat"], mesh.shape["lon"]

    def step(fields, qkv_low, proj_low, merge_proj, qkv_high, proj_high, bias_low, bias_high):
        def vmem(*shape, dtype=BF16):
            return pltpu.VMEM(shape, dtype)

        operands = (
            fields.transpose(1, 0, 2),
            qkv_low,
            proj_low,
            merge_proj,
            qkv_high,
            proj_high,
            bias_low.transpose(0, 2, 1, 3),
            bias_high.transpose(0, 2, 1, 3),
        )
        operands = [pltpu.with_memory_space_constraint(operand, pltpu.HBM) for operand in operands]
        halo = [vmem(176, WIDE), vmem(80, WIDE), vmem(32, WIDE)]
        last_halo = [vmem(96, WIDE), vmem(48, WIDE), vmem(48, WIDE), vmem(48, WIDE)]
        return pl.pallas_call(
            functools.partial(kernel, lat_total=lat_total, lon_total=lon_total),
            out_shape=jax.ShapeDtypeStruct((6, 2, PAIRS * WIDE), BF16),
            in_specs=[pl.BlockSpec(memory_space=pl.ANY)] * 8,
            out_specs=pl.BlockSpec(memory_space=pltpu.VMEM),
            scratch_shapes=[
                vmem(15, 2, (PAIRS + 3) * WIDE),
                vmem((PAIRS + 3) * 3, 32, 128, dtype=F32),
                vmem(192, 576),
                vmem(192, 192),
                vmem(768, 384),
                vmem(384, 1152),
                vmem(384, 384),
                vmem(1, 6, 2, NPOS, dtype=F32),
                vmem(1, 12, 1, NPOS, dtype=F32),
                vmem(256, 768),
                vmem(256, 768),
                vmem(256, 384),
                vmem(256, 384),
                vmem(64, 896, dtype=F32),
                vmem(384, 256, dtype=F32),
                vmem(512, 128, dtype=F32),
                vmem(512, 128, dtype=F32),
                vmem(2, 12, 96, 128, dtype=F32),
                vmem(24, 96, 128, dtype=F32),
                vmem(16, 48, WIDE, dtype=F32),
                vmem(16, 48, WIDE),
                vmem(16, 96, 768),
                vmem(16, 96, 256),
                vmem(16, 48, WIDE, dtype=F32),
                *halo, *halo, *last_halo, *last_halo,
                vmem(2, 384, WIDE, dtype=F32),
                vmem(2, 384, WIDE),
                vmem(4, 96, WIDE, dtype=F32),
                vmem(4, 96, WIDE),
                vmem(4, 96, 3 * WIDE),
                vmem(4, 96, WIDE),
                vmem(4, 96, WIDE, dtype=F32),
                pltpu.SemaphoreType.DMA((10,)),
                pltpu.SemaphoreType.DMA((10,)),
                pltpu.SemaphoreType.DMA((10,)),
            ],
            compiler_params=pltpu.CompilerParams(
                collective_id=0, has_side_effects=True, vmem_limit_bytes=28 * 1024 * 1024
            ),
            name="block",
        )(*operands).transpose(1, 0, 2)

    return jax.shard_map(
        step,
        mesh=mesh,
        in_specs=(
            P(None, "lat", "lon"),
            P(),
            P(),
            P(),
            P(),
            P(),
            P(None, "lat", None, None),
            P(None, "lat", None, None),
        ),
        out_specs=P(None, "lat", "lon"),
        check_vma=False,
    )
```
